32 devices in a mesh: dp: 4 (over z), row: 4 (over x, core), col: 2 (over y).
Axes of the slice: x: 2, y: 2, z: 4, core: 2. Of those that a mesh axis runs over, the one named last changes fastest.
Arguments:
- tokens: bfloat16 [4096, 2048], P(('dp', 'row'), 'col'), may hold values from -8 to 8
- cotangent: bfloat16 [4096, 2048], P(('dp', 'row'), 'col'), may hold values from -8 to 8
- doc_lengths: int32 [12], replicated, may hold values from 1 to 1022, as said below
- doc_groups: int32 [12], replicated, may hold values from 0 to 3, as said below
- w_qkv: float32 [2048, 3, 2048], P(('col', 'dp'), None, 'row'), may hold values from -0.125 to 0.125
- w_up: float32 [2048, 4, 2048], P(('col', 'dp'), None, 'row'), may hold values from -0.125 to 0.125
- w_dense: float32 [2048, 2048], P(('row', 'dp'), 'col'), may hold values from -1.5 to 1.5
- w_down: float32 [2048, 4, 2048], P(('row', 'dp'), None, 'col'), may hold values from -0.0625 to 0.0625
- vectors: float32 [11, 2048], replicated, may hold values from -0.8 to 1.3
- m_qkv: float32 [2048, 3, 2048], P(('col', 'dp'), None, 'row'), may hold values from -40 to 40
- v_qkv: float32 [2048, 3, 2048], P(('col', 'dp'), None, 'row'), may hold values from 217.088 to 860.16
- m_up: float32 [2048, 4, 2048], P(('col', 'dp'), None, 'row'), may hold values from -12 to 12
- v_up: float32 [2048, 4, 2048], P(('col', 'dp'), None, 'row'), may hold values from 19.6608 to 77.824
- m_dense: float32 [2048, 2048], P(('row', 'dp'), 'col'), may hold values from -4 to 4
- v_dense: float32 [2048, 2048], P(('row', 'dp'), 'col'), may hold values from 1.68 to 6.8
- m_down: float32 [2048, 4, 2048], P(('row', 'dp'), None, 'col'), may hold values from -24 to 24
- v_down: float32 [2048, 4, 2048], P(('row', 'dp'), None, 'col'), may hold values from 77.824 to 311.296
- m_vec: float32 [11, 2048], replicated, may hold values from -44.8 to 44.8
- v_vec: float32 [11, 2048], replicated, may hold values from 16.384 to 2048
Outputs:
- block_out: bfloat16 [4096, 2048], P(('dp', 'row'), 'col')
- grad_tokens: float32 [4096, 2048], P(('dp', 'row'), 'col')
- m_qkv_next: float32 [2048, 3, 2048], P(('col', 'dp'), None, 'row')
- v_qkv_next: float32 [2048, 3, 2048], P(('col', 'dp'), None, 'row')
- w_qkv_next: float32 [2048, 3, 2048], P(('col', 'dp'), None, 'row')
- m_up_next: float32 [2048, 4, 2048], P(('col', 'dp'), None, 'row')
- v_up_next: float32 [2048, 4, 2048], P(('col', 'dp'), None, 'row')
- w_up_next: float32 [2048, 4, 2048], P(('col', 'dp'), None, 'row')
- m_dense_next: float32 [2048, 2048], P(('row', 'dp'), 'col')
- v_dense_next: float32 [2048, 2048], P(('row', 'dp'), 'col')
- w_dense_next: float32 [2048, 2048], P(('row', 'dp'), 'col')
- m_down_next: float32 [2048, 4, 2048], P(('row', 'dp'), None, 'col')
- v_down_next: float32 [2048, 4, 2048], P(('row', 'dp'), None, 'col')
- w_down_next: float32 [2048, 4, 2048], P(('row', 'dp'), None, 'col')
- m_vec_next: float32 [11, 2048], replicated
- v_vec_next: float32 [11, 2048], replicated
- vec_next: float32 [11, 2048], replicated
The draws below stay inside these ranges and needn't reach their ends.
Inputs may be any that keep to these rules, and one draw needn't show every extreme that they name: `doc_lengths`: the sequences of one group hold at most 1024 tokens together, exactly 1024 in at least one group; in each group one sequence is longer than 768 and the others are shorter than 128. `doc_groups`: every data group holds exactly 3 sequences.
All inputs are finite; a program needn't handle non-finite values.
Results may differ from the reference program's by a relative error of at most 0.012.
Values may be sent and summed in bfloat16 or wider, within the bound.
A program may use at most 256 MiB of HBM per device.

```python
import math
import jax
import jax.numpy as jnp
from jax import lax

D = 2048
HEADS = 32
HDIM = 64
ROT = 32
FF = 8192
CAP = 1024
SEQS_GRP = 3
BLK = 512
STEP = 10
NSEQ = 12
TOKENS = 4096
N_DP = 4


def seq_tables(key):
    key_perm, key_long, key_short, key_full, key_len = jax.random.split(key, 5)
    shuffled = jax.random.permutation(key_perm, NSEQ).astype(jnp.int32)
    group_of = shuffled // SEQS_GRP
    slot_of = shuffled % SEQS_GRP
    long_slot = jax.random.randint(key_long, (N_DP,), 0, SEQS_GRP)
    full_group = jax.random.randint(key_full, (), 0, N_DP)
    is_full = jnp.arange(N_DP, dtype=jnp.int32) == full_group
    short_len = jax.random.randint(key_short, (N_DP, SEQS_GRP), 1, CAP // (4 * (SEQS_GRP - 1)))
    short_len = jnp.where(is_full[:, None], 1, short_len)
    slot_ids = jnp.arange(SEQS_GRP, dtype=jnp.int32)
    is_long = slot_ids[None, :] == long_slot[:, None]
    room_left = CAP - jnp.sum(jnp.where(is_long, 0, short_len), axis=1)
    long_len = jax.random.randint(key_len, (N_DP,), 3 * CAP // 4 + 1, room_left + 1)
    long_len = jnp.where(is_full, room_left, long_len)
    len_table = jnp.where(is_long, long_len[:, None], short_len)
    seq_lengths = len_table[group_of, slot_of]
    return (seq_lengths.astype(jnp.int32), group_of.astype(jnp.int32))


def draw_doc_lengths(key, part):
    tables = seq_tables(key)
    return tables[0]


def draw_doc_groups(key, part):
    tables = seq_tables(key)
    return tables[1]


def draw_tokens(key, part):
    key = jax.random.fold_in(key, 11)
    key_main = jax.random.fold_in(key, 0)
    ramp = jnp.arange(D, dtype=jnp.float32) / (D - 1)
    spread = 0.6 + 1.2 * ramp
    noise = jnp.clip(jax.random.normal(key_main, (TOKENS, D), jnp.float32), -4.0, 4.0)
    return (spread[None, :] * noise).astype(jnp.bfloat16)


def draw_cotangent(key, part):
    key = jax.random.fold_in(key, 23)
    ramp = jnp.arange(TOKENS, dtype=jnp.float32) / (TOKENS - 1)
    spread = 0.6 + 1.2 * ramp
    noise = jnp.clip(jax.random.normal(key, (TOKENS, D), jnp.float32), -4.0, 4.0)
    return (spread[:, None] * noise).astype(jnp.bfloat16)


def row_scales():
    return jnp.array([1.5, 1.5, 0.8, 0.8, 0.8, 0.3, 0.3, 0.3, 0.3, 1.2, 1.2], jnp.float32)


def draw_vectors(key, part):
    key = jax.random.fold_in(key, 31)
    key_gain, key_bias = jax.random.split(key)
    gains = jax.random.uniform(key_gain, (1, D), jnp.float32, 0.7, 1.3)
    biases = 0.2 * jnp.clip(jax.random.normal(key_bias, (10, D), jnp.float32), -4.0, 4.0)
    return jnp.concatenate([gains, biases], axis=0)


def draw_m_vec(key, part):
    key = jax.random.fold_in(key, 47)
    noise = jnp.clip(jax.random.normal(key, (11, D), jnp.float32), -4.0, 4.0)
    return 0.111 * math.sqrt(TOKENS) * row_scales()[:, None] * noise


def draw_v_vec(key, part):
    key = jax.random.fold_in(key, 59)
    factor = jnp.exp(jax.random.uniform(key, (11, D), jnp.float32, 0.0, math.log(4.0)))
    scales = row_scales()
    return 0.0526 * TOKENS * (scales * scales)[:, None] * factor


def steps_of(key, dims, cuts, low, top_value):
    gain, own = 1.0, jax.random.fold_in(key, 6)
    for dim, parts in cuts:
        steps = jnp.exp(jax.random.uniform(jax.random.fold_in(own, dim), (parts,), jnp.float32, low / len(cuts), top_value / len(cuts)))
        gain = gain * jnp.repeat(steps, dims[dim] // parts).reshape([-1 if axis == dim else 1 for axis in range(len(dims))])
    return gain


def bell_draw(rng, dims, deviation, limit, cuts=(), kind=jnp.bfloat16):
    values = deviation * jax.random.normal(rng, dims, jnp.float32)
    if cuts:
        values = values * steps_of(rng, dims, cuts, -0.22, 0.18)
    return jnp.clip(values, -limit, limit).astype(kind)


def setup_inputs(seed: int = 0) -> dict:
    seeds = jax.random.split(jax.random.key(seed), 20)
    return {
        "tokens": draw_tokens(jax.random.fold_in(seeds[19], 71), 0),
        "cotangent": draw_cotangent(jax.random.fold_in(seeds[19], 71), 0),
        "doc_lengths": draw_doc_lengths(jax.random.fold_in(seeds[19], 71), 0),
        "doc_groups": draw_doc_groups(jax.random.fold_in(seeds[19], 71), 0),
        "w_qkv": bell_draw(seeds[4], (D, 3, D), D ** -0.5, 0.125, ((0, 8), (2, 4)), jnp.float32),
        "w_up": bell_draw(seeds[5], (D, 4, D), D ** -0.5, 0.125, ((0, 8), (2, 4)), jnp.float32),
        "w_dense": bell_draw(seeds[6], (D, D), (max(D // 128, 4)) ** -0.5, 1.5, ((0, 16), (1, 2)), jnp.float32),
        "w_down": bell_draw(seeds[7], (D, 4, D), FF ** -0.5, 0.0625, ((0, 16), (2, 2)), jnp.float32),
        "vectors": draw_vectors(jax.random.fold_in(seeds[19], 71), 0),
        "m_qkv": bell_draw(seeds[9], (D, 3, D), (0.111 * TOKENS ** 0.5), 40.0, ((0, 8), (2, 4)), jnp.float32),
        "v_qkv": jnp.clip(jnp.exp(math.log(860.16) - 1.3768156 * jax.random.uniform(seeds[10], (D, 3, D), jnp.float32) ** steps_of(seeds[10], (D, 3, D), ((0, 8), (2, 4)), -0.2, 0.2)), 217.088, 860.16),
        "m_up": bell_draw(seeds[11], (D, 4, D), (0.033 * TOKENS ** 0.5), 12.0, ((0, 8), (2, 4)), jnp.float32),
        "v_up": jnp.clip(jnp.exp(math.log(77.824) - 1.375823 * jax.random.uniform(seeds[12], (D, 4, D), jnp.float32) ** steps_of(seeds[12], (D, 4, D), ((0, 8), (2, 4)), -0.2, 0.2)), 19.6608, 77.824),
        "m_dense": bell_draw(seeds[13], (D, D), (0.31 * N_DP ** 0.5), 4.0, ((0, 16), (1, 2)), jnp.float32),
        "v_dense": jnp.clip(jnp.exp(math.log(6.8) - 1.3981289 * jax.random.uniform(seeds[14], (D, D), jnp.float32) ** steps_of(seeds[14], (D, D), ((0, 16), (1, 2)), -0.2, 0.2)), 1.68, 6.8),
        "m_down": bell_draw(seeds[15], (D, 4, D), (0.067 * TOKENS ** 0.5), 24.0, ((0, 16), (2, 2)), jnp.float32),
        "v_down": jnp.clip(jnp.exp(math.log(311.296) - 1.3862944 * jax.random.uniform(seeds[16], (D, 4, D), jnp.float32) ** steps_of(seeds[16], (D, 4, D), ((0, 16), (2, 2)), -0.2, 0.2)), 77.824, 311.296),
        "m_vec": draw_m_vec(jax.random.fold_in(seeds[19], 71), 0),
        "v_vec": draw_v_vec(jax.random.fold_in(seeds[19], 71), 0),
    }


@jax.custom_vjp
def low(v):
    return lax.optimization_barrier(v.astype(jnp.bfloat16)).astype(jnp.float32)

@jax.custom_vjp
def low_back(v):
    return v

def low_keep(v):
    return (low(v), None)

def low_pass(kept, grad):
    return (grad,)

def back_keep(v):
    return (v, None)

def back_low(kept, grad):
    return (low(grad),)
low.defvjp(low_keep, low_pass)
low_back.defvjp(back_keep, back_low)
HIGH = lax.Precision.HIGHEST
eps_norm = 1e-05

def layout(doc_lengths, doc_groups, group_id, slot_count):
    in_group = (doc_groups == group_id).astype(jnp.int32)
    group_sizes = doc_lengths * in_group
    seq_ends = jnp.cumsum(group_sizes, dtype=jnp.int32)
    starts = seq_ends - group_sizes
    total_len = jnp.sum(group_sizes, dtype=jnp.int32)
    places = jnp.arange(slot_count, dtype=jnp.int32)
    member = (places[:, None] >= starts[None, :]) & (places[:, None] < seq_ends[None, :]) & (in_group[None, :] == 1)
    member = member.astype(jnp.int32)
    number = jnp.arange(doc_lengths.shape[0], dtype=jnp.int32) + 1
    segment = lax.optimization_barrier(jnp.sum(member * number[None, :], axis=1, dtype=jnp.int32)) - 1
    seq_first = lax.optimization_barrier(jnp.sum(member * starts[None, :], axis=1, dtype=jnp.int32))
    position = jnp.where(segment >= 0, places - seq_first, places - total_len)
    return (segment, position)

def turn_angles(position):
    half_rot = ROT // 2
    freq_base = jnp.power(10000.0, -2.0 * jnp.arange(half_rot, dtype=jnp.float32) / ROT)
    angle = position.astype(jnp.float32)[:, None] * freq_base[None, :]
    return (jnp.cos(angle), jnp.sin(angle))

def rotate(heads_view, cos_part, sin_part):
    half_rot = ROT // 2
    lead_part = heads_view[..., :half_rot]
    trail_part = heads_view[..., half_rot:ROT]
    cos_wide = cos_part[:, None, :]
    sin_wide = sin_part[:, None, :]
    return jnp.concatenate([lead_part * cos_wide - trail_part * sin_wide, trail_part * cos_wide + lead_part * sin_wide, heads_view[..., ROT:]], axis=-1)

def attend(queries, key_rows, values, segment, score_scale):
    slot_count = queries.shape[0]
    places = jnp.arange(slot_count, dtype=jnp.int32)

    def one_block(block_id):
        row_begin = block_id * BLK
        query_block = lax.dynamic_slice_in_dim(queries, row_begin, BLK, 0)
        seg_block = lax.dynamic_slice_in_dim(segment, row_begin, BLK, 0)
        place_block = lax.dynamic_slice_in_dim(places, row_begin, BLK, 0)
        scores = jnp.einsum('qhd,khd->hqk', query_block, key_rows, precision=HIGH)
        scores = low_back(score_scale * scores)
        allowed = (seg_block[:, None] == segment[None, :]) & (place_block[:, None] >= places[None, :])
        scores = jnp.where(allowed[None], scores, -1e+30)
        top_score = lax.optimization_barrier(jnp.max(scores, axis=-1, keepdims=True))
        weights = jnp.exp(scores - top_score)
        probs_low = low(weights / lax.optimization_barrier(jnp.sum(weights, axis=-1, keepdims=True)))
        return jnp.einsum('hqk,khd->qhd', probs_low, values, precision=HIGH)
    blocks = lax.map(jax.checkpoint(one_block), jnp.arange(slot_count // BLK, dtype=jnp.int32))
    return blocks.reshape(slot_count, queries.shape[1], queries.shape[2])

def group_forward(tokens_group, segment, position, low_qkv, low_up, low_dense, low_down, vectors):
    slot_count = tokens_group.shape[0]
    mean_tok = lax.optimization_barrier(jnp.mean(tokens_group, axis=-1, keepdims=True))
    var_tok = lax.optimization_barrier(jnp.mean(tokens_group * tokens_group, axis=-1, keepdims=True)) - mean_tok * mean_tok
    normed = low((tokens_group - mean_tok) * lax.rsqrt(var_tok + eps_norm) * vectors[0] + vectors[1])
    pre_qkv = low_back(jnp.einsum('tc,ckj->tkj', normed, low_qkv, precision=HIGH) + vectors[2:5][None])
    heads_view = pre_qkv.reshape(slot_count, 3, HEADS, HDIM)
    cos_part, sin_part = turn_angles(position)
    queries = low(rotate(heads_view[:, 0], cos_part, sin_part))
    key_rows = low(rotate(heads_view[:, 1], cos_part, sin_part))
    values = low(heads_view[:, 2])
    attn_out = attend(queries, key_rows, values, segment, HDIM ** (-0.5))
    attn_out = low_back(low(attn_out.reshape(slot_count, D)))
    pre_up = low_back(jnp.einsum('tc,ckj->tkj', normed, low_up, precision=HIGH) + vectors[5:9][None])
    hidden = low(jax.nn.gelu(pre_up, approximate=True))
    mixed = jnp.dot(attn_out, low_dense, precision=HIGH) + jnp.einsum('tij,jio->to', hidden, low_down, precision=HIGH)
    return tokens_group + mixed + vectors[9] + vectors[10]

def adamw(weight, first_moment, second_moment, gradient, rate, decay):
    first_next = 0.9 * first_moment + 0.1 * gradient
    second_next = 0.95 * second_moment + 0.05 * gradient * gradient
    correct_one = 1.0 - 0.9 ** STEP
    correct_two = 1.0 - 0.95 ** STEP
    update = first_next / correct_one / (jnp.sqrt(second_next / correct_two) + 1e-08)
    return (first_next, second_next, weight - rate * (update + decay * weight))

def reference(tokens, cotangent, doc_lengths, doc_groups, w_qkv, w_up, w_dense, w_down, vectors, m_qkv, v_qkv, m_up, v_up, m_dense, v_dense, m_down, v_down, m_vec, v_vec):
    group_ids = jnp.arange(N_DP, dtype=jnp.int32)
    segments, positions = jax.vmap(lambda group_id: layout(doc_lengths, doc_groups, group_id, CAP))(group_ids)
    valid_rows = segments.reshape(N_DP * CAP) >= 0

    def whole_forward(tokens_in, qkv_in, up_in, dense_in, down_in, vector_in):
        low_qkv = low(qkv_in)
        low_up = low(up_in)
        low_dense = low(dense_in)
        low_down = low(down_in)
        grouped = tokens_in.reshape(N_DP, CAP, D)

        def run_group(group_items):
            return group_forward(group_items[0], group_items[1], group_items[2], low_qkv, low_up, low_dense, low_down, vector_in)
        outputs = lax.map(jax.checkpoint(run_group), (grouped, segments, positions))
        return outputs.reshape(N_DP * CAP, D)
    result, pullback = jax.vjp(whole_forward, tokens.astype(jnp.float32), w_qkv, w_up, w_dense, w_down, vectors)
    back_rows = jnp.where(valid_rows[:, None], cotangent.astype(jnp.float32), jnp.zeros((), jnp.float32))
    gradients = pullback(back_rows)
    block_out = result.astype(jnp.bfloat16)
    grad_tokens = gradients[0]
    qkv_new = adamw(w_qkv, m_qkv, v_qkv, gradients[1], D ** (-0.5), 0.1)
    up_new = adamw(w_up, m_up, v_up, gradients[2], D ** (-0.5), 0.1)
    dense_new = adamw(w_dense, m_dense, v_dense, gradients[3], max(D // 128, 4) ** (-0.5), 0.1)
    down_new = adamw(w_down, m_down, v_down, gradients[4], FF ** (-0.5), 0.1)
    vec_new = adamw(vectors, m_vec, v_vec, gradients[5], 0.5, 0.0)
    return (block_out, grad_tokens, qkv_new[0], qkv_new[1], qkv_new[2], up_new[0], up_new[1], up_new[2], dense_new[0], dense_new[1], dense_new[2], down_new[0], down_new[1], down_new[2], vec_new[0], vec_new[1], vec_new[2])
```

```python
import functools

import jax
import jax.numpy as jnp
from jax import lax
from jax.experimental import pallas as pl
from jax.experimental.pallas import tpu as pltpu
from jax.sharding import PartitionSpec as P

D = 2048
HDIM = 64
ROT = 32
FF = 8192
BLK = 512
STEP = 10
LINE = 4


eps_norm = 1e-05
f32 = jnp.float32
bf16 = jnp.bfloat16


def seq_layout(doc_lengths, doc_groups, group_id, places):
    in_group = (doc_groups == group_id).astype(jnp.int32)
    group_sizes = doc_lengths * in_group
    seq_ends = jnp.cumsum(group_sizes, dtype=jnp.int32)
    starts = seq_ends - group_sizes
    total_len = jnp.sum(group_sizes, dtype=jnp.int32)
    member = (
        (places[:, None] >= starts[None, :])
        & (places[:, None] < seq_ends[None, :])
        & (in_group[None, :] == 1)
    )
    member = member.astype(jnp.int32)
    number = jnp.arange(doc_lengths.shape[0], dtype=jnp.int32) + 1
    segment = jnp.sum(member * number[None, :], axis=1, dtype=jnp.int32) - 1
    seq_first = jnp.sum(member * starts[None, :], axis=1, dtype=jnp.int32)
    position = jnp.where(segment >= 0, places - seq_first, places - total_len)
    return (segment, position, total_len)


def turn_angles(position):
    half_rot = ROT // 2
    freq_base = jnp.power(10000.0, -2.0 * jnp.arange(half_rot, dtype=jnp.float32) / ROT)
    angle = position.astype(jnp.float32)[:, None] * freq_base[None, :]
    return (jnp.cos(angle), jnp.sin(angle))


def rotate(heads_view, cos_part, sin_part):
    half_rot = ROT // 2
    lead_part = heads_view[..., :half_rot]
    trail_part = heads_view[..., half_rot:ROT]
    cos_wide = cos_part[..., None, :]
    sin_wide = sin_part[..., None, :]
    return jnp.concatenate(
        [
            lead_part * cos_wide - trail_part * sin_wide,
            trail_part * cos_wide + lead_part * sin_wide,
            heads_view[..., ROT:],
        ],
        axis=-1,
    )


def adamw(weight, first_moment, second_moment, gradient, rate, decay):
    first_next = 0.9 * first_moment + 0.1 * gradient
    second_next = 0.95 * second_moment + 0.05 * gradient * gradient
    correct_one = 1.0 - 0.9**STEP
    correct_two = 1.0 - 0.95**STEP
    update = first_next / correct_one / (jnp.sqrt(second_next / correct_two) + 1e-08)
    return (first_next, second_next, weight - rate * (update + decay * weight))


class Copies:
    def __init__(self, send_sems, recv_sems):
        self.send_sems, self.recv_sems, self.sent, self.received = send_sems, recv_sems, 0, 0

    def slot(self):
        self.received += 1
        return self.received - 1

    def make(self, src, dst, device, slot=None):
        slot = self.slot() if slot is None else slot
        self.sent += 1
        return pltpu.make_async_remote_copy(
            src_ref=src, dst_ref=dst, send_sem=self.send_sems.at[self.sent - 1], recv_sem=self.recv_sems.at[slot],
            device_id=device, device_id_type=pl.DeviceIdType.MESH)

def neighbours(tier_count):
    dp_id, row_id, col_id = lax.axis_index("dp"), lax.axis_index("row"), lax.axis_index("col")
    line_id, tier_id = dp_id // tier_count, dp_id % tier_count
    flips = [line_id, line_id + 1 - 2 * (line_id % 2), (line_id + 2) % 4, 3 - line_id]
    line = [(flip * tier_count + tier_id, row_id, col_id) for flip in flips]
    core = (dp_id, row_id + 1 - 2 * (row_id % 2), col_id)
    far = (dp_id, (row_id + 2) % 4, col_id)
    col = (dp_id, row_id, 1 - col_id)
    return line_id, flips, line, core, far, col

def meet(peers):
    barrier = pltpu.get_barrier_semaphore()
    for peer in peers:
        pl.semaphore_signal(barrier, inc=1, device_id=peer, device_id_type=pl.DeviceIdType.MESH)
    pl.semaphore_wait(barrier, len(peers))


CH = 2

def gather_kernel(tier_count, order, tok, cot, norm_ref, wq, wu, dh, x_out, b_out, wq_out, wu_out, d_out,
                  tz, cz, ty, xs, send_sems, recv_sems, local_sems):
    line_id, flips, line, core, far, col = neighbours(tier_count)
    bit = (line_id % 2 + lax.axis_index("col")) % 2
    middle = (line_id == 1) | (line_id == 2)
    rows, half = tok.shape
    chunk = rows // CH
    copies = Copies(send_sems, recv_sems)
    sent, mid_sent, local_left, last = [], [], [], []
    n_local = [0]

    def local(src, dst):
        copy = pltpu.make_async_copy(src, dst, local_sems.at[n_local[0]])
        n_local[0] += 1
        copy.start()
        local_left.append(copy)
        return copy

    def settle(copy):
        copy.wait()
        local_left[:] = [c for c in local_left if c is not copy]

    def send(src, dst, device, slot=None):
        copy = copies.make(src, dst, device, slot)
        copy.start()
        sent.append(copy)
        return copy

    def cut(c):
        return pl.ds(c * chunk, chunk)

    class Stream:
        def __init__(self, own, stage, out, normed):
            self.own, self.stage, self.out, self.normed = own, stage, out, normed
            self.line, self.swap, self.spread, self.keep, self.relayed = {}, {}, {}, {}, {}

        def start(self, c):
            own, stage = self.own.at[cut(c)], self.stage
            own_copy = local(own, stage.at[0, cut(c)])
            near = send(own, stage.at[1, cut(c)], line[1])
            two = send(own, stage.at[2, cut(c)], line[2])
            slot = copies.slot()
            three = copies.make(own, stage.at[3, cut(c)], line[3], slot)
            relay = copies.make(stage.at[2, cut(c)], stage.at[3, cut(c)], line[1], slot)
            pl.when(middle)(three.start)
            mid_sent.extend([three, relay])
            self.line[c] = own_copy, near, two, three, relay

        def swap_cols(self, c, p):
            own_copy, near, two, three, relay = self.line[c]
            if p == 0:
                settle(own_copy)
                near.wait_recv()
            else:
                two.wait_recv()
                pl.when(middle)(relay.start)
                three.wait_recv()
            if self.normed:
                dst = ty.at[p, cut(c)]
            else:
                dst = self.out.at[p, 0, cut(c), pl.ds(half, half)]
                self.keep[c, p] = local(self.stage.at[2 * p + bit, cut(c)], self.out.at[p, 0, cut(c), pl.ds(0, half)])
            self.swap[c, p] = send(self.stage.at[2 * p + 1 - bit, cut(c)], dst, col)

        def give(self, c, p):
            self.swap[c, p].wait_recv()
            if self.normed:
                norm(c, p)
                src = xs.at[p, cut(c)]
                local(src, self.out.at[p, 0, cut(c)])
            else:
                settle(self.keep[c, p])
                src = self.out.at[p, 0, cut(c)]
            self.spread[c, p] = send(src, self.out.at[p, 2, cut(c)], far)
            last.append(send(src, self.out.at[p, 1, cut(c)], core))

        def relay(self, c, p):
            self.spread[c, p].wait_recv()
            last.append(send(self.out.at[p, 2, cut(c)], self.out.at[p, 3, cut(c)], core))

    def norm(c, p):
        step = 64
        def body(i, carry):
            at = pl.ds(pl.multiple_of(c * chunk + i * step, step), step)
            one = tz[2 * p + bit, at, :].astype(f32)
            two = ty[p, at, :].astype(f32)
            width = 2 * half
            mean = (jnp.sum(one, axis=-1, keepdims=True) + jnp.sum(two, axis=-1, keepdims=True)) / width
            square = (jnp.sum(one * one, axis=-1, keepdims=True) + jnp.sum(two * two, axis=-1, keepdims=True)) / width
            inv = lax.rsqrt(square - mean * mean + eps_norm)
            xs[p, at, pl.ds(0, half)] = ((one - mean) * inv * norm_ref[0:1, 0:half] + norm_ref[1:2, 0:half]).astype(bf16)
            xs[p, at, pl.ds(half, half)] = ((two - mean) * inv * norm_ref[0:1, half:] + norm_ref[1:2, half:]).astype(bf16)
            return carry
        lax.fori_loop(0, chunk // step, body, 0)

    class Weight:
        def __init__(self, src, out):
            self.src, self.out, self.got = src, out, {}

        def own(self):
            local(self.src.at[line_id], self.out.at[0, line_id])
            last.append(send(self.src.at[line_id], self.out.at[1, line_id], col))

        def start(self):
            for s in (1, 2, 3):
                self.got[s] = send(self.src.at[flips[s]], self.out.at[0, line_id], line[s])

        def swap(self):
            for s in (1, 2, 3):
                self.got[s].wait_recv()
                last.append(send(self.out.at[0, flips[s]], self.out.at[1, flips[s]], col))

    part = dh.shape[0] // 5

    def dense(i):
        at = pl.ds(i * part, part)
        last.append(send(dh.at[at], d_out.at[at, pl.ds(half, half)], col))

    meet([line[1], line[2], line[3], core, far, col])
    T = Stream(tok, tz, x_out, True)
    C = Stream(cot, cz, b_out, False)
    Q = Weight(wq, wq_out)
    U = Weight(wu, wu_out)
    for what, *args in order:
        if what == "Ts": T.start(*args)
        if what == "Ty": T.swap_cols(*args)
        if what == "Tx": T.give(*args)
        if what == "Tk": T.relay(*args)
        if what == "Cs": C.start(*args)
        if what == "Cy": C.swap_cols(*args)
        if what == "Cx": C.give(*args)
        if what == "Ck": C.relay(*args)
        if what == "Qo": Q.own()
        if what == "Qs": Q.start()
        if what == "Qy": Q.swap()
        if what == "Uo": U.own()
        if what == "Us": U.start()
        if what == "Uy": U.swap()
        if what == "D": dense(*args)
        if what == "Dl": local(dh, d_out.at[:, pl.ds(0, half)])
    for copy in last:
        copy.wait_recv()
    for copy in list(local_left):
        settle(copy)
    for copy in sent:
        copy.wait_send()
    for copy in mid_sent:
        pl.when(middle)(copy.wait_send)

ORDER_A = [("Ts",0),("Ts",1),("Qo",),("Uo",),("D",0),("Dl",),
 ("Ty",0,0),("Ty",0,1),("Tx",0,0),("Tx",0,1),
 ("Ty",1,0),("Ty",1,1),("Cs",0),("Tx",1,0),("Tx",1,1),("D",1),("D",2),
 ("Tk",0,0),("Tk",0,1),("Cy",0,0),("Cy",0,1),("Qs",),("Cs",1),("Cx",0,0),("Cx",0,1),("Tk",1,0),("Tk",1,1),
 ("Qy",),("Cy",1,0),("Cy",1,1),("Us",),("Cx",1,0),("Cx",1,1),("D",3),("D",4),("Ck",0,0),("Ck",0,1),
 ("Uy",),("Ck",1,0),("Ck",1,1)]

def gather(tier_count, tok, cot, norm_vec, wq, wu, dh, order=ORDER_A):
    rows, half = tok.shape
    sds = jax.ShapeDtypeStruct
    any_ = pl.BlockSpec(memory_space=pl.ANY)
    return pl.pallas_call(
        functools.partial(gather_kernel, tier_count, order),
        out_shape=[sds((2, 4, rows, 2 * half), bf16), sds((2, 4, rows, 2 * half), bf16),
                   sds((2, *wq.shape), bf16), sds((2, *wu.shape), bf16), sds((dh.shape[0], 2 * half), bf16)],
        in_specs=[any_, any_, pl.BlockSpec(memory_space=pltpu.VMEM), any_, any_, any_],
        out_specs=[any_] * 5,
        scratch_shapes=[pltpu.VMEM((4, rows, half), bf16), pltpu.VMEM((4, rows, half), bf16), pltpu.VMEM((2, rows, half), bf16),
                        pltpu.VMEM((2, rows, 2 * half), bf16),
                        pltpu.SemaphoreType.DMA((80,)), pltpu.SemaphoreType.DMA((80,)), pltpu.SemaphoreType.DMA((24,))],
        compiler_params=pltpu.CompilerParams(collective_id=1, has_side_effects=True, vmem_limit_bytes=32 << 20),
    )(tok, cot, norm_vec, wq, wu, dh)


def per_device(
    tokens,
    cotangent,
    doc_lengths,
    doc_groups,
    w_qkv,
    w_up,
    w_dense,
    w_down,
    vectors,
    m_qkv,
    v_qkv,
    m_up,
    v_up,
    m_dense,
    v_dense,
    m_down,
    v_down,
    m_vec,
    v_vec,
):
    dp_count = lax.axis_size("dp")
    tier_count = dp_count // LINE
    dp_id = lax.axis_index("dp")
    line_id = dp_id // tier_count
    tier_id = dp_id % tier_count
    row_count = lax.axis_size("row")
    col_count = lax.axis_size("col")
    assert row_count == 4 and col_count == 2 and dp_count % LINE == 0
    row_id = lax.axis_index("row")
    col_id = lax.axis_index("col")
    tok_dev, half_width = tokens.shape
    slot_count = tok_dev * row_count
    full_width = half_width * col_count
    row_width = full_width // row_count
    part = row_width // LINE
    heads_dev = part // HDIM
    score_scale = HDIM ** (-0.5)
    zero_index = jnp.int32(0)
    tier_groups = [[line * tier_count + tier for tier in range(tier_count)] for line in range(LINE)]

    def over_line(value, bits):
        pairs = [(i, ((i // tier_count) ^ bits) * tier_count + i % tier_count) for i in range(dp_count)]
        return lax.ppermute(value, "dp", pairs)

    def over_row(value, bits):
        return lax.ppermute(value, "row", [(i, i ^ bits) for i in range(row_count)])

    def over_col(value):
        return lax.ppermute(value, "col", [(0, 1), (1, 0)])

    def reorder(blocks, place):
        one = (place & 1) == 1
        two = (place & 2) == 2
        blocks = [jnp.where(one, blocks[i ^ 1], blocks[i]) for i in range(4)]
        return [jnp.where(two, blocks[i ^ 2], blocks[i]) for i in range(4)]

    def sum_all(value):
        value = sum(reorder([value] + [over_line(value, s) for s in (1, 2, 3)], line_id))
        value = sum(reorder([value] + [over_row(value, s) for s in (1, 2, 3)], row_id))
        value = value + over_col(value)
        if tier_count > 1:
            value = lax.psum(value, "dp", axis_index_groups=tier_groups)
        return value

    odd = ((line_id & 1) ^ col_id) == 1
    first_bits = (line_id & 1) ^ col_id
    part_start = row_id * row_width + line_id * part
    col_start = col_id * half_width

    def by_half(vector):
        mine = lax.dynamic_slice_in_dim(vector, col_start, half_width, 0)
        other = lax.dynamic_slice_in_dim(vector, (1 - col_id) * half_width, half_width, 0)
        return jnp.concatenate([mine, other])

    places = jnp.concatenate(
        [(row_id ^ t) * tok_dev + jnp.arange(tok_dev, dtype=jnp.int32) for t in range(4)]
    )
    segments, cosines, sines = [], [], []
    for p in range(2):
        group_id = (line_id ^ first_bits ^ (2 * p)) * tier_count + tier_id
        segment, position, unused = seq_layout(doc_lengths, doc_groups, group_id, places)
        cos_part, sin_part = turn_angles(position)
        segments.append(segment)
        cosines.append(cos_part)
        sines.append(sin_part)
    cos_part = jnp.stack(cosines)
    sin_part = jnp.stack(sines)
    total_len = jnp.sum(jnp.where(doc_groups == dp_id, doc_lengths, 0), dtype=jnp.int32)
    own_valid = places[:tok_dev] < total_len
    back_own = jnp.where(own_valid[:, None], cotangent, jnp.zeros_like(cotangent))

    def tier_gather(value):
        if tier_count > 1:
            value = lax.all_gather(value, "dp", axis=0, tiled=True, axis_index_groups=tier_groups)
        return value

    def pieces_of(weight):
        low = tier_gather(weight.astype(bf16))
        rows, parts = low.shape[:2]
        return low.reshape(rows, parts, LINE, part).transpose(2, 0, 1, 3).reshape(LINE, rows, parts * part)

    down_low = tier_gather(w_down.astype(bf16)).transpose(1, 0, 2).reshape(4 * part, half_width)
    out_low = jnp.concatenate([tier_gather(w_dense.astype(bf16)), down_low], axis=0)
    norm_vec = jnp.stack([by_half(vectors[0]), by_half(vectors[1])])
    normed, back, qkv_mat, up_mat, out_mat = gather(
        tier_count, tokens, back_own, norm_vec, pieces_of(w_qkv), pieces_of(w_up), out_low
    )
    rows_all = 2 * slot_count
    normed = normed.reshape(rows_all, full_width)
    back = back.reshape(rows_all, full_width)
    qkv_mat = qkv_mat.reshape(full_width, 3 * part)
    up_mat = up_mat.reshape(full_width, 4 * part)
    dense_mat = out_mat[:part]
    down_mat = out_mat[part:]

    bias_qkv = lax.dynamic_slice(vectors[2:5], (zero_index, part_start), (3, part)).reshape(3 * part)
    bias_up = lax.dynamic_slice(vectors[5:9], (zero_index, part_start), (4, part)).reshape(4 * part)

    def mm(a, b):
        return jnp.dot(a, b, preferred_element_type=f32)

    def mm_t(a, b):
        return lax.dot_general(a, b, (((1,), (1,)), ((), ())), preferred_element_type=f32)

    def t_mm(a, b):
        return lax.dot_general(a, b, (((0,), (0,)), ((), ())), preferred_element_type=f32)

    pre_qkv = mm(normed, qkv_mat) + bias_qkv
    heads_view = pre_qkv.reshape(2, slot_count, 3, heads_dev, HDIM)
    queries = rotate(heads_view[:, :, 0], cos_part, sin_part).astype(bf16)
    key_rows = rotate(heads_view[:, :, 1], cos_part, sin_part).astype(bf16)
    values = heads_view[:, :, 2].astype(bf16)
    segment_all = jnp.stack(segments)
    allowed = (segment_all[:, :, None] == segment_all[:, None, :]) & (
        places[None, :, None] >= places[None, None, :]
    )

    def scores_of():
        scores = (
            jnp.einsum("pqhd,pkhd->phqk", queries, key_rows, preferred_element_type=f32) * score_scale
        )
        return jnp.where(allowed[:, None], scores, -1e30)

    scores = scores_of()
    top_score = jnp.max(scores, axis=-1, keepdims=True)
    weights = jnp.exp(scores - top_score)
    denominator = jnp.sum(weights, axis=-1, keepdims=True)
    probs_low = (weights / denominator).astype(bf16)
    attn = jnp.einsum("phqk,pkhd->pqhd", probs_low, values, preferred_element_type=f32)
    attn = attn.reshape(rows_all, part).astype(bf16)
    total = top_score + jnp.log(denominator)

    pre_up = mm(normed, up_mat) + bias_up
    hidden = jax.nn.gelu(pre_up, approximate=True).astype(bf16)

    def scatter_rows(partial):
        low = partial.astype(bf16).reshape(2, 4, tok_dev, full_width)
        kept = []
        for p in range(2):
            near = low[p, 0::2].astype(f32) + over_row(low[p, 1::2], 1).astype(f32)
            mine = near[0] + over_row(near[1].astype(bf16), 2).astype(f32)
            kept.append(mine.astype(bf16))
        out = None
        for p in (1, 0):
            mine = kept[p][:, :half_width]
            theirs = over_col(kept[p][:, half_width:])
            even_block = jnp.where(odd, theirs, mine)
            odd_block = jnp.where(odd, mine, theirs)
            first = over_line(even_block, 2) if p else even_block
            both = first.astype(f32) + over_line(odd_block, 2 * p + 1).astype(f32)
            out = both if out is None else out + both
        return out

    branch = scatter_rows(mm(attn, dense_mat) + mm(hidden, down_mat))
    out_bias = lax.dynamic_slice_in_dim(vectors[9] + vectors[10], col_start, half_width, 0)
    block_out = (tokens.astype(f32) + branch + out_bias[None, :]).astype(bf16)

    d_attn = mm_t(back, dense_mat).astype(bf16).reshape(2, slot_count, heads_dev, HDIM)
    d_hidden = mm_t(back, down_mat)
    unused_value, gelu_back = jax.vjp(lambda inputs: jax.nn.gelu(inputs, approximate=True), pre_up)
    d_pre_up = gelu_back(d_hidden)[0].astype(bf16)

    probs_full = jnp.exp(scores_of() - total)
    probs_back = probs_full.astype(bf16)
    d_probs = jnp.einsum("pqhd,pkhd->phqk", d_attn, values, preferred_element_type=f32)
    delta_rows = jnp.sum(probs_full * d_probs, axis=-1, keepdims=True)
    d_scores = (probs_full * (d_probs - delta_rows)).astype(bf16)
    d_queries = jnp.einsum("phqk,pkhd->pqhd", d_scores, key_rows, preferred_element_type=f32) * score_scale
    d_keys = jnp.einsum("phqk,pqhd->pkhd", d_scores, queries, preferred_element_type=f32) * score_scale
    d_values = jnp.einsum("phqk,pqhd->pkhd", probs_back, d_attn, preferred_element_type=f32)
    d_qkv = jnp.stack(
        [rotate(d_queries, cos_part, -sin_part), rotate(d_keys, cos_part, -sin_part), d_values], axis=2
    )
    d_qkv = d_qkv.astype(bf16).reshape(rows_all, 3 * part)

    def scatter_out(grad):
        return grad[:, :half_width] + over_col(grad[:, half_width:].astype(bf16)).astype(f32)

    def tier_sum(value):
        if tier_count > 1:
            value = lax.psum_scatter(
                value, "dp", scatter_dimension=0, tiled=True, axis_index_groups=tier_groups
            )
        return value

    red_dense = tier_sum(scatter_out(t_mm(attn, back)))
    red_down = scatter_out(t_mm(hidden, back)).reshape(4, part, half_width).transpose(1, 0, 2)
    red_down = tier_sum(red_down)

    def scatter_in(grad, parts):
        half = grad[:half_width] + over_col(grad[half_width:].astype(bf16)).astype(f32)
        low = half.astype(bf16)
        rows = half_width // LINE
        pieces = []
        for s in range(LINE):
            piece = lax.dynamic_slice_in_dim(low, (line_id ^ s) * rows, rows, 0)
            piece = over_line(piece, s) if s else piece
            pieces.append(piece.reshape(rows, parts, part))
        own = jnp.concatenate(reorder(pieces, line_id), axis=2)
        return tier_sum(own.astype(f32))

    red_up = scatter_in(t_mm(normed, d_pre_up), 4)
    red_qkv = scatter_in(t_mm(normed, d_qkv), 3)

    d_normed = scatter_rows(mm_t(d_qkv, qkv_mat) + mm_t(d_pre_up, up_mat))
    tokens_own = tokens.astype(f32)
    own_sums = jnp.stack([jnp.sum(tokens_own, axis=-1), jnp.sum(tokens_own * tokens_own, axis=-1)])
    own_sums = (own_sums + over_col(own_sums)) / full_width
    mean_own = own_sums[0][:, None]
    inv_own = lax.rsqrt(own_sums[1][:, None] - mean_own * mean_own + eps_norm)
    centred = (tokens_own - mean_own) * inv_own
    gain_cols = lax.dynamic_slice_in_dim(vectors[0], col_start, half_width, 0)
    d_hat = d_normed * gain_cols[None, :]
    hat_sums = jnp.stack([jnp.sum(d_hat, axis=-1), jnp.sum(d_hat * centred, axis=-1)])
    hat_sums = (hat_sums + over_col(hat_sums)) / full_width
    back_float = back_own.astype(f32)
    grad_tokens = inv_own * (d_hat - hat_sums[0][:, None] - centred * hat_sums[1][:, None]) + back_float

    early = jnp.zeros((9, full_width), f32)
    early = lax.dynamic_update_slice(
        early, jnp.sum(d_qkv.astype(f32), axis=0).reshape(3, part), (zero_index, part_start)
    )
    early = lax.dynamic_update_slice(
        early, jnp.sum(d_pre_up.astype(f32), axis=0).reshape(4, part), (jnp.int32(3), part_start)
    )
    out_sums = jnp.sum(back_float, axis=0)
    early = lax.dynamic_update_slice(early, jnp.stack([out_sums, out_sums]), (jnp.int32(7), col_start))
    late = lax.dynamic_update_slice(
        jnp.zeros((2, full_width), f32),
        jnp.stack([jnp.sum(d_normed * centred, axis=0), jnp.sum(d_normed, axis=0)]),
        (zero_index, col_start),
    )
    vec_grad = jnp.concatenate([sum_all(late), sum_all(early)], axis=0)
    qkv_new = adamw(w_qkv, m_qkv, v_qkv, red_qkv, D ** (-0.5), 0.1)
    up_new = adamw(w_up, m_up, v_up, red_up, D ** (-0.5), 0.1)
    dense_new = adamw(w_dense, m_dense, v_dense, red_dense, max(D // 128, 4) ** (-0.5), 0.1)
    down_new = adamw(w_down, m_down, v_down, red_down, FF ** (-0.5), 0.1)
    vec_new = adamw(vectors, m_vec, v_vec, vec_grad, 0.5, 0.0)
    return (
        block_out,
        grad_tokens,
        qkv_new[0],
        qkv_new[1],
        qkv_new[2],
        up_new[0],
        up_new[1],
        up_new[2],
        dense_new[0],
        dense_new[1],
        dense_new[2],
        down_new[0],
        down_new[1],
        down_new[2],
        vec_new[0],
        vec_new[1],
        vec_new[2],
    )


def solution(mesh):
    placed = (
        P(("dp", "row"), "col"),
        P(("dp", "row"), "col"),
        P(),
        P(),
        P(("col", "dp"), None, "row"),
        P(("col", "dp"), None, "row"),
        P(("row", "dp"), "col"),
        P(("row", "dp"), None, "col"),
        P(),
        P(("col", "dp"), None, "row"),
        P(("col", "dp"), None, "row"),
        P(("col", "dp"), None, "row"),
        P(("col", "dp"), None, "row"),
        P(("row", "dp"), "col"),
        P(("row", "dp"), "col"),
        P(("row", "dp"), None, "col"),
        P(("row", "dp"), None, "col"),
        P(),
        P(),
    )
    return jax.shard_map(
        per_device,
        mesh=mesh,
        in_specs=placed,
        out_specs=(
            P(("dp", "row"), "col"),
            P(("dp", "row"), "col"),
            P(("col", "dp"), None, "row"),
            P(("col", "dp"), None, "row"),
            P(("col", "dp"), None, "row"),
            P(("col", "dp"), None, "row"),
            P(("col", "dp"), None, "row"),
            P(("col", "dp"), None, "row"),
            P(("row", "dp"), "col"),
            P(("row", "dp"), "col"),
            P(("row", "dp"), "col"),
            P(("row", "dp"), None, "col"),
            P(("row", "dp"), None, "col"),
            P(("row", "dp"), None, "col"),
            P(),
            P(),
            P(),
        ),
        check_vma=False,
    )
```

```python
import functools

import jax
import jax.numpy as jnp
from jax import lax
from jax.experimental import pallas as pl
from jax.experimental.pallas import tpu as pltpu
from jax.sharding import PartitionSpec as P

D = 2048
HDIM = 64
ROT = 32
FF = 8192
BLK = 512
STEP = 10
LINE = 4


eps_norm = 1e-05
f32 = jnp.float32
bf16 = jnp.bfloat16


def seq_layout(doc_lengths, doc_groups, group_id, places):
    in_group = (doc_groups == group_id).astype(jnp.int32)
    group_sizes = doc_lengths * in_group
    seq_ends = jnp.cumsum(group_sizes, dtype=jnp.int32)
    starts = seq_ends - group_sizes
    total_len = jnp.sum(group_sizes, dtype=jnp.int32)
    member = (
        (places[:, None] >= starts[None, :])
        & (places[:, None] < seq_ends[None, :])
        & (in_group[None, :] == 1)
    )
    member = member.astype(jnp.int32)
    number = jnp.arange(doc_lengths.shape[0], dtype=jnp.int32) + 1
    segment = jnp.sum(member * number[None, :], axis=1, dtype=jnp.int32) - 1
    seq_first = jnp.sum(member * starts[None, :], axis=1, dtype=jnp.int32)
    position = jnp.where(segment >= 0, places - seq_first, places - total_len)
    return position


def turn_angles(position):
    half_rot = ROT // 2
    freq_base = jnp.power(10000.0, -2.0 * jnp.arange(half_rot, dtype=jnp.float32) / ROT)
    angle = position.astype(jnp.float32)[..., None] * freq_base
    return (jnp.cos(angle), jnp.sin(angle))


def adamw(weight, first_moment, second_moment, gradient, rate, decay):
    first_next = 0.9 * first_moment + 0.1 * gradient
    second_next = 0.95 * second_moment + 0.05 * gradient * gradient
    correct_one = 1.0 - 0.9**STEP
    correct_two = 1.0 - 0.95**STEP
    update = first_next / correct_one / (jnp.sqrt(second_next / correct_two) + 1e-08)
    return (first_next, second_next, weight - rate * (update + decay * weight))


class Copies:
    def __init__(self, send_sems, recv_sems):
        self.send_sems, self.recv_sems, self.sent, self.received = send_sems, recv_sems, 0, 0

    def slot(self):
        self.received += 1
        return self.received - 1

    def make(self, src, dst, device, slot=None):
        slot = self.slot() if slot is None else slot
        self.sent += 1
        return pltpu.make_async_remote_copy(
            src_ref=src, dst_ref=dst, send_sem=self.send_sems.at[self.sent - 1], recv_sem=self.recv_sems.at[slot],
            device_id=device, device_id_type=pl.DeviceIdType.MESH)

def neighbours(tier_count):
    dp_id, row_id, col_id = lax.axis_index("dp"), lax.axis_index("row"), lax.axis_index("col")
    line_id, tier_id = dp_id // tier_count, dp_id % tier_count
    flips = [line_id, line_id + 1 - 2 * (line_id % 2), (line_id + 2) % 4, 3 - line_id]
    line = [(flip * tier_count + tier_id, row_id, col_id) for flip in flips]
    core = (dp_id, row_id + 1 - 2 * (row_id % 2), col_id)
    far = (dp_id, (row_id + 2) % 4, col_id)
    col = (dp_id, row_id, 1 - col_id)
    return line_id, flips, line, core, far, col

def meet(peers):
    barrier = pltpu.get_barrier_semaphore()
    for peer in peers:
        pl.semaphore_signal(barrier, inc=1, device_id=peer, device_id_type=pl.DeviceIdType.MESH)
    pl.semaphore_wait(barrier, len(peers))


CH = 2

def gather_kernel(tier_count, order, tok, cot, norm_ref, wq, wu, dh, x_out, b_out, wq_out, wu_out, d_out,
                  tz, cz, ty, xs, send_sems, recv_sems, local_sems):
    line_id, flips, line, core, far, col = neighbours(tier_count)
    bit = (line_id % 2 + lax.axis_index("col")) % 2
    middle = (line_id == 1) | (line_id == 2)
    rows, half = tok.shape
    chunk = rows // CH
    copies = Copies(send_sems, recv_sems)
    sent, mid_sent, local_left, last = [], [], [], []
    n_local = [0]

    def local(src, dst):
        copy = pltpu.make_async_copy(src, dst, local_sems.at[n_local[0]])
        n_local[0] += 1
        copy.start()
        local_left.append(copy)
        return copy

    def settle(copy):
        copy.wait()
        local_left[:] = [c for c in local_left if c is not copy]

    def send(src, dst, device, slot=None):
        copy = copies.make(src, dst, device, slot)
        copy.start()
        sent.append(copy)
        return copy

    def cut(c):
        return pl.ds(c * chunk, chunk)

    class Stream:
        def __init__(self, own, stage, out, normed):
            self.own, self.stage, self.out, self.normed = own, stage, out, normed
            self.line, self.swap, self.spread, self.keep, self.relayed = {}, {}, {}, {}, {}

        def start(self, c):
            own, stage = self.own.at[cut(c)], self.stage
            own_copy = local(own, stage.at[0, cut(c)])
            near = send(own, stage.at[1, cut(c)], line[1])
            two = send(own, stage.at[2, cut(c)], line[2])
            slot = copies.slot()
            three = copies.make(own, stage.at[3, cut(c)], line[3], slot)
            relay = copies.make(stage.at[2, cut(c)], stage.at[3, cut(c)], line[1], slot)
            pl.when(middle)(three.start)
            mid_sent.extend([three, relay])
            self.line[c] = own_copy, near, two, three, relay

        def swap_cols(self, c, p):
            own_copy, near, two, three, relay = self.line[c]
            if p == 0:
                settle(own_copy)
                near.wait_recv()
            else:
                two.wait_recv()
                pl.when(middle)(relay.start)
                three.wait_recv()
            if self.normed:
                dst = ty.at[p, cut(c)]
            else:
                dst = self.out.at[p, 0, cut(c), pl.ds(half, half)]
                self.keep[c, p] = local(self.stage.at[2 * p + bit, cut(c)], self.out.at[p, 0, cut(c), pl.ds(0, half)])
            self.swap[c, p] = send(self.stage.at[2 * p + 1 - bit, cut(c)], dst, col)

        def give(self, c, p):
            self.swap[c, p].wait_recv()
            if self.normed:
                norm(c, p)
                src = xs.at[p, cut(c)]
                local(src, self.out.at[p, 0, cut(c)])
            else:
                settle(self.keep[c, p])
                src = self.out.at[p, 0, cut(c)]
            self.spread[c, p] = send(src, self.out.at[p, 2, cut(c)], far)
            last.append(send(src, self.out.at[p, 1, cut(c)], core))

        def relay(self, c, p):
            self.spread[c, p].wait_recv()
            last.append(send(self.out.at[p, 2, cut(c)], self.out.at[p, 3, cut(c)], core))

    def norm(c, p):
        step = 64
        def body(i, carry):
            at = pl.ds(pl.multiple_of(c * chunk + i * step, step), step)
            one = tz[2 * p + bit, at, :].astype(f32)
            two = ty[p, at, :].astype(f32)
            width = 2 * half
            mean = (jnp.sum(one, axis=-1, keepdims=True) + jnp.sum(two, axis=-1, keepdims=True)) / width
            square = (jnp.sum(one * one, axis=-1, keepdims=True) + jnp.sum(two * two, axis=-1, keepdims=True)) / width
            inv = lax.rsqrt(square - mean * mean + eps_norm)
            xs[p, at, pl.ds(0, half)] = ((one - mean) * inv * norm_ref[0:1, 0:half] + norm_ref[1:2, 0:half]).astype(bf16)
            xs[p, at, pl.ds(half, half)] = ((two - mean) * inv * norm_ref[0:1, half:] + norm_ref[1:2, half:]).astype(bf16)
            return carry
        lax.fori_loop(0, chunk // step, body, 0)

    class Weight:
        def __init__(self, src, out):
            self.src, self.out, self.got = src, out, {}

        def own(self):
            local(self.src.at[line_id], self.out.at[0, line_id])
            last.append(send(self.src.at[line_id], self.out.at[1, line_id], col))

        def start(self):
            for s in (1, 2, 3):
                self.got[s] = send(self.src.at[flips[s]], self.out.at[0, line_id], line[s])

        def swap(self):
            for s in (1, 2, 3):
                self.got[s].wait_recv()
                last.append(send(self.out.at[0, flips[s]], self.out.at[1, flips[s]], col))

    part = dh.shape[0] // 5

    def dense(i):
        at = pl.ds(i * part, part)
        last.append(send(dh.at[at], d_out.at[at, pl.ds(half, half)], col))

    meet([line[1], line[2], line[3], core, far, col])
    T = Stream(tok, tz, x_out, True)
    C = Stream(cot, cz, b_out, False)
    Q = Weight(wq, wq_out)
    U = Weight(wu, wu_out)
    for what, *args in order:
        if what == "Ts": T.start(*args)
        if what == "Ty": T.swap_cols(*args)
        if what == "Tx": T.give(*args)
        if what == "Tk": T.relay(*args)
        if what == "Cs": C.start(*args)
        if what == "Cy": C.swap_cols(*args)
        if what == "Cx": C.give(*args)
        if what == "Ck": C.relay(*args)
        if what == "Qo": Q.own()
        if what == "Qs": Q.start()
        if what == "Qy": Q.swap()
        if what == "Uo": U.own()
        if what == "Us": U.start()
        if what == "Uy": U.swap()
        if what == "D": dense(*args)
        if what == "Dl": local(dh, d_out.at[:, pl.ds(0, half)])
    for copy in last:
        copy.wait_recv()
    for copy in list(local_left):
        settle(copy)
    for copy in sent:
        copy.wait_send()
    for copy in mid_sent:
        pl.when(middle)(copy.wait_send)

ORDER_A = [("Ts",0),("Ts",1),("Qo",),("Uo",),("D",0),("Dl",),
 ("Ty",0,0),("Ty",0,1),("Tx",0,0),("Tx",0,1),
 ("Ty",1,0),("Ty",1,1),("Cs",0),("Tx",1,0),("Tx",1,1),("D",1),("D",2),
 ("Tk",0,0),("Tk",0,1),("Cy",0,0),("Cy",0,1),("Qs",),("Cs",1),("Cx",0,0),("Cx",0,1),("Tk",1,0),("Tk",1,1),
 ("Qy",),("Cy",1,0),("Cy",1,1),("Us",),("Cx",1,0),("Cx",1,1),("D",3),("D",4),("Ck",0,0),("Ck",0,1),
 ("Uy",),("Ck",1,0),("Ck",1,1)]

def gather(tier_count, tok, cot, norm_vec, wq, wu, dh, order=ORDER_A):
    rows, half = tok.shape
    sds = jax.ShapeDtypeStruct
    any_ = pl.BlockSpec(memory_space=pl.ANY)
    return pl.pallas_call(
        functools.partial(gather_kernel, tier_count, order),
        out_shape=[sds((2, 4, rows, 2 * half), bf16), sds((2, 4, rows, 2 * half), bf16),
                   sds((2, *wq.shape), bf16), sds((2, *wu.shape), bf16), sds((dh.shape[0], 2 * half), bf16)],
        in_specs=[any_, any_, pl.BlockSpec(memory_space=pltpu.VMEM), any_, any_, any_],
        out_specs=[any_] * 5,
        scratch_shapes=[pltpu.VMEM((4, rows, half), bf16), pltpu.VMEM((4, rows, half), bf16), pltpu.VMEM((2, rows, half), bf16),
                        pltpu.VMEM((2, rows, 2 * half), bf16),
                        pltpu.SemaphoreType.DMA((80,)), pltpu.SemaphoreType.DMA((80,)), pltpu.SemaphoreType.DMA((24,))],
        compiler_params=pltpu.CompilerParams(collective_id=1, has_side_effects=True, vmem_limit_bytes=32 << 20),
    )(tok, cot, norm_vec, wq, wu, dh)

def mm(a, b):
    return jnp.dot(a, b, preferred_element_type=f32)


def mm_t(a, b):
    return lax.dot_general(a, b, (((1,), (1,)), ((), ())), preferred_element_type=f32)


def t_mm(a, b):
    return lax.dot_general(a, b, (((0,), (0,)), ((), ())), preferred_element_type=f32)


def gelu_both(v):
    root = 0.7978845608028654
    square = v * v
    slope = root * (1.0 + 3 * 0.044715 * square)
    tanh = jnp.tanh(root * v * (1.0 + 0.044715 * square))
    outer = 0.5 * (1.0 + tanh)
    return v * outer, outer + 0.5 * v * (1.0 - tanh * tanh) * slope


def local_kernel(x_ref, b_ref, wq_ref, wu_ref, d_ref, bias_ref, cos_ref, lead_ref, trail_ref, from_ref, place_ref, key_ref,
                 attn_ref, hidden_ref, dqkv_ref, dup_ref, sums_ref,
                 q_s, k_s, v_s, da_s, dk_s, dv_s):
    slots, part = q_s.shape
    qb = 256
    scale = HDIM ** (-0.5)
    quarter = ROT // 2

    def turn(value, at, sign):
        left = jnp.roll(value, -quarter, axis=1)
        right = jnp.roll(value, quarter, axis=1)
        return value * cos_ref[0, at, :] + sign * (left * lead_ref[0, at, :] + right * trail_ref[0, at, :])

    def project(i, carry):
        at = pl.ds(pl.multiple_of(i * qb, qb), qb)
        pre = mm(x_ref[0, at, :], wq_ref[...]) + bias_ref[0:1, 0:3 * part]
        q_s[at, :] = (turn(pre[:, 0:part], at, 1.0)).astype(bf16)
        k_s[at, :] = (turn(pre[:, part:2 * part], at, 1.0)).astype(bf16)
        v_s[at, :] = pre[:, 2 * part:].astype(bf16)
        back = b_ref[0, at, :]
        da_s[at, :] = mm_t(back, d_ref[0:part, :]).astype(bf16)
        return carry

    lax.fori_loop(0, slots // qb, project, 0)

    def up(i, carry):
        at = pl.ds(pl.multiple_of(i * qb, qb), qb)
        pre = mm(x_ref[0, at, :], wu_ref[...]) + bias_ref[0:1, 3 * part:]
        value, slope = gelu_both(pre)
        hidden_ref[0, at, :] = value.astype(bf16)
        d_up = (mm_t(b_ref[0, at, :], d_ref[part:, :]) * slope).astype(bf16)
        dup_ref[0, at, :] = d_up
        return carry + jnp.sum(d_up.astype(f32), axis=0, keepdims=True)

    up_sum = lax.fori_loop(0, slots // qb, up, jnp.zeros((1, 4 * part), f32))
    sums_ref[0, 0:1, 3 * part:] = up_sum

    dk_s[...] = jnp.zeros_like(dk_s)
    dv_s[...] = jnp.zeros_like(dv_s)
    lane = lax.broadcasted_iota(jnp.int32, (qb, part), 1)

    def attend(i, q_sum):
        at = pl.ds(pl.multiple_of(i * qb, qb), qb)
        key_place = key_ref[0:1, :]
        allowed = (key_place >= from_ref[0, at, :]) & (key_place <= place_ref[0, at, :])
        queries, d_attn = q_s[at, :], da_s[at, :]
        out = jnp.zeros((qb, part), f32)
        d_q = jnp.zeros((qb, part), f32)
        for h in range(part // HDIM):
            head = (lane >= h * HDIM) & (lane < (h + 1) * HDIM)
            q_h = jnp.where(head, queries, jnp.zeros_like(queries))
            da_h = jnp.where(head, d_attn, jnp.zeros_like(d_attn))
            scores = jnp.where(allowed, mm_t(q_h, k_s[...]) * scale, -1e30)
            weights = jnp.exp(scores - jnp.max(scores, axis=-1, keepdims=True))
            probs = weights * (1.0 / jnp.sum(weights, axis=-1, keepdims=True))
            low = probs.astype(bf16)
            d_probs = mm_t(da_h, v_s[...])
            delta = jnp.sum(probs * d_probs, axis=-1, keepdims=True)
            d_scores = (probs * (d_probs - delta)).astype(bf16)
            out = jnp.where(head, mm(low, v_s[...]), out)
            d_q = jnp.where(head, mm(d_scores, k_s[...]), d_q)
            dk_s[...] += t_mm(q_h, d_scores)
            dv_s[...] += t_mm(da_h, low)
        attn_ref[0, at, :] = out.astype(bf16)
        d_q = turn(d_q * scale, at, -1.0).astype(bf16)
        dqkv_ref[0, at, 0:part] = d_q
        return q_sum + jnp.sum(d_q.astype(f32), axis=0, keepdims=True)

    sums_ref[0, 0:1, 0:part] = lax.fori_loop(0, slots // qb, attend, jnp.zeros((1, part), f32))
    whole = pl.ds(0, slots)
    d_k = turn(dk_s[...].T * scale, whole, -1.0).astype(bf16)
    d_v = dv_s[...].T.astype(bf16)
    dqkv_ref[0, :, part:2 * part] = d_k
    dqkv_ref[0, :, 2 * part:] = d_v
    sums_ref[0, 0:1, part:2 * part] = jnp.sum(d_k.astype(f32), axis=0, keepdims=True)
    sums_ref[0, 0:1, 2 * part:3 * part] = jnp.sum(d_v.astype(f32), axis=0, keepdims=True)


def local_part(normed, back, qkv_mat, up_mat, out_mat, bias, cosine, lead, trail, first, place, key_place):
    groups, slots, width = normed.shape
    part = out_mat.shape[0] // 5

    def each(last):
        return pl.BlockSpec((1, slots, last), lambda p: (p, 0, 0))

    def once(value):
        return pl.BlockSpec(value.shape, lambda p: (0,) * value.ndim, pipeline_mode=pl.Buffered(1))

    def like(last, kind=bf16):
        return jax.ShapeDtypeStruct((groups, slots, last), kind)

    return pl.pallas_call(
        local_kernel,
        grid=(groups,),
        out_shape=[like(part), like(4 * part), like(3 * part), like(4 * part), jax.ShapeDtypeStruct((groups, 8, 7 * part), f32)],
        in_specs=[each(width), each(width), once(qkv_mat), once(up_mat), once(out_mat), once(bias),
                  each(part), each(part), each(part), each(1), each(1), once(key_place)],
        out_specs=[each(part), each(4 * part), each(3 * part), each(4 * part), pl.BlockSpec((1, 8, 7 * part), lambda p: (p, 0, 0))],
        scratch_shapes=[pltpu.VMEM((slots, part), bf16)] * 4 + [pltpu.VMEM((part, slots), f32)] * 2,
        compiler_params=pltpu.CompilerParams(vmem_limit_bytes=56 << 20),
    )(normed, back, qkv_mat, up_mat, out_mat, bias, cosine, lead, trail, first, place, key_place)

def scatter_kernel(tier_count, order, attn, hidden, dqkv, dup, x_in, b_in, wq, wu, dm, tok, bias_ref,
                   block_out, dn_out, g_out, gd_out,
                   a_v, h_v, q_v, u_v, wq_v, wu_v, d_v, at_v, col_v, part_s, near_r, far_r, line_s, line_r,
                   go_s, go_r, gm_s, do_s, do_r, dm_s, dn_s, send_sems, recv_sems, load_sems, col_sems):
    line_id, flips, line, core, far, col = neighbours(tier_count)
    bit = (line_id % 2 + lax.axis_index("col")) % 2
    middle = (line_id == 1) | (line_id == 2)
    ends = (line_id == 0) | (line_id == 3)
    rows, half = tok.shape
    chunk = rows // CH
    width = 2 * half
    step = half // 2
    part = a_v.shape[1]
    block = half // 4
    copies = Copies(send_sems, recv_sems)
    loads = []
    for src, dst in ((attn, a_v), (hidden, h_v), (dm, d_v), (dup, u_v), (dqkv, q_v), (wu, wu_v), (wq, wq_v)):
        load = pltpu.make_async_copy(src, dst, load_sems.at[len(loads)])
        load.start()
        loads.append([load, False])

    def need(*which):
        for i in which:
            if not loads[i][1]:
                loads[i][0].wait()
                loads[i][1] = True

    sent = []

    def send(src, dst, device, when=None, slot=None):
        copy = copies.make(src, dst, device, slot)
        if when is None:
            copy.start()
        else:
            pl.when(when)(copy.start)
        sent.append([copy, when])
        return copy

    def wait_sent(copy):
        for entry in sent:
            if entry[0] is copy:
                sent[:] = [e for e in sent if e is not entry]
                if entry[1] is None:
                    copy.wait_send()
                else:
                    pl.when(entry[1])(copy.wait_send)

    wanted = []
    for what, *args in order:
        if what in ("go", "gm"):
            first = flips[args[0]] * block + (half if what == "go" else 0)
            wanted.append((x_in, first))
        if what in ("do", "dm"):
            wanted.append((b_in, args[0] * block + (half if what == "do" else 0)))
    taken = [0]
    fetches = []

    def fetch(i):
        src, first = wanted[i]
        if not isinstance(first, int):
            first = pl.multiple_of(first, block)
        copy = pltpu.make_async_copy(src.at[:, pl.ds(first, block)], col_v.at[i % 2], col_sems.at[i % 2])
        copy.start()
        fetches.append(copy)

    def take():
        i = taken[0]
        taken[0] += 1
        if i + 1 < len(wanted):
            fetch(i + 1)
        fetches[i].wait()
        return col_v.at[i % 2]

    if wanted:
        fetch(0)
    meet([line[1], line[2], line[3], core, far, col])

    def cut(c):
        return pl.ds(c * chunk, chunk)

    class Stream:
        def __init__(self, number):
            self.number = number
            self.near, self.far, self.col, self.one, self.two, self.three, self.relay = {}, {}, {}, {}, {}, {}, {}

        def compute(self, p, c):
            place = 2 * p + c
            out = part_s.at[place]
            if self.number:
                for copy in old.near[p, c] + [old.far[p, c], old.col[p, c]]:
                    wait_sent(copy)
                left, right = (q_v, wq_v), (u_v, wu_v)
                need(3, 4, 5, 6)
            else:
                left, right = (a_v, None), (h_v, None)
                need(0, 1, 2)

            def body(n, carry):
                at = pl.ds(pl.multiple_of(n * step, step), step)

                def lhs(ref):
                    base = p * 4 * rows + c * chunk
                    return jnp.concatenate([ref[pl.ds(base + t * rows, chunk), :] for t in range(4)], axis=0)

                if self.number:
                    total = mm_t(lhs(q_v), wq_v[at, :]) + mm_t(lhs(u_v), wu_v[at, :])
                else:
                    total = mm(lhs(a_v), d_v[0:part, at]) + mm(lhs(h_v), d_v[part:, at])
                low = total.astype(bf16)
                for t in range(4):
                    out[t, :, at] = low[t * chunk:(t + 1) * chunk]
                return carry

            lax.fori_loop(0, width // step, body, 0)
            into = near_r.at[4 * self.number + place]
            self.near[p, c] = [send(out.at[1], into.at[0], core), send(out.at[3], into.at[1], core)]

        def give_far(self, p, c):
            place = 2 * p + c
            self.near[p, c][1].wait_recv()
            mine = part_s.at[place, 2]
            mine[...] = (mine[...].astype(f32) + near_r[4 * self.number + place, 1].astype(f32)).astype(bf16)
            self.far[p, c] = send(mine, far_r.at[4 * self.number + place], far)

        def give_col(self, p, c):
            place = 2 * p + c
            self.near[p, c][0].wait_recv()
            self.far[p, c].wait_recv()
            mine = part_s.at[place, 0]
            total = mine[...].astype(f32) + near_r[4 * self.number + place, 0].astype(f32)
            total = (total + far_r[4 * self.number + place].astype(f32)).astype(bf16)
            line_s[self.number, 2 * p + bit, cut(c), :] = total[:, :half]
            mine[:, pl.ds(half, half)] = total[:, half:]
            self.col[p, c] = send(mine.at[:, pl.ds(half, half)], line_s.at[self.number, 2 * p + bit, cut(c)], col)

        def give_line(self, p, c):
            self.col[p, c].wait_recv()
            own, got = line_s.at[self.number], line_r.at[self.number]
            if p == 0:
                self.one[c] = send(own.at[1, cut(c)], got.at[0, cut(c)], line[1])
            else:
                self.relay[c] = send(own.at[3, cut(c)], got.at[3, cut(c)], line[1], ends)
                self.three[c] = send(own.at[3, cut(c)], got.at[2, cut(c)], line[3], middle)
                slot = copies.slot()
                self.two[c] = send(own.at[2, cut(c)], got.at[1, cut(c)], line[2], ends, slot)

        def relay_line(self, c):
            own, got = line_s.at[self.number], line_r.at[self.number]

            @pl.when(middle)
            def _():
                self.relay[c].wait_recv()
                own[2, cut(c), :] = (own[2, cut(c), :].astype(f32) + got[3, cut(c), :].astype(f32)).astype(bf16)
                self.two[c].start()

            sent[:] = [[e[0], None] if e[0] is self.two[c] else e for e in sent]

        def finish(self, c):
            own, got = line_s.at[self.number], line_r.at[self.number]
            self.one[c].wait_recv()
            self.two[c].wait_recv()
            total = own[0, cut(c), :].astype(f32) + got[0, cut(c), :].astype(f32) + got[1, cut(c), :].astype(f32)
            dn_s[cut(c), :] = total

            @pl.when(middle)
            def _():
                self.three[c].wait_recv()
                dn_s[cut(c), :] += got[2, cut(c), :].astype(f32)

            if self.number:
                dn_out[cut(c), :] = dn_s[cut(c), :]
            else:
                block_out[cut(c), :] = (tok[cut(c), :].astype(f32) + dn_s[cut(c), :] + bias_ref[0:1, :]).astype(bf16)

    g_near, g_line, d_near = {}, {}, {}
    q_width, u_width = q_v.shape[1], u_v.shape[1]

    def grad_block(dst):
        need(3, 4)
        source = take()
        dst[:, pl.ds(0, q_width)] = t_mm(source[...], q_v[...]).astype(bf16)
        dst[:, pl.ds(q_width, u_width)] = t_mm(source[...], u_v[...]).astype(bf16)

    def grad_other(s):
        grad_block(go_s.at[s])
        g_near[s] = send(go_s.at[s], go_r.at[s], col)

    def grad_line(s):
        g_near[s].wait_recv()
        gm_s[s] = (gm_s[s].astype(f32) + go_r[s].astype(f32)).astype(bf16)
        if s:
            g_line[s] = send(gm_s.at[s], g_out.at[line_id], line[s])
        else:
            load = pltpu.make_async_copy(gm_s.at[0], g_out.at[line_id], load_sems.at[len(loads)])
            load.start()
            loads.append([load, False])

    turned = [False]

    def out_block(j, other):
        need(0, 1)
        if not turned[0]:
            at_v[0:part, :] = a_v[...].T
            at_v[part:, :] = h_v[...].T
            turned[0] = True
        source = take()
        at = pl.ds(j * block, block)
        value = mm(at_v[...], source[...])
        if other:
            do_s[j] = value.astype(bf16)
            d_near[j] = send(do_s.at[j], do_r.at[j], col)
        else:
            dm_s[:, at] = value

    def out_finish(j):
        d_near[j].wait_recv()
        at = pl.ds(j * block, block)
        dm_s[:, at] += do_r[j].astype(f32)
        load = pltpu.make_async_copy(dm_s.at[:, at], gd_out.at[:, at], load_sems.at[len(loads)])
        load.start()
        loads.append([load, False])

    old, new = Stream(0), Stream(1)
    both = (old, new)
    for what, *args in order:
        if what == "c": both[args[0]].compute(*args[1:])
        if what == "x": both[args[0]].give_far(*args[1:])
        if what == "y": both[args[0]].give_col(*args[1:])
        if what == "z": both[args[0]].give_line(*args[1:])
        if what == "r": both[args[0]].relay_line(*args[1:])
        if what == "f": both[args[0]].finish(*args[1:])
        if what == "go": grad_other(*args)
        if what == "gm": grad_block(gm_s.at[args[0]])
        if what == "gz": grad_line(*args)
        if what == "do": out_block(args[0], True)
        if what == "dm": out_block(args[0], False)
        if what == "df": out_finish(*args)
    for copy in g_line.values():
        copy.wait_recv()
    need(*range(len(loads)))
    for copy, when in list(sent):
        wait_sent(copy)


def scatter_order():
    return [
        ("c", 0, 1, 0), ("go", 1), ("c", 0, 1, 1), ("x", 0, 1, 0), ("go", 2), ("x", 0, 1, 1),
        ("c", 0, 0, 0), ("gm", 1), ("x", 0, 0, 0), ("c", 0, 0, 1), ("gm", 2), ("x", 0, 0, 1),
        ("gz", 1), ("y", 0, 1, 0), ("go", 3), ("gm", 3), ("z", 0, 1, 0), ("y", 0, 1, 1), ("gz", 2),
        ("c", 1, 1, 0), ("x", 1, 1, 0), ("z", 0, 1, 1), ("r", 0, 0), ("y", 0, 0, 0), ("c", 1, 1, 1), ("x", 1, 1, 1), ("go", 0), ("gm", 0),
        ("r", 0, 1), ("z", 0, 0, 0), ("y", 0, 0, 1), ("c", 1, 0, 0), ("x", 1, 0, 0), ("gz", 3),
        ("z", 0, 0, 1), ("c", 1, 0, 1), ("x", 1, 0, 1), ("do", 0), ("f", 0, 0), ("y", 1, 1, 0), ("do", 1), ("gz", 0),
        ("z", 1, 1, 0), ("y", 1, 1, 1), ("f", 0, 1), ("do", 2), ("r", 1, 0), ("z", 1, 1, 1), ("y", 1, 0, 0), ("do", 3),
        ("r", 1, 1), ("z", 1, 0, 0), ("dm", 0), ("dm", 1), ("y", 1, 0, 1), ("dm", 2), ("dm", 3), ("z", 1, 0, 1),
        ("f", 1, 0), ("df", 0), ("df", 1), ("df", 2), ("df", 3), ("f", 1, 1),
    ]


def scatter(tier_count, attn, hidden, dqkv, dup, normed, back, qkv_mat, up_mat, out_mat, tok, bias, order=None):
    rows, half = tok.shape
    width = 2 * half
    chunk = rows // CH
    all_rows = attn.shape[0]
    part = attn.shape[1]
    sds = jax.ShapeDtypeStruct
    any_ = pl.BlockSpec(memory_space=pl.ANY)
    vmem = pl.BlockSpec(memory_space=pltpu.VMEM)
    block = half // 4

    def buf(*shape, kind=bf16):
        return pltpu.VMEM(shape, kind)

    return pl.pallas_call(
        functools.partial(scatter_kernel, tier_count, order or scatter_order()),
        out_shape=[sds((rows, half), bf16), sds((rows, half), f32), sds((4, block, 7 * part), bf16), sds((5 * part, half), f32)],
        in_specs=[any_] * 9 + [vmem, vmem],
        out_specs=[vmem, vmem, any_, any_],
        scratch_shapes=[
            buf(all_rows, part), buf(all_rows, 4 * part), buf(all_rows, 3 * part), buf(all_rows, 4 * part),
            buf(width, 3 * part), buf(width, 4 * part), buf(5 * part, width), buf(5 * part, all_rows),
            buf(2, all_rows, block), buf(4, 4, chunk, width), buf(8, 2, chunk, width), buf(8, chunk, width),
            buf(2, 4, rows, half), buf(2, 4, rows, half),
            buf(4, block, 7 * part), buf(4, block, 7 * part), buf(4, block, 7 * part),
            buf(4, 5 * part, block), buf(4, 5 * part, block), buf(5 * part, half, kind=f32), buf(rows, half, kind=f32),
            pltpu.SemaphoreType.DMA((64,)), pltpu.SemaphoreType.DMA((64,)), pltpu.SemaphoreType.DMA((16,)), pltpu.SemaphoreType.DMA((2,)),
        ],
        compiler_params=pltpu.CompilerParams(collective_id=2, has_side_effects=True, vmem_limit_bytes=62 << 20),
    )(attn, hidden, dqkv, dup, normed, back, qkv_mat, up_mat, out_mat, tok, bias)


def per_device(
    tokens,
    cotangent,
    doc_lengths,
    doc_groups,
    w_qkv,
    w_up,
    w_dense,
    w_down,
    vectors,
    m_qkv,
    v_qkv,
    m_up,
    v_up,
    m_dense,
    v_dense,
    m_down,
    v_down,
    m_vec,
    v_vec,
):
    dp_count = lax.axis_size("dp")
    tier_count = dp_count // LINE
    dp_id = lax.axis_index("dp")
    line_id = dp_id // tier_count
    tier_id = dp_id % tier_count
    row_count = lax.axis_size("row")
    col_count = lax.axis_size("col")
    assert row_count == 4 and col_count == 2 and dp_count % LINE == 0
    row_id = lax.axis_index("row")
    col_id = lax.axis_index("col")
    tok_dev, half_width = tokens.shape
    slot_count = tok_dev * row_count
    full_width = half_width * col_count
    row_width = full_width // row_count
    part = row_width // LINE
    heads_dev = part // HDIM
    zero_index = jnp.int32(0)
    tier_groups = [[line * tier_count + tier for tier in range(tier_count)] for line in range(LINE)]

    def over_line(value, bits):
        pairs = [(i, ((i // tier_count) ^ bits) * tier_count + i % tier_count) for i in range(dp_count)]
        return lax.ppermute(value, "dp", pairs)

    def over_row(value, bits):
        return lax.ppermute(value, "row", [(i, i ^ bits) for i in range(row_count)])

    def over_col(value):
        return lax.ppermute(value, "col", [(0, 1), (1, 0)])

    def reorder(blocks, place):
        one = (place & 1) == 1
        two = (place & 2) == 2
        blocks = [jnp.where(one, blocks[i ^ 1], blocks[i]) for i in range(4)]
        return [jnp.where(two, blocks[i ^ 2], blocks[i]) for i in range(4)]

    def sum_all(value):
        value = sum(reorder([value] + [over_line(value, s) for s in (1, 2, 3)], line_id))
        value = sum(reorder([value] + [over_row(value, s) for s in (1, 2, 3)], row_id))
        value = value + over_col(value)
        if tier_count > 1:
            value = lax.psum(value, "dp", axis_index_groups=tier_groups)
        return value

    odd = ((line_id & 1) ^ col_id) == 1
    first_bits = (line_id & 1) ^ col_id
    part_start = row_id * row_width + line_id * part
    col_start = col_id * half_width

    def by_half(vector):
        mine = lax.dynamic_slice_in_dim(vector, col_start, half_width, 0)
        other = lax.dynamic_slice_in_dim(vector, (1 - col_id) * half_width, half_width, 0)
        return jnp.concatenate([mine, other])

    places = jnp.concatenate(
        [(row_id ^ t) * tok_dev + jnp.arange(tok_dev, dtype=jnp.int32) for t in range(4)]
    )
    positions = []
    for p in range(2):
        group_id = (line_id ^ first_bits ^ (2 * p)) * tier_count + tier_id
        positions.append(seq_layout(doc_lengths, doc_groups, group_id, places))
    positions = jnp.stack(positions)
    cos_part, sin_part = turn_angles(positions)
    nothing = jnp.zeros((2, slot_count, HDIM - ROT), f32)
    still = jnp.zeros_like(sin_part)

    def over_heads(*pieces):
        return jnp.tile(jnp.concatenate(pieces, axis=-1), (1, 1, heads_dev))

    cosine = over_heads(cos_part, cos_part, nothing + 1.0)
    lead = over_heads(-sin_part, still, nothing)
    trail = over_heads(still, sin_part, nothing)
    seq_from = (places[None] - positions)[:, :, None]
    place_col = jnp.broadcast_to(places[None, :, None], seq_from.shape)
    total_len = jnp.sum(jnp.where(doc_groups == dp_id, doc_lengths, 0), dtype=jnp.int32)
    own_valid = places[:tok_dev] < total_len
    back_own = jnp.where(own_valid[:, None], cotangent, jnp.zeros_like(cotangent))

    def tier_gather(value):
        if tier_count > 1:
            value = lax.all_gather(value, "dp", axis=0, tiled=True, axis_index_groups=tier_groups)
        return value

    def pieces_of(weight):
        low = tier_gather(weight.astype(bf16))
        rows, parts = low.shape[:2]
        return low.reshape(rows, parts, LINE, part).transpose(2, 0, 1, 3).reshape(LINE, rows, parts * part)

    down_low = tier_gather(w_down.astype(bf16)).transpose(1, 0, 2).reshape(4 * part, half_width)
    out_low = jnp.concatenate([tier_gather(w_dense.astype(bf16)), down_low], axis=0)
    norm_vec = jnp.stack([by_half(vectors[0]), by_half(vectors[1])])
    normed, back, qkv_mat, up_mat, out_mat = gather(
        tier_count, tokens, back_own, norm_vec, pieces_of(w_qkv), pieces_of(w_up), out_low
    )
    rows_all = 2 * slot_count
    normed = normed.reshape(rows_all, full_width)
    back = back.reshape(rows_all, full_width)
    qkv_mat = qkv_mat.reshape(full_width, 3 * part)
    up_mat = up_mat.reshape(full_width, 4 * part)
    dense_mat = out_mat[:part]
    down_mat = out_mat[part:]

    bias_qkv = lax.dynamic_slice(vectors[2:5], (zero_index, part_start), (3, part)).reshape(3 * part)
    bias_up = lax.dynamic_slice(vectors[5:9], (zero_index, part_start), (4, part)).reshape(4 * part)

    bias = jnp.concatenate([bias_qkv, bias_up])[None]
    attn, hidden, d_qkv, d_pre_up, bias_sums = local_part(
        normed.reshape(2, slot_count, full_width),
        back.reshape(2, slot_count, full_width),
        qkv_mat,
        up_mat,
        out_mat,
        bias,
        cosine,
        lead,
        trail,
        seq_from,
        place_col,
        places[None],
    )
    out_bias = lax.dynamic_slice_in_dim(vectors[9] + vectors[10], col_start, half_width, 0)
    block_out, d_normed, grad_in, grad_out = scatter(
        tier_count,
        attn.reshape(rows_all, part),
        hidden.reshape(rows_all, 4 * part),
        d_qkv.reshape(rows_all, 3 * part),
        d_pre_up.reshape(rows_all, 4 * part),
        normed,
        back,
        qkv_mat,
        up_mat,
        out_mat,
        tokens,
        out_bias[None],
    )
    bias_sums = jnp.sum(bias_sums[:, 0], axis=0).reshape(7, part)

    def tier_sum(value):
        if tier_count > 1:
            value = lax.psum_scatter(
                value, "dp", scatter_dimension=0, tiled=True, axis_index_groups=tier_groups
            )
        return value

    def own_columns(value, parts):
        value = value.astype(f32).reshape(LINE, half_width // LINE, parts, part)
        return tier_sum(value.transpose(1, 2, 0, 3).reshape(half_width // LINE, parts, row_width))

    red_qkv = own_columns(grad_in[:, :, : 3 * part], 3)
    red_up = own_columns(grad_in[:, :, 3 * part :], 4)
    red_dense = tier_sum(grad_out[:part])
    red_down = tier_sum(grad_out[part:].reshape(4, part, half_width).transpose(1, 0, 2))
    tokens_own = tokens.astype(f32)
    own_sums = jnp.stack([jnp.sum(tokens_own, axis=-1), jnp.sum(tokens_own * tokens_own, axis=-1)])
    own_sums = (own_sums + over_col(own_sums)) / full_width
    mean_own = own_sums[0][:, None]
    inv_own = lax.rsqrt(own_sums[1][:, None] - mean_own * mean_own + eps_norm)
    centred = (tokens_own - mean_own) * inv_own
    gain_cols = lax.dynamic_slice_in_dim(vectors[0], col_start, half_width, 0)
    d_hat = d_normed * gain_cols[None, :]
    hat_sums = jnp.stack([jnp.sum(d_hat, axis=-1), jnp.sum(d_hat * centred, axis=-1)])
    hat_sums = (hat_sums + over_col(hat_sums)) / full_width
    back_float = back_own.astype(f32)
    grad_tokens = inv_own * (d_hat - hat_sums[0][:, None] - centred * hat_sums[1][:, None]) + back_float

    early = jnp.zeros((9, full_width), f32)
    early = lax.dynamic_update_slice(early, bias_sums, (zero_index, part_start))
    out_sums = jnp.sum(back_float, axis=0)
    early = lax.dynamic_update_slice(early, jnp.stack([out_sums, out_sums]), (jnp.int32(7), col_start))
    late = lax.dynamic_update_slice(
        jnp.zeros((2, full_width), f32),
        jnp.stack([jnp.sum(d_normed * centred, axis=0), jnp.sum(d_normed, axis=0)]),
        (zero_index, col_start),
    )
    vec_grad = jnp.concatenate([sum_all(late), sum_all(early)], axis=0)
    qkv_new = adamw(w_qkv, m_qkv, v_qkv, red_qkv, D ** (-0.5), 0.1)
    up_new = adamw(w_up, m_up, v_up, red_up, D ** (-0.5), 0.1)
    dense_new = adamw(w_dense, m_dense, v_dense, red_dense, max(D // 128, 4) ** (-0.5), 0.1)
    down_new = adamw(w_down, m_down, v_down, red_down, FF ** (-0.5), 0.1)
    vec_new = adamw(vectors, m_vec, v_vec, vec_grad, 0.5, 0.0)
    return (
        block_out,
        grad_tokens,
        qkv_new[0],
        qkv_new[1],
        qkv_new[2],
        up_new[0],
        up_new[1],
        up_new[2],
        dense_new[0],
        dense_new[1],
        dense_new[2],
        down_new[0],
        down_new[1],
        down_new[2],
        vec_new[0],
        vec_new[1],
        vec_new[2],
    )


def solution(mesh):
    placed = (
        P(("dp", "row"), "col"),
        P(("dp", "row"), "col"),
        P(),
        P(),
        P(("col", "dp"), None, "row"),
        P(("col", "dp"), None, "row"),
        P(("row", "dp"), "col"),
        P(("row", "dp"), None, "col"),
        P(),
        P(("col", "dp"), None, "row"),
        P(("col", "dp"), None, "row"),
        P(("col", "dp"), None, "row"),
        P(("col", "dp"), None, "row"),
        P(("row", "dp"), "col"),
        P(("row", "dp"), "col"),
        P(("row", "dp"), None, "col"),
        P(("row", "dp"), None, "col"),
        P(),
        P(),
    )
    return jax.shard_map(
        per_device,
        mesh=mesh,
        in_specs=placed,
        out_specs=(
            P(("dp", "row"), "col"),
            P(("dp", "row"), "col"),
            P(("col", "dp"), None, "row"),
            P(("col", "dp"), None, "row"),
            P(("col", "dp"), None, "row"),
            P(("col", "dp"), None, "row"),
            P(("col", "dp"), None, "row"),
            P(("col", "dp"), None, "row"),
            P(("row", "dp"), "col"),
            P(("row", "dp"), "col"),
            P(("row", "dp"), "col"),
            P(("row", "dp"), None, "col"),
            P(("row", "dp"), None, "col"),
            P(("row", "dp"), None, "col"),
            P(),
            P(),
            P(),
        ),
        check_vma=False,
    )
```

```python
import functools

import jax
import jax.numpy as jnp
from jax import lax
from jax.experimental import pallas as pl
from jax.experimental.pallas import tpu as pltpu
from jax.sharding import PartitionSpec as P

D = 2048
HDIM = 64
ROT = 32
FF = 8192
BLK = 512
STEP = 10
LINE = 4


eps_norm = 1e-05
f32 = jnp.float32
bf16 = jnp.bfloat16


def adamw(weight, first_moment, second_moment, gradient, rate, decay):
    first_next = 0.9 * first_moment + 0.1 * gradient
    second_next = 0.95 * second_moment + 0.05 * gradient * gradient
    correct_one = 1.0 - 0.9**STEP
    correct_two = 1.0 - 0.95**STEP
    update = first_next / correct_one / (jnp.sqrt(second_next / correct_two) + 1e-08)
    return (first_next, second_next, weight - rate * (update + decay * weight))


class Copies:
    def __init__(self, send_sems, recv_sems):
        self.send_sems, self.recv_sems, self.sent, self.received = send_sems, recv_sems, 0, 0

    def slot(self):
        self.received += 1
        return self.received - 1

    def make(self, src, dst, device, slot=None):
        slot = self.slot() if slot is None else slot
        self.sent += 1
        return pltpu.make_async_remote_copy(
            src_ref=src, dst_ref=dst, send_sem=self.send_sems.at[self.sent - 1], recv_sem=self.recv_sems.at[slot],
            device_id=device, device_id_type=pl.DeviceIdType.MESH)

def neighbours(tier_count):
    dp_id, row_id, col_id = lax.axis_index("dp"), lax.axis_index("row"), lax.axis_index("col")
    line_id, tier_id = dp_id // tier_count, dp_id % tier_count
    flips = [line_id, line_id + 1 - 2 * (line_id % 2), (line_id + 2) % 4, 3 - line_id]
    line = [(flip * tier_count + tier_id, row_id, col_id) for flip in flips]
    core = (dp_id, row_id + 1 - 2 * (row_id % 2), col_id)
    far = (dp_id, (row_id + 2) % 4, col_id)
    col = (dp_id, row_id, 1 - col_id)
    return line_id, flips, line, core, far, col

def meet(peers):
    barrier = pltpu.get_barrier_semaphore()
    for peer in peers:
        pl.semaphore_signal(barrier, inc=1, device_id=peer, device_id_type=pl.DeviceIdType.MESH)
    pl.semaphore_wait(barrier, len(peers))


CH = 2

def gather_kernel(tier_count, order, lengths, groups, tok, cot, vec_ref, w_qkv, w_up, w_dense, w_down,
                  x_out, b_out, wq_out, wu_out, d_out,
                  tz, cz, ty, xs, cot_s, qkv_f, up_f, dense_f, down_f, wq, wu, dh,
                  send_sems, recv_sems, local_sems, load_sems):
    line_id, flips, line, core, far, col = neighbours(tier_count)
    bit = (line_id % 2 + lax.axis_index("col")) % 2
    middle = (line_id == 1) | (line_id == 2)
    rows, half = tok.shape
    chunk = rows // CH
    copies = Copies(send_sems, recv_sems)
    sent, mid_sent, local_left, last = [], [], [], []
    n_local = [0]

    def local(src, dst):
        copy = pltpu.make_async_copy(src, dst, local_sems.at[n_local[0]])
        n_local[0] += 1
        copy.start()
        local_left.append(copy)
        return copy

    def settle(copy):
        copy.wait()
        local_left[:] = [c for c in local_left if c is not copy]

    def send(src, dst, device, slot=None):
        copy = copies.make(src, dst, device, slot)
        copy.start()
        sent.append(copy)
        return copy

    def cut(c):
        return pl.ds(c * chunk, chunk)

    class Stream:
        def __init__(self, own, stage, out, normed):
            self.own, self.stage, self.out, self.normed = own, stage, out, normed
            self.line, self.swap, self.spread, self.keep, self.relayed = {}, {}, {}, {}, {}

        def start(self, c):
            own, stage = self.own.at[cut(c)], self.stage
            own_copy = local(own, stage.at[0, cut(c)])
            near = send(own, stage.at[1, cut(c)], line[1])
            two = send(own, stage.at[2, cut(c)], line[2])
            slot = copies.slot()
            three = copies.make(own, stage.at[3, cut(c)], line[3], slot)
            relay = copies.make(stage.at[2, cut(c)], stage.at[3, cut(c)], line[1], slot)
            pl.when(middle)(three.start)
            mid_sent.extend([three, relay])
            self.line[c] = own_copy, near, two, three, relay

        def swap_cols(self, c, p):
            own_copy, near, two, three, relay = self.line[c]
            if p == 0:
                settle(own_copy)
                near.wait_recv()
            else:
                two.wait_recv()
                pl.when(middle)(relay.start)
                three.wait_recv()
            if self.normed:
                dst = ty.at[p, cut(c)]
            else:
                dst = self.out.at[p, 0, cut(c), pl.ds(half, half)]
                self.keep[c, p] = local(self.stage.at[2 * p + bit, cut(c)], self.out.at[p, 0, cut(c), pl.ds(0, half)])
            self.swap[c, p] = send(self.stage.at[2 * p + 1 - bit, cut(c)], dst, col)

        def give(self, c, p):
            self.swap[c, p].wait_recv()
            if self.normed:
                norm(c, p)
                src = xs.at[p, cut(c)]
                local(src, self.out.at[p, 0, cut(c)])
            else:
                settle(self.keep[c, p])
                src = self.out.at[p, 0, cut(c)]
            self.spread[c, p] = send(src, self.out.at[p, 2, cut(c)], far)
            last.append(send(src, self.out.at[p, 1, cut(c)], core))

        def relay(self, c, p):
            self.spread[c, p].wait_recv()
            last.append(send(self.out.at[p, 2, cut(c)], self.out.at[p, 3, cut(c)], core))

    norm_ref = [[vec_ref.at[i:i + 1, pl.ds(pl.multiple_of(side * half, half), half)] for i in range(2)]
                for side in (lax.axis_index("col"), 1 - lax.axis_index("col"))]

    def norm(c, p):
        step = 64
        def body(i, carry):
            at = pl.ds(pl.multiple_of(c * chunk + i * step, step), step)
            one = tz[2 * p + bit, at, :].astype(f32)
            two = ty[p, at, :].astype(f32)
            width = 2 * half
            mean = (jnp.sum(one, axis=-1, keepdims=True) + jnp.sum(two, axis=-1, keepdims=True)) / width
            square = (jnp.sum(one * one, axis=-1, keepdims=True) + jnp.sum(two * two, axis=-1, keepdims=True)) / width
            inv = lax.rsqrt(square - mean * mean + eps_norm)
            xs[p, at, pl.ds(0, half)] = ((one - mean) * inv * norm_ref[0][0][...] + norm_ref[0][1][...]).astype(bf16)
            xs[p, at, pl.ds(half, half)] = ((two - mean) * inv * norm_ref[1][0][...] + norm_ref[1][1][...]).astype(bf16)
            return carry
        lax.fori_loop(0, chunk // step, body, 0)

    class Weight:
        def __init__(self, src, out):
            self.src, self.out, self.got = src, out, {}

        def own(self):
            local(self.src.at[line_id], self.out.at[0, line_id])
            last.append(send(self.src.at[line_id], self.out.at[1, line_id], col))

        def start(self):
            for s in (1, 2, 3):
                self.got[s] = send(self.src.at[flips[s]], self.out.at[0, line_id], line[s])

        def swap(self):
            for s in (1, 2, 3):
                self.got[s].wait_recv()
                last.append(send(self.out.at[0, flips[s]], self.out.at[1, flips[s]], col))

    part = dh.shape[0] // 5
    loads = []
    for i, (src, dst) in enumerate(((w_qkv, qkv_f), (w_up, up_f), (w_dense, dense_f), (w_down, down_f), (cot, cot_s))):
        loads.append(pltpu.make_async_copy(src, dst, load_sems.at[i]))
        loads[-1].start()

    def prepare(what):
        if what == 0:
            loads[0].wait()
            for j in range(LINE):
                for k in range(3):
                    wq[j, :, k * part:(k + 1) * part] = qkv_f[k, :, j * part:(j + 1) * part].astype(bf16)
        if what == 1:
            loads[1].wait()
            for j in range(LINE):
                for k in range(4):
                    wu[j, :, k * part:(k + 1) * part] = up_f[:, k, j * part:(j + 1) * part].astype(bf16)
        if what == 2:
            loads[2].wait()
            dh[0:part, :] = dense_f[...].astype(bf16)
        if what == 3:
            loads[3].wait()
            for k in range(4):
                dh[(k + 1) * part:(k + 2) * part, :] = down_f[:, k, :].astype(bf16)
        if what == 4:
            loads[4].wait()
            total = jnp.int32(0)
            for i in range(lengths.shape[0]):
                total = total + jnp.where(groups[i] == lax.axis_index("dp"), lengths[i], 0)
            place = lax.axis_index("row") * rows + lax.broadcasted_iota(jnp.int32, (rows, half), 0)
            cot_s[...] = jnp.where(place < total, cot_s[...], jnp.zeros_like(cot_s))

    def dense(i):
        at = pl.ds(i * part, part)
        last.append(send(dh.at[at], d_out.at[at, pl.ds(half, half)], col))

    meet([line[1], line[2], line[3], core, far, col])
    T = Stream(tok, tz, x_out, True)
    C = Stream(cot_s, cz, b_out, False)
    Q = Weight(wq, wq_out)
    U = Weight(wu, wu_out)
    for what, *args in order:
        if what == "P": prepare(*args)
        if what == "Ts": T.start(*args)
        if what == "Ty": T.swap_cols(*args)
        if what == "Tx": T.give(*args)
        if what == "Tk": T.relay(*args)
        if what == "Cs": C.start(*args)
        if what == "Cy": C.swap_cols(*args)
        if what == "Cx": C.give(*args)
        if what == "Ck": C.relay(*args)
        if what == "Qo": Q.own()
        if what == "Qs": Q.start()
        if what == "Qy": Q.swap()
        if what == "Uo": U.own()
        if what == "Us": U.start()
        if what == "Uy": U.swap()
        if what == "D": dense(*args)
        if what == "Dl": local(dh, d_out.at[:, pl.ds(0, half)])
    for copy in last:
        copy.wait_recv()
    for copy in list(local_left):
        settle(copy)
    for copy in sent:
        copy.wait_send()
    for copy in mid_sent:
        pl.when(middle)(copy.wait_send)

ORDER_A = [("Ts",0),("Ts",1),("P",0),("Qo",),("P",1),("Uo",),("P",2),("D",0),("P",3),("Dl",),("P",4),
 ("Ty",0,0),("Ty",0,1),("Tx",0,0),("Tx",0,1),
 ("Ty",1,0),("Ty",1,1),("Cs",0),("Tx",1,0),("Tx",1,1),("D",1),("D",2),
 ("Tk",0,0),("Tk",0,1),("Cy",0,0),("Cy",0,1),("Qs",),("Cs",1),("Cx",0,0),("Cx",0,1),("Tk",1,0),("Tk",1,1),
 ("Qy",),("Cy",1,0),("Cy",1,1),("Us",),("Cx",1,0),("Cx",1,1),("D",3),("D",4),("Ck",0,0),("Ck",0,1),
 ("Uy",),("Ck",1,0),("Ck",1,1)]

def gather(tier_count, lengths, groups, tok, cot, vectors, w_qkv, w_up, w_dense, w_down):
    rows, half = tok.shape
    part = w_dense.shape[0]
    c_rows = w_up.shape[0]
    sds = jax.ShapeDtypeStruct
    any_ = pl.BlockSpec(memory_space=pl.ANY)
    smem = pl.BlockSpec(memory_space=pltpu.SMEM)
    return pl.pallas_call(
        functools.partial(gather_kernel, tier_count, ORDER_A),
        out_shape=[sds((2, 4, rows, 2 * half), bf16), sds((2, 4, rows, 2 * half), bf16),
                   sds((2, LINE, c_rows, 3 * part), bf16), sds((2, LINE, c_rows, 4 * part), bf16), sds((5 * part, 2 * half), bf16)],
        in_specs=[smem, smem, any_, any_, pl.BlockSpec(memory_space=pltpu.VMEM), any_, any_, any_, any_],
        out_specs=[any_] * 5,
        scratch_shapes=[pltpu.VMEM((4, rows, half), bf16), pltpu.VMEM((4, rows, half), bf16), pltpu.VMEM((2, rows, half), bf16),
                        pltpu.VMEM((2, rows, 2 * half), bf16), pltpu.VMEM((rows, half), bf16),
                        pltpu.VMEM(w_qkv.shape, f32), pltpu.VMEM(w_up.shape, f32), pltpu.VMEM(w_dense.shape, f32), pltpu.VMEM(w_down.shape, f32),
                        pltpu.VMEM((LINE, c_rows, 3 * part), bf16), pltpu.VMEM((LINE, c_rows, 4 * part), bf16), pltpu.VMEM((5 * part, half), bf16),
                        pltpu.SemaphoreType.DMA((80,)), pltpu.SemaphoreType.DMA((80,)), pltpu.SemaphoreType.DMA((24,)), pltpu.SemaphoreType.DMA((5,))],
        compiler_params=pltpu.CompilerParams(collective_id=1, has_side_effects=True, vmem_limit_bytes=60 << 20),
    )(lengths, groups, tok, cot, vectors, w_qkv, w_up, w_dense, w_down)


def mm(a, b):
    return jnp.dot(a, b, preferred_element_type=f32)


def mm_t(a, b):
    return lax.dot_general(a, b, (((1,), (1,)), ((), ())), preferred_element_type=f32)


def t_mm(a, b):
    return lax.dot_general(a, b, (((0,), (0,)), ((), ())), preferred_element_type=f32)


def gelu_both(v):
    root = 0.7978845608028654
    square = v * v
    slope = root * (1.0 + 3 * 0.044715 * square)
    tanh = jnp.tanh(root * v * (1.0 + 0.044715 * square))
    outer = 0.5 * (1.0 + tanh)
    return v * outer, outer + 0.5 * v * (1.0 - tanh * tanh) * slope


def local_kernel(tier_count, lengths, groups, x_ref, b_ref, wq_ref, wu_ref, d_ref, bias_ref,
                 attn_ref, hidden_ref, dqkv_ref, dup_ref, sums_ref,
                 q_s, k_s, v_s, da_s, dk_s, dv_s, cos_s, sin_s, from_s):
    slots, part = q_s.shape
    qb = slots // 4
    scale = HDIM ** (-0.5)
    quarter = ROT // 2

    row_id = lax.axis_index("row")
    quarters = [row_id, row_id + 1 - 2 * (row_id % 2), (row_id + 2) % 4, 3 - row_id]
    rows = slots // 4
    line_id, tier_id = lax.axis_index("dp") // tier_count, lax.axis_index("dp") % tier_count
    bit = (line_id % 2 + lax.axis_index("col")) % 2
    group = line_id + bit * (1 - 2 * (line_id % 2))
    group = ((group + 2 * pl.program_id(0)) % 4) * tier_count + tier_id
    lanes = lax.broadcasted_iota(jnp.int32, (1, part), 1) % HDIM
    turned = lanes < ROT
    lead = lanes < quarter
    powers = (lanes % quarter).astype(f32) * (-2.0 / ROT)
    speed = jnp.where(turned, jnp.exp(powers * 9.210340371976184), 0.0)
    key_place = jnp.concatenate([quarters[t] * rows + lax.broadcasted_iota(jnp.int32, (1, rows), 1) for t in range(4)], axis=1)
    fine = lax.broadcasted_iota(jnp.int32, (32, part), 0).astype(f32) * speed
    fine_cos, fine_sin = jnp.cos(fine), jnp.sin(fine)

    def fill(t, carry):
        quarter_id = jnp.where(t == 0, quarters[0], jnp.where(t == 1, quarters[1], jnp.where(t == 2, quarters[2], quarters[3])))
        base = quarter_id * rows
        coarse = (base + 32 * lax.broadcasted_iota(jnp.int32, (rows // 32, part), 0)).astype(f32) * speed
        coarse_cos, coarse_sin = jnp.cos(coarse), jnp.sin(coarse)
        place_cos = jnp.concatenate([coarse_cos[i:i + 1] * fine_cos - coarse_sin[i:i + 1] * fine_sin for i in range(rows // 32)])
        place_sin = jnp.concatenate([coarse_sin[i:i + 1] * fine_cos + coarse_cos[i:i + 1] * fine_sin for i in range(rows // 32)])
        place = base + lax.broadcasted_iota(jnp.int32, (rows, part), 0)
        first = jnp.zeros((rows, part), jnp.int32)
        first_cos = jnp.ones((rows, part), f32)
        first_sin = jnp.zeros((rows, part), f32)
        start = jnp.int32(0)
        for i in range(lengths.shape[0] + 1):
            here = groups[i] == group if i < lengths.shape[0] else True
            after = place >= (jnp.where(here, start, 1 << 30) if i < lengths.shape[0] else start)
            angle = start.astype(f32) * speed
            first = jnp.where(after, start, first)
            first_cos = jnp.where(after, jnp.cos(angle), first_cos)
            first_sin = jnp.where(after, jnp.sin(angle), first_sin)
            if i < lengths.shape[0]:
                start = start + jnp.where(here, lengths[i], 0)
        at = pl.ds(pl.multiple_of(t * rows, rows), rows)
        from_s[at, :] = first
        cos_s[at, :] = place_cos * first_cos + place_sin * first_sin
        sin = place_sin * first_cos - place_cos * first_sin
        sin_s[at, :] = jnp.where(lead, -sin, sin)
        return carry

    lax.fori_loop(0, 4, fill, 0)

    def turn(value, at, sign):
        left = jnp.roll(value, -quarter, axis=1)
        right = jnp.roll(value, quarter, axis=1)
        return value * cos_s[at, :] + sign * (jnp.where(lead, left, right) * sin_s[at, :])

    def project(i, carry):
        at = pl.ds(pl.multiple_of(i * qb, qb), qb)
        pre = mm(x_ref[0, at, :], wq_ref[...]) + bias_ref[0:1, 0:3 * part]
        q_s[at, :] = (turn(pre[:, 0:part], at, 1.0)).astype(bf16)
        k_s[at, :] = (turn(pre[:, part:2 * part], at, 1.0)).astype(bf16)
        v_s[at, :] = pre[:, 2 * part:].astype(bf16)
        back = b_ref[0, at, :]
        da_s[at, :] = mm_t(back, d_ref[0:part, :]).astype(bf16)
        return carry

    lax.fori_loop(0, slots // qb, project, 0)

    def up(i, carry):
        at = pl.ds(pl.multiple_of(i * qb, qb), qb)
        pre = mm(x_ref[0, at, :], wu_ref[...]) + bias_ref[0:1, 3 * part:]
        value, slope = gelu_both(pre)
        hidden_ref[0, at, :] = value.astype(bf16)
        d_up = (mm_t(b_ref[0, at, :], d_ref[part:, :]) * slope).astype(bf16)
        dup_ref[0, at, :] = d_up
        return carry + jnp.sum(d_up.astype(f32), axis=0, keepdims=True)

    up_sum = lax.fori_loop(0, slots // qb, up, jnp.zeros((1, 4 * part), f32))
    sums_ref[0, 0:1, 3 * part:] = up_sum

    dk_s[...] = jnp.zeros_like(dk_s)
    dv_s[...] = jnp.zeros_like(dv_s)
    lane = lax.broadcasted_iota(jnp.int32, (qb, part), 1)

    def attend(i, q_sum):
        at = pl.ds(pl.multiple_of(i * qb, qb), qb)
        quarter_id = jnp.where(i == 0, quarters[0], jnp.where(i == 1, quarters[1], jnp.where(i == 2, quarters[2], quarters[3])))
        place = quarter_id * rows + lax.broadcasted_iota(jnp.int32, (rows, 1), 0)
        allowed = (key_place >= from_s[at, 0:1]) & (key_place <= place)
        queries, d_attn = q_s[at, :], da_s[at, :]
        out = jnp.zeros((qb, part), f32)
        d_q = jnp.zeros((qb, part), f32)
        for h in range(part // HDIM):
            head = (lane >= h * HDIM) & (lane < (h + 1) * HDIM)
            q_h = jnp.where(head, queries, jnp.zeros_like(queries))
            da_h = jnp.where(head, d_attn, jnp.zeros_like(d_attn))
            scores = jnp.where(allowed, mm_t(q_h, k_s[...]) * scale, -1e30)
            weights = jnp.exp(scores - jnp.max(scores, axis=-1, keepdims=True))
            probs = weights * (1.0 / jnp.sum(weights, axis=-1, keepdims=True))
            low = probs.astype(bf16)
            d_probs = mm_t(da_h, v_s[...])
            delta = jnp.sum(probs * d_probs, axis=-1, keepdims=True)
            d_scores = (probs * (d_probs - delta)).astype(bf16)
            out = jnp.where(head, mm(low, v_s[...]), out)
            d_q = jnp.where(head, mm(d_scores, k_s[...]), d_q)
            dk_s[...] += t_mm(q_h, d_scores)
            dv_s[...] += t_mm(da_h, low)
        attn_ref[0, at, :] = out.astype(bf16)
        d_q = turn(d_q * scale, at, -1.0).astype(bf16)
        dqkv_ref[0, at, 0:part] = d_q
        return q_sum + jnp.sum(d_q.astype(f32), axis=0, keepdims=True)

    sums_ref[0, 0:1, 0:part] = lax.fori_loop(0, slots // qb, attend, jnp.zeros((1, part), f32))
    whole = pl.ds(0, slots)
    d_k = turn(dk_s[...].T * scale, whole, -1.0).astype(bf16)
    d_v = dv_s[...].T.astype(bf16)
    dqkv_ref[0, :, part:2 * part] = d_k
    dqkv_ref[0, :, 2 * part:] = d_v
    sums_ref[0, 0:1, part:2 * part] = jnp.sum(d_k.astype(f32), axis=0, keepdims=True)
    sums_ref[0, 0:1, 2 * part:3 * part] = jnp.sum(d_v.astype(f32), axis=0, keepdims=True)


def local_part(tier_count, lengths, groups, normed, back, qkv_mat, up_mat, out_mat, bias):
    count, slots, width = normed.shape
    part = out_mat.shape[0] // 5

    def each(last):
        return pl.BlockSpec((1, slots, last), lambda p: (p, 0, 0))

    def once(value):
        return pl.BlockSpec(value.shape, lambda p: (0,) * value.ndim, pipeline_mode=pl.Buffered(1))

    def like(last, kind=bf16):
        return jax.ShapeDtypeStruct((count, slots, last), kind)

    smem = pl.BlockSpec(memory_space=pltpu.SMEM)
    return pl.pallas_call(
        functools.partial(local_kernel, tier_count),
        grid=(count,),
        out_shape=[like(part), like(4 * part), like(3 * part), like(4 * part), jax.ShapeDtypeStruct((count, 8, 7 * part), f32)],
        in_specs=[smem, smem, each(width), each(width), once(qkv_mat), once(up_mat), once(out_mat), once(bias)],
        out_specs=[each(part), each(4 * part), each(3 * part), each(4 * part), pl.BlockSpec((1, 8, 7 * part), lambda p: (p, 0, 0))],
        scratch_shapes=[pltpu.VMEM((slots, part), bf16)] * 4 + [pltpu.VMEM((part, slots), f32)] * 2
        + [pltpu.VMEM((slots, part), f32)] * 2 + [pltpu.VMEM((slots, part), jnp.int32)],
        compiler_params=pltpu.CompilerParams(vmem_limit_bytes=62 << 20),
    )(lengths, groups, normed, back, qkv_mat, up_mat, out_mat, bias)


def scatter_kernel(tier_count, order, attn, hidden, dqkv, dup, x_in, b_in, wq, wu, dm, tok, bias_ref,
                   block_out, dn_out, g_out, gd_out,
                   a_v, h_v, q_v, u_v, wq_v, wu_v, d_v, at_v, col_v, part_s, near_r, far_r, line_s, line_r,
                   go_s, go_r, gm_s, do_s, do_r, dm_s, dn_s, send_sems, recv_sems, load_sems, col_sems):
    line_id, flips, line, core, far, col = neighbours(tier_count)
    bit = (line_id % 2 + lax.axis_index("col")) % 2
    middle = (line_id == 1) | (line_id == 2)
    ends = (line_id == 0) | (line_id == 3)
    rows, half = tok.shape
    chunk = rows // CH
    width = 2 * half
    step = half // 2
    part = a_v.shape[1]
    block = half // 4
    copies = Copies(send_sems, recv_sems)
    loads = []
    for src, dst in ((attn, a_v), (hidden, h_v), (dm, d_v), (dup, u_v), (dqkv, q_v), (wu, wu_v), (wq, wq_v)):
        load = pltpu.make_async_copy(src, dst, load_sems.at[len(loads)])
        load.start()
        loads.append([load, False])

    def need(*which):
        for i in which:
            if not loads[i][1]:
                loads[i][0].wait()
                loads[i][1] = True

    sent = []

    def send(src, dst, device, when=None, slot=None):
        copy = copies.make(src, dst, device, slot)
        if when is None:
            copy.start()
        else:
            pl.when(when)(copy.start)
        sent.append([copy, when])
        return copy

    def wait_sent(copy):
        for entry in sent:
            if entry[0] is copy:
                sent[:] = [e for e in sent if e is not entry]
                if entry[1] is None:
                    copy.wait_send()
                else:
                    pl.when(entry[1])(copy.wait_send)

    wanted = []
    for what, *args in order:
        if what in ("go", "gm"):
            first = flips[args[0]] * block + (half if what == "go" else 0)
            wanted.append((x_in, first))
        if what in ("do", "dm"):
            wanted.append((b_in, args[0] * block + (half if what == "do" else 0)))
    taken = [0]
    fetches = []

    def fetch(i):
        src, first = wanted[i]
        if not isinstance(first, int):
            first = pl.multiple_of(first, block)
        copy = pltpu.make_async_copy(src.at[:, pl.ds(first, block)], col_v.at[i % 2], col_sems.at[i % 2])
        copy.start()
        fetches.append(copy)

    def take():
        i = taken[0]
        taken[0] += 1
        if i + 1 < len(wanted):
            fetch(i + 1)
        fetches[i].wait()
        return col_v.at[i % 2]

    if wanted:
        fetch(0)
    meet([line[1], line[2], line[3], core, far, col])

    def cut(c):
        return pl.ds(c * chunk, chunk)

    class Stream:
        def __init__(self, number):
            self.number = number
            self.near, self.far, self.col, self.one, self.two, self.three, self.relay = {}, {}, {}, {}, {}, {}, {}

        def compute(self, p, c):
            place = 2 * p + c
            out = part_s.at[place]
            if self.number:
                for copy in old.near[p, c] + [old.far[p, c], old.col[p, c]]:
                    wait_sent(copy)
                left, right = (q_v, wq_v), (u_v, wu_v)
                need(3, 4, 5, 6)
            else:
                left, right = (a_v, None), (h_v, None)
                need(0, 1, 2)

            def body(n, carry):
                at = pl.ds(pl.multiple_of(n * step, step), step)

                def lhs(ref):
                    base = p * 4 * rows + c * chunk
                    return jnp.concatenate([ref[pl.ds(base + t * rows, chunk), :] for t in range(4)], axis=0)

                if self.number:
                    total = mm_t(lhs(q_v), wq_v[at, :]) + mm_t(lhs(u_v), wu_v[at, :])
                else:
                    total = mm(lhs(a_v), d_v[0:part, at]) + mm(lhs(h_v), d_v[part:, at])
                low = total.astype(bf16)
                for t in range(4):
                    out[t, :, at] = low[t * chunk:(t + 1) * chunk]
                return carry

            lax.fori_loop(0, width // step, body, 0)
            into = near_r.at[4 * self.number + place]
            self.near[p, c] = [send(out.at[1], into.at[0], core), send(out.at[3], into.at[1], core)]

        def give_far(self, p, c):
            place = 2 * p + c
            self.near[p, c][1].wait_recv()
            mine = part_s.at[place, 2]
            mine[...] = (mine[...].astype(f32) + near_r[4 * self.number + place, 1].astype(f32)).astype(bf16)
            self.far[p, c] = send(mine, far_r.at[4 * self.number + place], far)

        def give_col(self, p, c):
            place = 2 * p + c
            self.near[p, c][0].wait_recv()
            self.far[p, c].wait_recv()
            mine = part_s.at[place, 0]
            total = mine[...].astype(f32) + near_r[4 * self.number + place, 0].astype(f32)
            total = (total + far_r[4 * self.number + place].astype(f32)).astype(bf16)
            line_s[self.number, 2 * p + bit, cut(c), :] = total[:, :half]
            mine[:, pl.ds(half, half)] = total[:, half:]
            self.col[p, c] = send(mine.at[:, pl.ds(half, half)], line_s.at[self.number, 2 * p + bit, cut(c)], col)

        def give_line(self, p, c):
            self.col[p, c].wait_recv()
            own, got = line_s.at[self.number], line_r.at[self.number]
            if p == 0:
                self.one[c] = send(own.at[1, cut(c)], got.at[0, cut(c)], line[1])
            else:
                self.relay[c] = send(own.at[3, cut(c)], got.at[3, cut(c)], line[1], ends)
                self.three[c] = send(own.at[3, cut(c)], got.at[2, cut(c)], line[3], middle)
                slot = copies.slot()
                self.two[c] = send(own.at[2, cut(c)], got.at[1, cut(c)], line[2], ends, slot)

        def relay_line(self, c):
            own, got = line_s.at[self.number], line_r.at[self.number]

            @pl.when(middle)
            def _():
                self.relay[c].wait_recv()
                own[2, cut(c), :] = (own[2, cut(c), :].astype(f32) + got[3, cut(c), :].astype(f32)).astype(bf16)
                self.two[c].start()

            sent[:] = [[e[0], None] if e[0] is self.two[c] else e for e in sent]

        def finish(self, c):
            own, got = line_s.at[self.number], line_r.at[self.number]
            self.one[c].wait_recv()
            self.two[c].wait_recv()
            total = own[0, cut(c), :].astype(f32) + got[0, cut(c), :].astype(f32) + got[1, cut(c), :].astype(f32)
            dn_s[cut(c), :] = total

            @pl.when(middle)
            def _():
                self.three[c].wait_recv()
                dn_s[cut(c), :] += got[2, cut(c), :].astype(f32)

            if self.number:
                dn_out[cut(c), :] = dn_s[cut(c), :]
            else:
                block_out[cut(c), :] = (tok[cut(c), :].astype(f32) + dn_s[cut(c), :] + bias_ref[0:1, :]).astype(bf16)

    g_near, g_line, d_near = {}, {}, {}
    q_width, u_width = q_v.shape[1], u_v.shape[1]

    def grad_block(dst):
        need(3, 4)
        source = take()
        dst[:, pl.ds(0, q_width)] = t_mm(source[...], q_v[...]).astype(bf16)
        dst[:, pl.ds(q_width, u_width)] = t_mm(source[...], u_v[...]).astype(bf16)

    def grad_other(s):
        grad_block(go_s.at[s])
        g_near[s] = send(go_s.at[s], go_r.at[s], col)

    def grad_line(s):
        g_near[s].wait_recv()
        gm_s[s] = (gm_s[s].astype(f32) + go_r[s].astype(f32)).astype(bf16)
        if s:
            g_line[s] = send(gm_s.at[s], g_out.at[line_id], line[s])
        else:
            load = pltpu.make_async_copy(gm_s.at[0], g_out.at[line_id], load_sems.at[len(loads)])
            load.start()
            loads.append([load, False])

    turned = [False]

    def out_block(j, other):
        need(0, 1)
        if not turned[0]:
            at_v[0:part, :] = a_v[...].T
            at_v[part:, :] = h_v[...].T
            turned[0] = True
        source = take()
        at = pl.ds(j * block, block)
        value = mm(at_v[...], source[...])
        if other:
            do_s[j] = value.astype(bf16)
            d_near[j] = send(do_s.at[j], do_r.at[j], col)
        else:
            dm_s[:, at] = value

    def out_finish(j):
        d_near[j].wait_recv()
        at = pl.ds(j * block, block)
        dm_s[:, at] += do_r[j].astype(f32)
        load = pltpu.make_async_copy(dm_s.at[:, at], gd_out.at[:, at], load_sems.at[len(loads)])
        load.start()
        loads.append([load, False])

    old, new = Stream(0), Stream(1)
    both = (old, new)
    for what, *args in order:
        if what == "c": both[args[0]].compute(*args[1:])
        if what == "x": both[args[0]].give_far(*args[1:])
        if what == "y": both[args[0]].give_col(*args[1:])
        if what == "z": both[args[0]].give_line(*args[1:])
        if what == "r": both[args[0]].relay_line(*args[1:])
        if what == "f": both[args[0]].finish(*args[1:])
        if what == "go": grad_other(*args)
        if what == "gm": grad_block(gm_s.at[args[0]])
        if what == "gz": grad_line(*args)
        if what == "do": out_block(args[0], True)
        if what == "dm": out_block(args[0], False)
        if what == "df": out_finish(*args)
    for copy in g_line.values():
        copy.wait_recv()
    need(*range(len(loads)))
    for copy, when in list(sent):
        wait_sent(copy)


def scatter_order():
    return [
        ("c", 0, 1, 0), ("go", 1), ("c", 0, 1, 1), ("x", 0, 1, 0), ("go", 2), ("x", 0, 1, 1),
        ("c", 0, 0, 0), ("gm", 1), ("x", 0, 0, 0), ("c", 0, 0, 1), ("gm", 2), ("x", 0, 0, 1),
        ("gz", 1), ("y", 0, 1, 0), ("go", 3), ("gm", 3), ("z", 0, 1, 0), ("y", 0, 1, 1), ("gz", 2),
        ("c", 1, 1, 0), ("x", 1, 1, 0), ("z", 0, 1, 1), ("r", 0, 0), ("y", 0, 0, 0), ("c", 1, 1, 1), ("x", 1, 1, 1), ("go", 0), ("gm", 0),
        ("r", 0, 1), ("z", 0, 0, 0), ("y", 0, 0, 1), ("c", 1, 0, 0), ("x", 1, 0, 0), ("gz", 3),
        ("z", 0, 0, 1), ("c", 1, 0, 1), ("x", 1, 0, 1), ("do", 0), ("f", 0, 0), ("y", 1, 1, 0), ("do", 1), ("gz", 0),
        ("z", 1, 1, 0), ("y", 1, 1, 1), ("f", 0, 1), ("do", 2), ("r", 1, 0), ("z", 1, 1, 1), ("y", 1, 0, 0), ("do", 3),
        ("r", 1, 1), ("z", 1, 0, 0), ("dm", 0), ("dm", 1), ("y", 1, 0, 1), ("dm", 2), ("dm", 3), ("z", 1, 0, 1),
        ("f", 1, 0), ("df", 0), ("df", 1), ("df", 2), ("df", 3), ("f", 1, 1),
    ]


def scatter(tier_count, attn, hidden, dqkv, dup, normed, back, qkv_mat, up_mat, out_mat, tok, bias, order=None):
    rows, half = tok.shape
    width = 2 * half
    chunk = rows // CH
    all_rows = attn.shape[0]
    part = attn.shape[1]
    sds = jax.ShapeDtypeStruct
    any_ = pl.BlockSpec(memory_space=pl.ANY)
    vmem = pl.BlockSpec(memory_space=pltpu.VMEM)
    block = half // 4

    def buf(*shape, kind=bf16):
        return pltpu.VMEM(shape, kind)

    return pl.pallas_call(
        functools.partial(scatter_kernel, tier_count, order or scatter_order()),
        out_shape=[sds((rows, half), bf16), sds((rows, half), f32), sds((4, block, 7 * part), bf16), sds((5 * part, half), f32)],
        in_specs=[any_] * 9 + [vmem, vmem],
        out_specs=[vmem, vmem, any_, any_],
        scratch_shapes=[
            buf(all_rows, part), buf(all_rows, 4 * part), buf(all_rows, 3 * part), buf(all_rows, 4 * part),
            buf(width, 3 * part), buf(width, 4 * part), buf(5 * part, width), buf(5 * part, all_rows),
            buf(2, all_rows, block), buf(4, 4, chunk, width), buf(8, 2, chunk, width), buf(8, chunk, width),
            buf(2, 4, rows, half), buf(2, 4, rows, half),
            buf(4, block, 7 * part), buf(4, block, 7 * part), buf(4, block, 7 * part),
            buf(4, 5 * part, block), buf(4, 5 * part, block), buf(5 * part, half, kind=f32), buf(rows, half, kind=f32),
            pltpu.SemaphoreType.DMA((64,)), pltpu.SemaphoreType.DMA((64,)), pltpu.SemaphoreType.DMA((16,)), pltpu.SemaphoreType.DMA((2,)),
        ],
        compiler_params=pltpu.CompilerParams(collective_id=2, has_side_effects=True, vmem_limit_bytes=62 << 20),
    )(attn, hidden, dqkv, dup, normed, back, qkv_mat, up_mat, out_mat, tok, bias)


def per_device(
    tokens,
    cotangent,
    doc_lengths,
    doc_groups,
    w_qkv,
    w_up,
    w_dense,
    w_down,
    vectors,
    m_qkv,
    v_qkv,
    m_up,
    v_up,
    m_dense,
    v_dense,
    m_down,
    v_down,
    m_vec,
    v_vec,
):
    dp_count = lax.axis_size("dp")
    tier_count = dp_count // LINE
    dp_id = lax.axis_index("dp")
    line_id = dp_id // tier_count
    tier_id = dp_id % tier_count
    row_count = lax.axis_size("row")
    col_count = lax.axis_size("col")
    assert row_count == 4 and col_count == 2 and dp_count % LINE == 0
    row_id = lax.axis_index("row")
    col_id = lax.axis_index("col")
    tok_dev, half_width = tokens.shape
    slot_count = tok_dev * row_count
    full_width = half_width * col_count
    row_width = full_width // row_count
    part = row_width // LINE
    heads_dev = part // HDIM
    zero_index = jnp.int32(0)
    tier_groups = [[line * tier_count + tier for tier in range(tier_count)] for line in range(LINE)]

    def over_line(value, bits):
        pairs = [(i, ((i // tier_count) ^ bits) * tier_count + i % tier_count) for i in range(dp_count)]
        return lax.ppermute(value, "dp", pairs)

    def over_row(value, bits):
        return lax.ppermute(value, "row", [(i, i ^ bits) for i in range(row_count)])

    def over_col(value):
        return lax.ppermute(value, "col", [(0, 1), (1, 0)])

    def reorder(blocks, place):
        one = (place & 1) == 1
        two = (place & 2) == 2
        blocks = [jnp.where(one, blocks[i ^ 1], blocks[i]) for i in range(4)]
        return [jnp.where(two, blocks[i ^ 2], blocks[i]) for i in range(4)]

    def sum_all(value):
        value = sum(reorder([value] + [over_line(value, s) for s in (1, 2, 3)], line_id))
        value = sum(reorder([value] + [over_row(value, s) for s in (1, 2, 3)], row_id))
        value = value + over_col(value)
        if tier_count > 1:
            value = lax.psum(value, "dp", axis_index_groups=tier_groups)
        return value

    part_start = row_id * row_width + line_id * part
    col_start = col_id * half_width

    total_len = jnp.sum(jnp.where(doc_groups == dp_id, doc_lengths, 0), dtype=jnp.int32)
    own_valid = row_id * tok_dev + jnp.arange(tok_dev, dtype=jnp.int32) < total_len
    back_own = jnp.where(own_valid[:, None], cotangent, jnp.zeros_like(cotangent))

    def tier_gather(value):
        if tier_count > 1:
            value = lax.all_gather(value, "dp", axis=0, tiled=True, axis_index_groups=tier_groups)
        return value

    if tier_count > 1:
        full_qkv, full_up, full_dense, full_down = [
            tier_gather(weight.astype(bf16)).astype(f32) for weight in (w_qkv, w_up, w_dense, w_down)
        ]
    else:
        full_qkv, full_up, full_dense, full_down = w_qkv, w_up, w_dense, w_down
    normed, back, qkv_mat, up_mat, out_mat = gather(
        tier_count,
        doc_lengths,
        doc_groups,
        tokens,
        cotangent,
        vectors,
        full_qkv.transpose(1, 0, 2),
        full_up,
        full_dense,
        full_down,
    )
    rows_all = 2 * slot_count
    normed = normed.reshape(rows_all, full_width)
    back = back.reshape(rows_all, full_width)
    qkv_mat = qkv_mat.reshape(full_width, 3 * part)
    up_mat = up_mat.reshape(full_width, 4 * part)

    bias_qkv = lax.dynamic_slice(vectors[2:5], (zero_index, part_start), (3, part)).reshape(3 * part)
    bias_up = lax.dynamic_slice(vectors[5:9], (zero_index, part_start), (4, part)).reshape(4 * part)

    bias = jnp.concatenate([bias_qkv, bias_up])[None]
    attn, hidden, d_qkv, d_pre_up, bias_sums = local_part(
        tier_count,
        doc_lengths,
        doc_groups,
        normed.reshape(2, slot_count, full_width),
        back.reshape(2, slot_count, full_width),
        qkv_mat,
        up_mat,
        out_mat,
        bias,
    )
    bias_sums = bias_sums[:, 0]
    out_bias = lax.dynamic_slice_in_dim(vectors[9] + vectors[10], col_start, half_width, 0)
    block_out, d_normed, grad_in, grad_out = scatter(
        tier_count,
        attn.reshape(rows_all, part),
        hidden.reshape(rows_all, 4 * part),
        d_qkv.reshape(rows_all, 3 * part),
        d_pre_up.reshape(rows_all, 4 * part),
        normed,
        back,
        qkv_mat,
        up_mat,
        out_mat,
        tokens,
        out_bias[None],
    )
    bias_sums = jnp.sum(bias_sums, axis=0).reshape(7, part)

    def tier_sum(value):
        if tier_count > 1:
            value = lax.psum_scatter(
                value, "dp", scatter_dimension=0, tiled=True, axis_index_groups=tier_groups
            )
        return value

    def own_columns(value, parts):
        value = value.astype(f32).reshape(LINE, half_width // LINE, parts, part)
        return tier_sum(value.transpose(1, 2, 0, 3).reshape(half_width // LINE, parts, row_width))

    red_qkv = own_columns(grad_in[:, :, : 3 * part], 3)
    red_up = own_columns(grad_in[:, :, 3 * part :], 4)
    red_dense = tier_sum(grad_out[:part])
    red_down = tier_sum(grad_out[part:].reshape(4, part, half_width).transpose(1, 0, 2))
    tokens_own = tokens.astype(f32)
    own_sums = jnp.stack([jnp.sum(tokens_own, axis=-1), jnp.sum(tokens_own * tokens_own, axis=-1)])
    own_sums = (own_sums + over_col(own_sums)) / full_width
    mean_own = own_sums[0][:, None]
    inv_own = lax.rsqrt(own_sums[1][:, None] - mean_own * mean_own + eps_norm)
    centred = (tokens_own - mean_own) * inv_own
    gain_cols = lax.dynamic_slice_in_dim(vectors[0], col_start, half_width, 0)
    d_hat = d_normed * gain_cols[None, :]
    hat_sums = jnp.stack([jnp.sum(d_hat, axis=-1), jnp.sum(d_hat * centred, axis=-1)])
    hat_sums = (hat_sums + over_col(hat_sums)) / full_width
    back_float = back_own.astype(f32)
    grad_tokens = inv_own * (d_hat - hat_sums[0][:, None] - centred * hat_sums[1][:, None]) + back_float

    early = jnp.zeros((9, full_width), f32)
    early = lax.dynamic_update_slice(early, bias_sums, (zero_index, part_start))
    out_sums = jnp.sum(back_float, axis=0)
    early = lax.dynamic_update_slice(early, jnp.stack([out_sums, out_sums]), (jnp.int32(7), col_start))
    late = lax.dynamic_update_slice(
        jnp.zeros((2, full_width), f32),
        jnp.stack([jnp.sum(d_normed * centred, axis=0), jnp.sum(d_normed, axis=0)]),
        (zero_index, col_start),
    )
    vec_grad = jnp.concatenate([sum_all(late), sum_all(early)], axis=0)
    qkv_new = adamw(w_qkv, m_qkv, v_qkv, red_qkv, D ** (-0.5), 0.1)
    up_new = adamw(w_up, m_up, v_up, red_up, D ** (-0.5), 0.1)
    dense_new = adamw(w_dense, m_dense, v_dense, red_dense, max(D // 128, 4) ** (-0.5), 0.1)
    down_new = adamw(w_down, m_down, v_down, red_down, FF ** (-0.5), 0.1)
    vec_new = adamw(vectors, m_vec, v_vec, vec_grad, 0.5, 0.0)
    return (
        block_out,
        grad_tokens,
        qkv_new[0],
        qkv_new[1],
        qkv_new[2],
        up_new[0],
        up_new[1],
        up_new[2],
        dense_new[0],
        dense_new[1],
        dense_new[2],
        down_new[0],
        down_new[1],
        down_new[2],
        vec_new[0],
        vec_new[1],
        vec_new[2],
    )


def solution(mesh):
    placed = (
        P(("dp", "row"), "col"),
        P(("dp", "row"), "col"),
        P(),
        P(),
        P(("col", "dp"), None, "row"),
        P(("col", "dp"), None, "row"),
        P(("row", "dp"), "col"),
        P(("row", "dp"), None, "col"),
        P(),
        P(("col", "dp"), None, "row"),
        P(("col", "dp"), None, "row"),
        P(("col", "dp"), None, "row"),
        P(("col", "dp"), None, "row"),
        P(("row", "dp"), "col"),
        P(("row", "dp"), "col"),
        P(("row", "dp"), None, "col"),
        P(("row", "dp"), None, "col"),
        P(),
        P(),
    )
    return jax.shard_map(
        per_device,
        mesh=mesh,
        in_specs=placed,
        out_specs=(
            P(("dp", "row"), "col"),
            P(("dp", "row"), "col"),
            P(("col", "dp"), None, "row"),
            P(("col", "dp"), None, "row"),
            P(("col", "dp"), None, "row"),
            P(("col", "dp"), None, "row"),
            P(("col", "dp"), None, "row"),
            P(("col", "dp"), None, "row"),
            P(("row", "dp"), "col"),
            P(("row", "dp"), "col"),
            P(("row", "dp"), "col"),
            P(("row", "dp"), None, "col"),
            P(("row", "dp"), None, "col"),
            P(("row", "dp"), None, "col"),
            P(),
            P(),
            P(),
        ),
        check_vma=False,
    )
```

```python
import functools

import jax
import jax.numpy as jnp
from jax import lax
from jax.experimental import pallas as pl
from jax.experimental.pallas import tpu as pltpu
from jax.sharding import PartitionSpec as P

D = 2048
HDIM = 64
ROT = 32
FF = 8192
BLK = 512
STEP = 10
LINE = 4


eps_norm = 1e-05
f32 = jnp.float32
bf16 = jnp.bfloat16


def adamw(weight, first_moment, second_moment, gradient, rate, decay):
    first_next = 0.9 * first_moment + 0.1 * gradient
    second_next = 0.95 * second_moment + 0.05 * gradient * gradient
    correct_one = 1.0 - 0.9**STEP
    correct_two = 1.0 - 0.95**STEP
    update = first_next / correct_one / (jnp.sqrt(second_next / correct_two) + 1e-08)
    return (first_next, second_next, weight - rate * (update + decay * weight))


def mm(a, b):
    return jnp.dot(a, b, preferred_element_type=f32)


def mm_t(a, b):
    return lax.dot_general(a, b, (((1,), (1,)), ((), ())), preferred_element_type=f32)


def t_mm(a, b):
    return lax.dot_general(a, b, (((0,), (0,)), ((), ())), preferred_element_type=f32)


def gelu_both(v):
    root = 0.7978845608028654
    square = v * v
    slope = root * (1.0 + 3 * 0.044715 * square)
    tanh = jnp.tanh(root * v * (1.0 + 0.044715 * square))
    outer = 0.5 * (1.0 + tanh)
    return v * outer, outer + 0.5 * v * (1.0 - tanh * tanh) * slope


def turn(value, turns, sign):
    part = value.shape[1]
    quarter = ROT // 2
    lead = lax.broadcasted_iota(jnp.int32, (1, part), 1) % HDIM < quarter
    other = jnp.where(lead, jnp.roll(value, -quarter, axis=1), jnp.roll(value, quarter, axis=1))
    return value * turns[:, 0:part] + sign * (other * turns[:, part:])


class Forward:
    def __init__(self, tier_count, lengths, groups, x_ref, wq_ref, wu_ref, vec_ref, attn_ref, hidden_ref, slope_ref, qkv_ref, turn_ref, stat_ref):
        self.tier_count, self.lengths, self.groups = tier_count, lengths, groups
        self.x_ref, self.wq_ref, self.wu_ref = x_ref, wq_ref, wu_ref
        self.attn_ref, self.hidden_ref, self.slope_ref = attn_ref, hidden_ref, slope_ref
        self.qkv_ref, self.turn_ref, self.stat_ref = qkv_ref, turn_ref, stat_ref
        slots, part = attn_ref.shape
        self.slots, self.part, self.rows = slots, part, slots // 4
        row_id = lax.axis_index("row")
        self.quarters = [row_id, row_id + 1 - 2 * (row_id % 2), (row_id + 2) % 4, 3 - row_id]
        self.line_id = lax.axis_index("dp") // tier_count
        bias_at = pl.ds(pl.multiple_of((row_id * LINE + self.line_id) * part, part), part)
        self.bias = jnp.concatenate([vec_ref[k:k + 1, bias_at] for k in range(2, 9)], axis=1)
        self.key_place = jnp.concatenate(
            [self.quarters[t] * self.rows + lax.broadcasted_iota(jnp.int32, (1, self.rows), 1) for t in range(4)], axis=1)

    def cut(self, i):
        return pl.ds(i * self.rows, self.rows)

    def angles(self, p):
        lengths, groups, part, rows, quarters = self.lengths, self.groups, self.part, self.rows, self.quarters
        line_id, tier_id = self.line_id, lax.axis_index("dp") % self.tier_count
        turn_ref, stat_ref = self.turn_ref, self.stat_ref
        quarter = ROT // 2
        bit = (line_id % 2 + lax.axis_index("col")) % 2
        group = line_id + bit * (1 - 2 * (line_id % 2))
        group = ((group + 2 * p) % 4) * self.tier_count + tier_id
        lanes = lax.broadcasted_iota(jnp.int32, (1, part), 1) % HDIM
        lead = lanes < quarter
        powers = (lanes % quarter).astype(f32) * (-2.0 / ROT)
        speed = jnp.where(lanes < ROT, jnp.exp(powers * 9.210340371976184), 0.0)
        fine = lax.broadcasted_iota(jnp.int32, (32, part), 0).astype(f32) * speed
        fine_cos, fine_sin = jnp.cos(fine), jnp.sin(fine)
        count = lengths.shape[0] + 1
        starts, start = [], jnp.int32(0)
        for i in range(count - 1):
            here = groups[i] == group
            starts.append(jnp.where(here, start, 1 << 30))
            start = start + jnp.where(here, lengths[i], 0)
        starts.append(start)
        which = lax.broadcasted_iota(jnp.int32, (-(-count // 8) * 8, part), 0)
        start_angle = jnp.zeros(which.shape, f32)
        for i in range(count):
            start_angle = jnp.where(which == i, jnp.where(starts[i] < (1 << 30), starts[i], 0).astype(f32), start_angle)
        start_angle = start_angle * speed
        start_cos, start_sin = jnp.cos(start_angle), jnp.sin(start_angle)
        steps = rows // 32
        for t in range(4):
            base = quarters[t] * rows
            coarse = (base + 32 * lax.broadcasted_iota(jnp.int32, (steps, part), 0)).astype(f32) * speed
            coarse_cos, coarse_sin = jnp.cos(coarse), jnp.sin(coarse)
            for j in range(2):
                some = range(j * steps // 2, (j + 1) * steps // 2)
                size = rows // 2
                place_cos = jnp.concatenate([coarse_cos[i:i + 1] * fine_cos - coarse_sin[i:i + 1] * fine_sin for i in some])
                place_sin = jnp.concatenate([coarse_sin[i:i + 1] * fine_cos + coarse_cos[i:i + 1] * fine_sin for i in some])
                place = base + j * size + lax.broadcasted_iota(jnp.int32, (size, part), 0)
                first = jnp.zeros((size, part), jnp.int32)
                first_cos = jnp.ones((size, part), f32)
                first_sin = jnp.zeros((size, part), f32)
                for i in range(count):
                    after = place >= starts[i]
                    first = jnp.where(after, starts[i], first)
                    first_cos = jnp.where(after, start_cos[i:i + 1], first_cos)
                    first_sin = jnp.where(after, start_sin[i:i + 1], first_sin)
                at = pl.ds(t * rows + j * size, size)
                turn_ref[at, 0:part] = place_cos * first_cos + place_sin * first_sin
                sin = place_sin * first_cos - place_cos * first_sin
                turn_ref[at, part:] = jnp.where(lead, -sin, sin)
                lane = lax.broadcasted_iota(jnp.int32, (size, part), 1)
                stat_ref[at, :] = jnp.where(lane == part - 1, first.astype(f32), 0.0)

    def project(self, i):
        part, at = self.part, self.cut(i)
        pre = mm(self.x_ref[at, :], self.wq_ref[...]) + self.bias[:, 0:3 * part]
        turns = self.turn_ref[at, :]
        self.qkv_ref[at, 0:part] = turn(pre[:, 0:part], turns, 1.0).astype(bf16)
        self.qkv_ref[at, part:2 * part] = turn(pre[:, part:2 * part], turns, 1.0).astype(bf16)
        self.qkv_ref[at, 2 * part:] = pre[:, 2 * part:].astype(bf16)

    def up(self, i):
        at = self.cut(i)
        value, slope = gelu_both(mm(self.x_ref[at, :], self.wu_ref[...]) + self.bias[:, 3 * self.part:])
        self.hidden_ref[at, :] = value.astype(bf16)
        self.slope_ref[at, :] = slope

    def attend(self, i):
        part, at, rows = self.part, self.cut(i), self.rows
        lane = lax.broadcasted_iota(jnp.int32, (rows, part), 1)
        keys, values = self.qkv_ref[:, part:2 * part], self.qkv_ref[:, 2 * part:]
        stat = self.stat_ref[at, :]
        place = self.quarters[i] * rows + lax.broadcasted_iota(jnp.int32, (rows, 1), 0)
        allowed = (self.key_place >= stat[:, part - 1:part].astype(jnp.int32)) & (self.key_place <= place)
        queries = self.qkv_ref[at, 0:part]
        out = jnp.zeros((rows, part), f32)
        for h in range(part // HDIM):
            head = (lane >= h * HDIM) & (lane < (h + 1) * HDIM)
            q_h = jnp.where(head, queries, jnp.zeros_like(queries))
            scores = jnp.where(allowed, mm_t(q_h, keys) * HDIM ** (-0.5), -1e30)
            top = jnp.max(scores, axis=-1, keepdims=True)
            weights = jnp.exp(scores - top)
            total = jnp.sum(weights, axis=-1, keepdims=True)
            low = (weights * (1.0 / total)).astype(bf16)
            out = jnp.where(head, mm(low, values), out)
            stat = jnp.where(lane == h, top + jnp.log(total), stat)
        self.attn_ref[at, :] = out.astype(bf16)
        self.stat_ref[at, :] = stat


class Copies:
    def __init__(self, send_sems, recv_sems):
        self.send_sems, self.recv_sems, self.sent, self.received = send_sems, recv_sems, 0, 0

    def slot(self):
        self.received += 1
        return self.received - 1

    def make(self, src, dst, device, slot=None):
        slot = self.slot() if slot is None else slot
        self.sent += 1
        return pltpu.make_async_remote_copy(
            src_ref=src, dst_ref=dst, send_sem=self.send_sems.at[self.sent - 1], recv_sem=self.recv_sems.at[slot],
            device_id=device, device_id_type=pl.DeviceIdType.MESH)

def neighbours(tier_count):
    dp_id, row_id, col_id = lax.axis_index("dp"), lax.axis_index("row"), lax.axis_index("col")
    line_id, tier_id = dp_id // tier_count, dp_id % tier_count
    flips = [line_id, line_id + 1 - 2 * (line_id % 2), (line_id + 2) % 4, 3 - line_id]
    line = [(flip * tier_count + tier_id, row_id, col_id) for flip in flips]
    core = (dp_id, row_id + 1 - 2 * (row_id % 2), col_id)
    far = (dp_id, (row_id + 2) % 4, col_id)
    col = (dp_id, row_id, 1 - col_id)
    return line_id, flips, line, core, far, col

def meet(peers):
    barrier = pltpu.get_barrier_semaphore()
    for peer in peers:
        pl.semaphore_signal(barrier, inc=1, device_id=peer, device_id_type=pl.DeviceIdType.MESH)
    pl.semaphore_wait(barrier, len(peers))


CH = 2
DEPTH = 2

def gather_kernel(tier_count, order, lengths, groups, tok, cot, vec_ref, w_qkv, w_up, w_dense, w_down,
                  x_out, b_out, wq_out, wu_out, d_out, cot_s, attn_out, hidden_out, slope_out, qkv_out, turn_out, stat_out,
                  x_v, wq_v, wu_v, attn_v, hidden_v, slope_v, qkv_v, turn_v, stat_v, tz, cz, ty, xs, qkv_f, up_f, dense_f, down_f, wq, wu, dh,
                  send_sems, recv_sems, local_sems, load_sems, into_sems, out_sems):
    line_id, flips, line, core, far, col = neighbours(tier_count)
    bit = (line_id % 2 + lax.axis_index("col")) % 2
    middle = (line_id == 1) | (line_id == 2)
    rows, half = tok.shape
    chunk = rows // CH
    copies = Copies(send_sems, recv_sems)
    sent, mid_sent, local_left, last = [], [], [], []
    n_local = [0]

    def local(src, dst):
        copy = pltpu.make_async_copy(src, dst, local_sems.at[n_local[0]])
        n_local[0] += 1
        copy.start()
        local_left.append(copy)
        return copy

    def settle(copy):
        if any(c is copy for c in local_left):
            copy.wait()
            local_left[:] = [c for c in local_left if c is not copy]

    def arrive(copy):
        if any(c is copy for c in last):
            copy.wait_recv()
            last[:] = [c for c in last if c is not copy]

    def send(src, dst, device, slot=None):
        copy = copies.make(src, dst, device, slot)
        copy.start()
        sent.append(copy)
        return copy

    def cut(c):
        return pl.ds(c * chunk, chunk)

    class Stream:
        def __init__(self, own, stage, out, normed):
            self.own, self.stage, self.out, self.normed = own, stage, out, normed
            self.line, self.swap, self.spread, self.keep, self.whole = {}, {}, {}, {}, ([], [])

        def start(self, c):
            own, stage = self.own.at[cut(c)], self.stage
            own_copy = local(own, stage.at[0, cut(c)])
            near = send(own, stage.at[1, cut(c)], line[1])
            two = send(own, stage.at[2, cut(c)], line[2])
            slot = copies.slot()
            three = copies.make(own, stage.at[3, cut(c)], line[3], slot)
            relay = copies.make(stage.at[2, cut(c)], stage.at[3, cut(c)], line[1], slot)
            pl.when(middle)(three.start)
            mid_sent.extend([three, relay])
            self.line[c] = own_copy, near, two, three, relay

        def swap_cols(self, c, p):
            own_copy, near, two, three, relay = self.line[c]
            if p == 0:
                settle(own_copy)
                near.wait_recv()
            else:
                three.wait_recv()
            if self.normed:
                dst = ty.at[p, cut(c)]
            else:
                dst = self.out.at[p, 0, cut(c), pl.ds(half, half)]
                self.keep[c, p] = local(self.stage.at[2 * p + bit, cut(c)], self.out.at[p, 0, cut(c), pl.ds(0, half)])
            self.swap[c, p] = send(self.stage.at[2 * p + 1 - bit, cut(c)], dst, col)

        def pass_on(self, c):
            own_copy, near, two, three, relay = self.line[c]
            two.wait_recv()
            pl.when(middle)(relay.start)

        def give(self, c, p):
            self.swap[c, p].wait_recv()
            if self.normed:
                norm(c, p)
                src = xs.at[p, cut(c)]
                self.whole[p].append((settle, local(src, self.out.at[p, 0, cut(c)])))
            else:
                settle(self.keep[c, p])
                src = self.out.at[p, 0, cut(c)]
            self.spread[c, p] = send(src, self.out.at[p, 2, cut(c)], far)
            last.append(send(src, self.out.at[p, 1, cut(c)], core))
            self.whole[p].append((arrive, last[-1]))

        def relay(self, c, p):
            self.spread[c, p].wait_recv()
            last.append(send(self.out.at[p, 2, cut(c)], self.out.at[p, 3, cut(c)], core))
            self.whole[p].append((arrive, last[-1]))

    norm_ref = [[vec_ref.at[i:i + 1, pl.ds(pl.multiple_of(side * half, half), half)] for i in range(2)]
                for side in (lax.axis_index("col"), 1 - lax.axis_index("col"))]

    def norm(c, p):
        step = 64
        def body(i, carry):
            at = pl.ds(pl.multiple_of(c * chunk + i * step, step), step)
            one = tz[2 * p + bit, at, :].astype(f32)
            two = ty[p, at, :].astype(f32)
            width = 2 * half
            mean = (jnp.sum(one, axis=-1, keepdims=True) + jnp.sum(two, axis=-1, keepdims=True)) / width
            square = (jnp.sum(one * one, axis=-1, keepdims=True) + jnp.sum(two * two, axis=-1, keepdims=True)) / width
            inv = lax.rsqrt(square - mean * mean + eps_norm)
            xs[p, at, pl.ds(0, half)] = ((one - mean) * inv * norm_ref[0][0][...] + norm_ref[0][1][...]).astype(bf16)
            xs[p, at, pl.ds(half, half)] = ((two - mean) * inv * norm_ref[1][0][...] + norm_ref[1][1][...]).astype(bf16)
            return carry
        lax.fori_loop(0, chunk // step, body, 0)

    class Weight:
        def __init__(self, src, out):
            self.src, self.out, self.got, self.whole = src, out, {}, []

        def own(self):
            self.whole.append((settle, local(self.src.at[line_id], self.out.at[0, line_id])))
            last.append(send(self.src.at[line_id], self.out.at[1, line_id], col))
            self.whole.append((arrive, last[-1]))

        def start(self):
            for s in (1, 2, 3):
                self.got[s] = send(self.src.at[flips[s]], self.out.at[0, line_id], line[s])

        def swap(self):
            for s in (1, 2, 3):
                self.got[s].wait_recv()
                last.append(send(self.out.at[0, flips[s]], self.out.at[1, flips[s]], col))
                self.whole.append((arrive, last[-1]))

    part = dh.shape[0] // 5
    loads = []
    for i, (src, dst) in enumerate(((w_qkv, qkv_f), (w_up, up_f), (w_dense, dense_f), (w_down, down_f), (cot, cot_s))):
        loads.append(pltpu.make_async_copy(src, dst, load_sems.at[i]))
        loads[-1].start()

    def prepare(what):
        if what == 0:
            loads[0].wait()
            for j in range(LINE):
                for k in range(3):
                    wq[j, :, k * part:(k + 1) * part] = qkv_f[k, :, j * part:(j + 1) * part].astype(bf16)
        if what == 1:
            loads[1].wait()
            for j in range(LINE):
                for k in range(4):
                    wu[j, :, k * part:(k + 1) * part] = up_f[:, k, j * part:(j + 1) * part].astype(bf16)
        if what == 2:
            loads[2].wait()
            dh[0:part, :] = dense_f[...].astype(bf16)
        if what == 3:
            loads[3].wait()
            for k in range(4):
                dh[(k + 1) * part:(k + 2) * part, :] = down_f[:, k, :].astype(bf16)
        if what == 4:
            loads[4].wait()
            total = jnp.int32(0)
            for i in range(lengths.shape[0]):
                total = total + jnp.where(groups[i] == lax.axis_index("dp"), lengths[i], 0)
            place = lax.axis_index("row") * rows + lax.broadcasted_iota(jnp.int32, (rows, half), 0)
            cot_s[...] = jnp.where(place < total, cot_s[...], jnp.zeros_like(cot_s))

    def dense(i):
        at = pl.ds(i * part, part)
        last.append(send(dh.at[at], d_out.at[at, pl.ds(half, half)], col))

    meet([line[1], line[2], line[3], core, far, col])
    T = Stream(tok, tz, x_out, True)
    C = Stream(cot_s, cz, b_out, False)
    Q = Weight(wq, wq_out)
    U = Weight(wu, wu_out)
    slots = 4 * rows
    wide = [ref.reshape(2 * half, ref.shape[-1]) for ref in (wq_v, wu_v)]
    fresh = (attn_v, hidden_v, slope_v, qkv_v, turn_v, stat_v)
    steps = [Forward(tier_count, lengths, groups, x_v.at[p].reshape(slots, 2 * half), *wide, vec_ref, *[ref.at[p] for ref in fresh])
             for p in range(2)]
    going, stored = {}, []

    def fetch(i, src, dst, whole):
        for wait, copy in whole:
            wait(copy)
        going[i] = pltpu.make_async_copy(src, dst, into_sems.at[i])
        going[i].start()

    def store(p, *pairs):
        for src, dst in pairs:
            stored.append(pltpu.make_async_copy(src.at[p], dst.at[p], out_sems.at[len(stored)]))
            stored[-1].start()

    def need(*which):
        for i in which:
            if i in going:
                going.pop(i).wait()

    for what, *args in order:
        if what == "Wq":
            for j in range(2):
                fetch(j, wq_out.at[j], wq_v.at[j], Q.whole)
        if what == "Wu":
            for j in range(2):
                fetch(2 + j, wu_out.at[j], wu_v.at[j], U.whole)
        if what == "X":
            fetch(4 + args[0], x_out.at[args[0]], x_v.at[args[0]], T.whole[args[0]])
        if what == "Fa":
            steps[args[0]].angles(args[0])
        if what == "Fp":
            need(0, 1, 4 + args[0])
            steps[args[0]].project(args[1])
        if what == "Fs":
            steps[args[0]].attend(args[1])
            if args[1] == 3:
                store(args[0], (attn_v, attn_out), (qkv_v, qkv_out), (turn_v, turn_out), (stat_v, stat_out))
        if what == "Fu":
            need(2, 3, 4 + args[0])
            steps[args[0]].up(args[1])
            if args[1] == 3:
                store(args[0], (hidden_v, hidden_out), (slope_v, slope_out))
        if what == "P": prepare(*args)
        if what == "Ts": T.start(*args)
        if what == "Tr": T.pass_on(*args)
        if what == "Cr": C.pass_on(*args)
        if what == "Ty": T.swap_cols(*args)
        if what == "Tx": T.give(*args)
        if what == "Tk": T.relay(*args)
        if what == "Cs": C.start(*args)
        if what == "Cy": C.swap_cols(*args)
        if what == "Cx": C.give(*args)
        if what == "Ck": C.relay(*args)
        if what == "Qo": Q.own()
        if what == "Qs": Q.start()
        if what == "Qy": Q.swap()
        if what == "Uo": U.own()
        if what == "Us": U.start()
        if what == "Uy": U.swap()
        if what == "D": dense(*args)
        if what == "Dl": local(dh, d_out.at[:, pl.ds(0, half)])
    for copy in list(last):
        arrive(copy)
    for copy in stored:
        copy.wait()
    for copy in list(local_left):
        settle(copy)
    for copy in sent:
        copy.wait_send()
    for copy in mid_sent:
        pl.when(middle)(copy.wait_send)

ORDER_A = [
    ("Ts", 0), ("P", 1), ("Uo",), ("P", 0), ("P", 3), ("Ts", 1), ("P", 4), ("Fa", 0), ("Fa", 1), ("Tr", 0), ("Tr", 1), ("Ty", 1, 0),
    ("Ty", 0, 1), ("Cs", 1), ("P", 2), ("Qs",), ("Ty", 0, 0), ("Tx", 1, 0), ("D", 4), ("Tx", 0, 0), ("Ty", 1, 1), ("D", 0), ("Cr", 1),
    ("Tx", 1, 1), ("Us",), ("Cy", 1, 0), ("Qo",), ("Tx", 0, 1), ("Tk", 0, 0), ("Tk", 1, 0), ("Qy",), ("Cy", 1, 1), ("Tk", 1, 1), ("Wq",),
    ("X", 0), ("Cx", 1, 0), ("Tk", 0, 1), ("Fp", 0, 0), ("Uy",), ("X", 1), ("Cx", 1, 1), ("Cs", 0), ("Cy", 0, 0), ("Fp", 1, 0),
    ("Fp", 0, 1), ("Fp", 0, 2), ("Fp", 0, 3), ("Dl",), ("Fp", 1, 1), ("Cr", 0), ("Wu",), ("Fs", 0, 0), ("Fu", 0, 0), ("Cx", 0, 0),
    ("Fp", 1, 2), ("Cy", 0, 1), ("Fu", 1, 0), ("Fu", 1, 1), ("Fu", 0, 1), ("Fu", 0, 2), ("D", 3), ("Fp", 1, 3), ("Fs", 1, 0), ("Fu", 1, 2),
    ("Cx", 0, 1), ("D", 2), ("Ck", 1, 1), ("Fs", 0, 1), ("Ck", 0, 0), ("Fu", 0, 3), ("Fu", 1, 3), ("D", 1), ("Fs", 0, 2), ("Ck", 1, 0),
    ("Fs", 1, 1), ("Fs", 1, 2), ("Fs", 1, 3), ("Ck", 0, 1), ("Fs", 0, 3),
]


def gather(tier_count, lengths, groups, tok, cot, vectors, w_qkv, w_up, w_dense, w_down, order=None):
    rows, half = tok.shape
    part = w_dense.shape[0]
    c_rows = w_up.shape[0]
    results = ((1, bf16), (4, bf16), (4, f32), (3, bf16), (2, f32), (1, f32))
    sds = jax.ShapeDtypeStruct
    any_ = pl.BlockSpec(memory_space=pl.ANY)
    smem = pl.BlockSpec(memory_space=pltpu.SMEM)
    return pl.pallas_call(
        functools.partial(gather_kernel, tier_count, order or ORDER_A),
        out_shape=[sds((2, 4, rows, 2 * half), bf16), sds((2, 4, rows, 2 * half), bf16),
                   sds((2, LINE, c_rows, 3 * part), bf16), sds((2, LINE, c_rows, 4 * part), bf16), sds((5 * part, 2 * half), bf16), sds(cot.shape, bf16),
                   *[sds((2, 4 * rows, count * part), kind) for count, kind in results]],
        in_specs=[smem, smem, any_, any_, pl.BlockSpec(memory_space=pltpu.VMEM), any_, any_, any_, any_],
        out_specs=[any_] * 5 + [pl.BlockSpec(memory_space=pltpu.VMEM)] + [any_] * 6,
        scratch_shapes=[pltpu.VMEM((2, 4, rows, 2 * half), bf16), pltpu.VMEM((2, LINE, c_rows, 3 * part), bf16), pltpu.VMEM((2, LINE, c_rows, 4 * part), bf16),
                        *[pltpu.VMEM((2, 4 * rows, count * part), kind) for count, kind in results],
                        pltpu.VMEM((4, rows, half), bf16), pltpu.VMEM((4, rows, half), bf16), pltpu.VMEM((2, rows, half), bf16),
                        pltpu.VMEM((2, rows, 2 * half), bf16),
                        pltpu.VMEM(w_qkv.shape, f32), pltpu.VMEM(w_up.shape, f32), pltpu.VMEM(w_dense.shape, f32), pltpu.VMEM(w_down.shape, f32),
                        pltpu.VMEM((LINE, c_rows, 3 * part), bf16), pltpu.VMEM((LINE, c_rows, 4 * part), bf16), pltpu.VMEM((5 * part, half), bf16),
                        pltpu.SemaphoreType.DMA((80,)), pltpu.SemaphoreType.DMA((80,)), pltpu.SemaphoreType.DMA((24,)), pltpu.SemaphoreType.DMA((5,)),
                        pltpu.SemaphoreType.DMA((6,)), pltpu.SemaphoreType.DMA((12,))],
        compiler_params=pltpu.CompilerParams(collective_id=1, has_side_effects=True, vmem_limit_bytes=60 << 20),
    )(lengths, groups, tok, cot, vectors, w_qkv, w_up, w_dense, w_down)


class Sender:
    def __init__(self, send_sems, recv_sems, load_sems):
        self.copies = Copies(send_sems, recv_sems)
        self.load_sems, self.loads, self.sent = load_sems, [], []

    def load(self, src, dst):
        copy = pltpu.make_async_copy(src, dst, self.load_sems.at[len(self.loads)])
        copy.start()
        self.loads.append([copy, False])
        return len(self.loads) - 1

    def need(self, *which):
        for i in which:
            if not self.loads[i][1]:
                self.loads[i][0].wait()
                self.loads[i][1] = True

    def send(self, src, dst, device, when=None, slot=None):
        copy = self.copies.make(src, dst, device, slot)
        if when is None:
            copy.start()
        else:
            pl.when(when)(copy.start)
        self.sent.append([copy, when])
        return copy

    def late(self, copy):
        self.sent = [[e[0], None] if e[0] is copy else e for e in self.sent]

    def wait_sent(self, copy):
        for entry in self.sent:
            if entry[0] is copy:
                self.sent = [e for e in self.sent if e is not entry]
                copy.wait_send()
                return

    def wait_all(self):
        self.need(*range(len(self.loads)))
        for copy, when in self.sent:
            if when is None:
                copy.wait_send()
            else:
                pl.when(when)(copy.wait_send)


class Columns:
    def __init__(self, buffer, sems, wanted):
        self.buffer, self.sems, self.wanted, self.taken, self.fetches = buffer, sems, wanted, 0, []
        if wanted:
            self.fetch(0)

    def fetch(self, i):
        src, at = self.wanted[i]
        copy = pltpu.make_async_copy(src.at[at], self.buffer.at[i % 2], self.sems.at[i % 2])
        copy.start()
        self.fetches.append(copy)

    def take(self):
        i = self.taken
        self.taken += 1
        if i + 1 < len(self.wanted):
            self.fetch(i + 1)
        self.fetches[i].wait()
        return self.buffer.at[i % 2]


def columns(first, count):
    if not isinstance(first, int):
        first = pl.multiple_of(first, count)
    return slice(None), pl.ds(first, count)


class Stream:
    def __init__(self, sender, tier_count, rows, half, product, part_s, near_r, far_r, line_s, line_r, total_s, free_core, free_far, before=None):
        self.sender, self.rows, self.half, self.product = sender, rows, half, product
        self.part_s, self.near_r, self.far_r, self.line_s, self.line_r, self.total_s = part_s, near_r, far_r, line_s, line_r, total_s
        self.line_id, flips, self.line, self.core, self.far_peer, self.col_peer = neighbours(tier_count)
        self.bit = (self.line_id % 2 + lax.axis_index("col")) % 2
        self.middle = (self.line_id == 1) | (self.line_id == 2)
        self.ends = (self.line_id == 0) | (self.line_id == 3)
        self.chunk = rows // CH
        self.free_core, self.free_far, self.before, self.far_here = free_core, free_far, before, []
        self.near, self.far, self.col, self.one, self.two, self.three, self.relay = {}, {}, {}, {}, {}, {}, {}

    def cut(self, c):
        return pl.ds(c * self.chunk, self.chunk)

    def compute(self, p, c):
        place = CH * p + c
        out = self.part_s.at[place]
        chunk, rows = self.chunk, self.rows
        if self.before:
            for copy in [*self.before.near[p, c], self.before.far[p, c], self.before.col[p, c]]:
                self.sender.wait_sent(copy)
        step = self.half // 2

        def body(n, carry):
            at = pl.ds(pl.multiple_of(n * step, step), step)

            def lhs(ref):
                base = p * 4 * rows + c * chunk
                return jnp.concatenate([ref[pl.ds(base + t * rows, chunk), :] for t in range(4)], axis=0)

            low = self.product(lhs, at).astype(bf16)
            for t in range(4):
                out[t, :, at] = low[t * chunk:(t + 1) * chunk]
            return carry

        lax.fori_loop(0, 2 * self.half // step, body, 0)
        into = self.near_r.at[place]
        if self.before:
            pl.semaphore_wait(self.free_core.at[place], 1)
        self.near[p, c] = [self.sender.send(out.at[1], into.at[0], self.core), self.sender.send(out.at[3], into.at[1], self.core)]

    def give_far(self, p, c):
        place = CH * p + c
        self.near[p, c][1].wait_recv()
        mine = self.part_s.at[place, 2]
        mine[...] = (mine[...].astype(f32) + self.near_r[place, 1].astype(f32)).astype(bf16)
        for copy in list(self.far.values())[:max(0, len(self.far) + 1 - DEPTH)]:
            if not any(copy is other for other in self.far_here):
                copy.wait_recv()
                self.far_here.append(copy)
        if self.before:
            pl.semaphore_wait(self.free_far.at[place], 1)
        self.far[p, c] = self.sender.send(mine, self.far_r.at[place], self.far_peer)

    def give_col(self, p, c):
        place, half = CH * p + c, self.half
        self.near[p, c][0].wait_recv()
        if not any(copy is self.far[p, c] for copy in self.far_here):
            self.far[p, c].wait_recv()
            self.far_here.append(self.far[p, c])
        mine = self.part_s.at[place, 0]
        total = mine[...].astype(f32) + self.near_r[place, 0].astype(f32)
        total = (total + self.far_r[place].astype(f32)).astype(bf16)
        if not self.before:
            for sem, peer in ((self.free_core, self.core), (self.free_far, self.far_peer)):
                pl.semaphore_signal(sem.at[place], inc=1, device_id=peer, device_id_type=pl.DeviceIdType.MESH)
        self.line_s[2 * p + self.bit, self.cut(c), :] = total[:, :half]
        mine[:, pl.ds(half, half)] = total[:, half:]
        self.col[p, c] = self.sender.send(mine.at[:, pl.ds(half, half)], self.line_s.at[2 * p + self.bit, self.cut(c)], self.col_peer)

    def give_line(self, p, c):
        self.col[p, c].wait_recv()
        own, got, cut, send = self.line_s, self.line_r, self.cut(c), self.sender.send
        if p == 0:
            self.one[c] = send(own.at[1, cut], got.at[0, cut], self.line[1])
        else:
            self.relay[c] = send(own.at[3, cut], got.at[3, cut], self.line[1], self.ends)
            self.three[c] = send(own.at[3, cut], got.at[2, cut], self.line[3], self.middle)
            self.two[c] = send(own.at[2, cut], got.at[1, cut], self.line[2], self.ends)

    def relay_line(self, c):
        own, got, cut = self.line_s, self.line_r, self.cut(c)

        @pl.when(self.middle)
        def _():
            self.relay[c].wait_recv()
            own[2, cut, :] = (own[2, cut, :].astype(f32) + got[3, cut, :].astype(f32)).astype(bf16)
            self.two[c].start()

        self.sender.late(self.two[c])

    def finish(self, c):
        own, got, cut, total_s = self.line_s, self.line_r, self.cut(c), self.total_s
        self.one[c].wait_recv()
        self.two[c].wait_recv()
        total_s[cut, :] = own[0, cut, :].astype(f32) + got[0, cut, :].astype(f32) + got[1, cut, :].astype(f32)

        @pl.when(self.middle)
        def _():
            self.three[c].wait_recv()
            total_s[cut, :] += got[2, cut, :].astype(f32)

    def run(self, what, args):
        {"c": self.compute, "x": self.give_far, "y": self.give_col, "z": self.give_line, "r": self.relay_line, "f": self.finish}[what](*args)


class InGrad:
    def __init__(self, sender, tier_count, taker, rhs, out, mine_s, mine_r):
        self.sender, self.taker, self.rhs, self.out, self.mine_s, self.mine_r = sender, taker, rhs, out, mine_s, mine_r
        self.line_id, flips, self.line, core, far, self.col = neighbours(tier_count)
        self.near, self.given = {}, []

    def other(self, s):
        self.mine_s[s] = t_mm(self.taker.take()[...], self.rhs[...]).astype(bf16)
        self.near[s] = self.sender.send(self.mine_s.at[s], self.mine_r.at[s], self.col)

    def mine(self, s):
        value = t_mm(self.taker.take()[...], self.rhs[...])
        self.near[s].wait_recv()
        self.sender.wait_sent(self.near[s])
        self.mine_s[s] = (value + self.mine_r[s].astype(f32)).astype(bf16)
        if s:
            self.given.append(self.sender.send(self.mine_s.at[s], self.out.at[self.line_id], self.line[s]))
        else:
            self.sender.load(self.mine_s.at[0], self.out.at[self.line_id])

    def wait(self):
        for copy in self.given:
            copy.wait_recv()


def backward_kernel(tier_count, order, attn, hidden, slope, qkv, turns, stat, x_in, b_in, dm, wq, wu, tok, cot, vec_ref,
                  block_out, grad_out, gin_out, gd_out, vec_out,
                  a_v, h_v, d_v, at_v, qkv_v, turn_v, stat_v, wq_v, wu_v, da_v, dq_v, du_v, dk_s, dv_s, col_v, back_v, slope_v,
                  part_s, near_r, far_r, line_s, line_r, dn_s, gq_s, gq_r, gu_s, gu_r, do_s, do_r, dm_s,
                  stat_s, stat_r, stat_own, hat_s, hat_r, row_s, row_r, mid_s, mid_r, end_s, end_r, out_s, out_r, out_mid, out_end,
                  bias_s, bias_r, bias_v, send_sems, recv_sems, load_sems, free_core, free_far, col_sems, back_sems, slope_sems):
    line_id, flips, line, core, far, col = neighbours(tier_count)
    rows, half = tok.shape
    part = a_v.shape[1]
    slots = 4 * rows
    width = 2 * half
    col_id, row_id = lax.axis_index("col"), lax.axis_index("row")
    across = (lax.axis_index("dp"), 3 - row_id, col_id)
    row_peers = [core, far, across]
    block = half // 4
    scale = HDIM ** (-0.5)
    sender = Sender(send_sems, recv_sems, load_sems)
    for src, dst in ((attn, a_v), (hidden, h_v), (dm, d_v), (qkv, qkv_v), (turns, turn_v), (stat, stat_v), (wq, wq_v), (wu, wu_v)):
        sender.load(src, dst)
    send = sender.send
    wanted = []
    for what, *args in order:
        if what in ("qo", "qm", "uo", "um"):
            wanted.append((x_in, columns(flips[args[0]] * block + (half if what[1] == "o" else 0), block)))
        if what in ("do", "dm"):
            wanted.append((b_in, columns(args[0] * block + (half if what == "do" else 0), block)))
    taker = Columns(col_v, col_sems, wanted)
    b_rows = Columns(back_v, back_sems, [(b_in, (pl.ds(args[0] * rows, rows), slice(None))) for what, *args in order if what == "a"])
    s_rows = Columns(slope_v, slope_sems, [(slope, (pl.ds(args[0] * rows, rows), slice(None))) for what, *args in order if what == "a"])
    meet([line[1], line[2], line[3], core, far, across, col])
    own_columns = pl.ds(pl.multiple_of(col_id * half, half), half)
    other_columns = pl.ds(pl.multiple_of((1 - col_id) * half, half), half)

    def rows_to_lanes(one, two):
        lane = lax.broadcasted_iota(jnp.int32, (rows, 128), 1)
        return jnp.where(lane == 0, one, jnp.where(lane == 1, two, 0.0)).T[0:8]

    def lanes_to_rows(value):
        return jnp.concatenate([value, jnp.zeros((120, rows), f32)], axis=0).T

    tail = {}

    def stats_start():
        wide = tok[...].astype(f32)
        stat_s[...] = rows_to_lanes(jnp.sum(wide, axis=1, keepdims=True), jnp.sum(wide * wide, axis=1, keepdims=True))
        tail["stat"] = send(stat_s, stat_r, col)

    def stats_end():
        tail["stat"].wait_recv()
        both = lanes_to_rows((stat_s[...] + stat_r[...]) / width)
        mean = both[:, 0:1]
        inv = lax.rsqrt(both[:, 1:2] - mean * mean + eps_norm)
        lane = lax.broadcasted_iota(jnp.int32, (rows, 128), 1)
        stat_own[...] = jnp.where(lane == 0, mean, inv)

    def fold(rows_of):
        step = half // 8
        return jnp.concatenate([jnp.concatenate([row[:, i * step:(i + 1) * step] for i in range(8)]) for row in rows_of], axis=1)

    def unfold(value, i):
        step = half // 8
        return jnp.concatenate([value[j:j + 1, i * step:(i + 1) * step] for j in range(8)], axis=1)

    def early_one():
        total = jnp.concatenate([jnp.sum(ref[...].astype(f32), axis=0, keepdims=True) for ref in (dq_v, du_v)], axis=1)
        blocks = [total[:, k * part:(k + 1) * part] for k in range(7)]
        bias_s[...] = jnp.concatenate(blocks + [jnp.zeros((1, part), f32)])
        tail["bias"] = [send(bias_s, bias_r, col)]
        out_s[...] = fold([jnp.sum(cot[...].astype(f32), axis=0, keepdims=True)])
        tail["out"] = [send(out_s, out_r.at[i], peer) for i, peer in enumerate(row_peers)]

    def early_two():
        for copy in tail["bias"] + tail["out"]:
            copy.wait_recv()
        bias_v[line_id, row_id] = bias_s[...] + bias_r[...]
        mine = bias_v.at[line_id, row_id]
        tail["bias"] = [send(mine, mine, peer) for peer in row_peers]
        out_mid[...] = (out_s[...] + out_r[0]) + (out_r[1] + out_r[2])
        tail["out"] = [send(out_mid, out_r.at[3 + i], line[1 + i]) for i in range(3)]

    def early_three():
        for copy in tail["bias"] + tail["out"]:
            copy.wait_recv()
        tail["bias"] = [send(bias_v.at[line_id], bias_v.at[line_id], line[1 + i]) for i in range(3)]
        out_end[...] = (out_mid[...] + out_r[3]) + (out_r[4] + out_r[5])
        tail["out"] = [send(out_end, out_r.at[6], col)]

    def early_four():
        for copy in tail["bias"] + tail["out"]:
            copy.wait_recv()
        for columns_of, value in ((own_columns, out_end[...]), (other_columns, out_r[6])):
            vec_out[9:10, columns_of] = unfold(value, 0)
            vec_out[10:11, columns_of] = unfold(value, 0)
        for r in range(4):
            for z in range(LINE):
                vec_out[2:9, (r * LINE + z) * part:(r * LINE + z + 1) * part] = bias_v[z, r, 0:7, :]

    def vectors_end():
        gain = vec_ref[0:1, own_columns]
        cuts = [pl.ds(i * 64, 64) for i in range(rows // 64)]
        sums, crosses = [], []
        totals = [jnp.zeros((1, half), f32) for _ in range(2)]
        for at in cuts:
            centred = (tok[at, :].astype(f32) - stat_own[at, 0:1]) * stat_own[at, 1:2]
            grad = dn_s[at, :]
            hat = grad * gain
            sums.append(jnp.sum(hat, axis=1, keepdims=True))
            crosses.append(jnp.sum(hat * centred, axis=1, keepdims=True))
            totals[0] += jnp.sum(grad * centred, axis=0, keepdims=True)
            totals[1] += jnp.sum(grad, axis=0, keepdims=True)
        row_s[...] = fold(totals)
        row_copies = [send(row_s, row_r.at[i], peer) for i, peer in enumerate(row_peers)]
        hat_s[...] = rows_to_lanes(jnp.concatenate(sums), jnp.concatenate(crosses))
        hat_copy = send(hat_s, hat_r, col)
        for copy in row_copies:
            copy.wait_recv()
        mid_s[...] = (row_s[...] + row_r[0]) + (row_r[1] + row_r[2])
        mid_copies = [send(mid_s, mid_r.at[i], line[1 + i]) for i in range(3)]
        hat_copy.wait_recv()
        both = lanes_to_rows((hat_s[...] + hat_r[...]) / width)
        for at, first in zip(cuts, range(0, rows, 64)):
            centred = (tok[at, :].astype(f32) - stat_own[at, 0:1]) * stat_own[at, 1:2]
            mine = both[first:first + 64]
            hat = dn_s[at, :] * gain
            grad_out[at, :] = stat_own[at, 1:2] * (hat - mine[:, 0:1] - centred * mine[:, 1:2]) + cot[at, :].astype(f32)
        for copy in mid_copies:
            copy.wait_recv()
        end_s[...] = (mid_s[...] + mid_r[0]) + (mid_r[1] + mid_r[2])
        end_copy = send(end_s, end_r, col)
        end_copy.wait_recv()
        for columns_of, value in ((own_columns, end_s[...]), (other_columns, end_r[...])):
            for i in range(2):
                vec_out[i:i + 1, columns_of] = unfold(value, i)


    def product(lhs, at):
        return mm(lhs(a_v), d_v[0:part, at]) + mm(lhs(h_v), d_v[part:, at])

    def product_back(lhs, at):
        return mm_t(lhs(dq_v), wq_v[at, :]) + mm_t(lhs(du_v), wu_v[at, :])

    first = Stream(sender, tier_count, rows, half, product, part_s, near_r, far_r, line_s.at[0], line_r.at[0], dn_s, free_core, free_far)
    second = Stream(sender, tier_count, rows, half, product_back, part_s, near_r, far_r, line_s.at[1], line_r.at[1], dn_s,
                    free_core, free_far, first)
    qkv_grad = InGrad(sender, tier_count, taker, dq_v, gin_out.at[:, :, pl.ds(0, 3 * part)], gq_s, gq_r)
    up_grad = InGrad(sender, tier_count, taker, du_v, gin_out.at[:, :, pl.ds(3 * part, 4 * part)], gu_s, gu_r)

    def back_block(i):
        sender.need(2)
        back, slopes = b_rows.take(), s_rows.take()
        at = pl.ds(i * rows, rows)
        da_v[at, :] = mm_t(back[...], d_v[0:part, :]).astype(bf16)
        du_v[at, :] = (mm_t(back[...], d_v[part:, :]) * slopes[...]).astype(bf16)

    quarters = [row_id, row_id + 1 - 2 * (row_id % 2), (row_id + 2) % 4, 3 - row_id]
    lane = lax.broadcasted_iota(jnp.int32, (rows, part), 1)

    def attend_back(p, i):
        sender.need(3, 4, 5)
        if i == 0:
            dk_s[...] = jnp.zeros_like(dk_s)
            dv_s[...] = jnp.zeros_like(dv_s)
        whole = pl.ds(p * slots, slots)
        at = pl.ds(p * slots + i * rows, rows)
        key_place = jnp.concatenate([quarters[t] * rows + lax.broadcasted_iota(jnp.int32, (1, rows), 1) for t in range(4)], axis=1)
        place = quarters[i] * rows + lax.broadcasted_iota(jnp.int32, (rows, 1), 0)
        allowed = (key_place >= stat_v[at, part - 1:part].astype(jnp.int32)) & (key_place <= place)
        queries, d_attn = qkv_v[at, 0:part], da_v[at, :]
        keys, values = qkv_v[whole, part:2 * part], qkv_v[whole, 2 * part:]
        d_q = jnp.zeros((rows, part), f32)
        for h in range(part // HDIM):
            head = (lane >= h * HDIM) & (lane < (h + 1) * HDIM)
            q_h = jnp.where(head, queries, jnp.zeros_like(queries))
            da_h = jnp.where(head, d_attn, jnp.zeros_like(d_attn))
            scores = jnp.where(allowed, mm_t(q_h, keys) * scale, -1e30)
            probs = jnp.exp(scores - stat_v[at, h:h + 1])
            low = probs.astype(bf16)
            d_probs = mm_t(da_h, values)
            delta = jnp.sum(probs * d_probs, axis=-1, keepdims=True)
            d_scores = (probs * (d_probs - delta)).astype(bf16)
            d_q = jnp.where(head, mm(d_scores, keys), d_q)
            dk_s[...] += t_mm(q_h, d_scores)
            dv_s[...] += t_mm(da_h, low)
        dq_v[at, 0:part] = turn(d_q * scale, turn_v[at, :], -1.0).astype(bf16)
        if i == 3:
            dq_v[whole, part:2 * part] = turn(dk_s[...].T * scale, turn_v[whole, :], -1.0).astype(bf16)
            dq_v[whole, 2 * part:] = dv_s[...].T.astype(bf16)

    d_near = {}

    def out_other(j):
        sender.need(0, 1)
        if not d_near:
            at_v[0:part, :] = a_v[...].T
            at_v[part:, :] = h_v[...].T
        do_s[j] = mm(at_v[...], taker.take()[...]).astype(bf16)
        d_near[j] = send(do_s.at[j], do_r.at[j], col)

    d_done = []

    def out_mine(j):
        if len(d_done) > 1:
            sender.need(d_done[-2])
        value = mm(at_v[...], taker.take()[...])
        d_near[j].wait_recv()
        staged = dm_s.at[len(d_done) % 2]
        staged[...] = value + do_r[j].astype(f32)
        d_done.append(sender.load(staged, gd_out.at[:, pl.ds(j * block, block)]))

    actions = {"a": back_block, "b": attend_back, "qo": qkv_grad.other, "qm": qkv_grad.mine, "uo": up_grad.other, "um": up_grad.mine,
               "do": out_other, "dm": out_mine, "s": stats_start, "S": stats_end, "e1": early_one, "e2": early_two, "e3": early_three,
               "e4": early_four, "v": vectors_end}
    for what, *args in order:
        if what in actions:
            actions[what](*args)
            continue
        which, args = args[0], args[1:]
        if what == "c":
            sender.need(*((6, 7) if which else (0, 1, 2)))
        (second if which else first).run(what, args)
        if what == "f" and not which:
            at = first.cut(args[0])
            bias = vec_ref[9:10, own_columns] + vec_ref[10:11, own_columns]
            block_out[at, :] = (tok[at, :].astype(f32) + dn_s[at, :] + bias).astype(bf16)
    qkv_grad.wait()
    up_grad.wait()
    sender.wait_all()


BACKWARD_ORDER = [
    ("c", 0, 1, 1), ("do", 1), ("x", 0, 1, 1), ("a", 0), ("c", 0, 1, 0), ("do", 0), ("a", 4), ("a", 6), ("a", 1), ("a", 7), ("x", 0, 1, 0),
    ("c", 0, 0, 0), ("y", 0, 1, 1), ("a", 2), ("b", 0, 0), ("c", 0, 0, 1), ("b", 0, 1), ("z", 0, 1, 1), ("a", 3), ("y", 0, 1, 0),
    ("x", 0, 0, 0), ("b", 0, 2), ("a", 5), ("uo", 3), ("x", 0, 0, 1), ("uo", 1), ("b", 0, 3), ("z", 0, 1, 0), ("b", 1, 0), ("b", 1, 1),
    ("b", 1, 2), ("b", 1, 3), ("um", 1), ("qo", 3), ("s",), ("r", 0, 1), ("qo", 1), ("c", 1, 1, 1), ("S",), ("um", 3), ("y", 0, 0, 0),
    ("x", 1, 1, 1), ("qo", 0), ("e1",), ("qm", 3), ("c", 1, 1, 0), ("qm", 1), ("e2",), ("x", 1, 1, 0), ("y", 0, 0, 1), ("z", 0, 0, 0),
    ("y", 1, 1, 1), ("z", 0, 0, 1), ("qo", 2), ("c", 1, 0, 1), ("dm", 1), ("y", 1, 1, 0), ("x", 1, 0, 1), ("r", 0, 0), ("e3",), ("dm", 0),
    ("z", 1, 1, 1), ("c", 1, 0, 0), ("do", 2), ("x", 1, 0, 0), ("uo", 0), ("z", 1, 1, 0), ("y", 1, 0, 1), ("f", 0, 0), ("um", 0), ("e4",),
    ("y", 1, 0, 0), ("z", 1, 0, 1), ("dm", 2), ("r", 1, 1), ("z", 1, 0, 0), ("f", 0, 1), ("uo", 2), ("qm", 0), ("f", 1, 1), ("r", 1, 0),
    ("do", 3), ("qm", 2), ("f", 1, 0), ("um", 2), ("v",), ("dm", 3),
]


def backward(tier_count, attn, hidden, slope, qkv, turns, stat, normed, back, out_mat, qkv_mat, up_mat, tok, cot, vectors, order=None):
    rows, half = tok.shape
    width = 2 * half
    chunk = rows // CH
    all_rows, part = attn.shape
    block = half // 4
    sds = jax.ShapeDtypeStruct
    any_ = pl.BlockSpec(memory_space=pl.ANY)
    vmem = pl.BlockSpec(memory_space=pltpu.VMEM)

    def buf(*shape, kind=bf16):
        return pltpu.VMEM(shape, kind)

    dma = pltpu.SemaphoreType.DMA
    regular = pltpu.SemaphoreType.REGULAR
    return pl.pallas_call(
        functools.partial(backward_kernel, tier_count, order or BACKWARD_ORDER),
        out_shape=[sds((rows, half), bf16), sds((rows, half), f32), sds((LINE, block, 7 * part), bf16), sds((5 * part, half), f32), sds((11, width), f32)],
        in_specs=[any_] * 11 + [vmem] * 3,
        out_specs=[vmem, vmem, any_, any_, vmem],
        scratch_shapes=[
            buf(all_rows, part), buf(all_rows, 4 * part), buf(5 * part, width), buf(5 * part, all_rows),
            buf(all_rows, 3 * part), buf(all_rows, 2 * part, kind=f32), buf(all_rows, part, kind=f32), buf(width, 3 * part), buf(width, 4 * part),
            buf(all_rows, part), buf(all_rows, 3 * part), buf(all_rows, 4 * part), buf(part, 4 * rows, kind=f32), buf(part, 4 * rows, kind=f32),
            buf(2, all_rows, block), buf(2, rows, width), buf(2, rows, 4 * part, kind=f32),
            buf(2 * CH, 4, chunk, width), buf(2 * CH, 2, chunk, width), buf(2 * CH, chunk, width),
            buf(2, 4, rows, half), buf(2, 4, rows, half), buf(rows, half, kind=f32),
            buf(4, block, 3 * part), buf(4, block, 3 * part), buf(4, block, 4 * part), buf(4, block, 4 * part),
            buf(4, 5 * part, block), buf(4, 5 * part, block), buf(2, 5 * part, block, kind=f32),
            buf(8, rows, kind=f32), buf(8, rows, kind=f32), buf(rows, 128, kind=f32), buf(8, rows, kind=f32), buf(8, rows, kind=f32),
            buf(8, half // 4, kind=f32), buf(3, 8, half // 4, kind=f32), buf(8, half // 4, kind=f32), buf(3, 8, half // 4, kind=f32),
            buf(8, half // 4, kind=f32), buf(8, half // 4, kind=f32),
            buf(8, half // 8, kind=f32), buf(7, 8, half // 8, kind=f32), buf(8, half // 8, kind=f32), buf(8, half // 8, kind=f32),
            buf(8, part, kind=f32), buf(8, part, kind=f32), buf(LINE, 4, 8, part, kind=f32),
            dma((128,)), dma((128,)), dma((24,)), regular((2 * CH,)), regular((2 * CH,)), dma((2,)), dma((2,)), dma((2,)),
        ],
        compiler_params=pltpu.CompilerParams(collective_id=2, has_side_effects=True, vmem_limit_bytes=63 << 20),
    )(attn, hidden, slope, qkv, turns, stat, normed, back, out_mat, qkv_mat, up_mat, tok, cot, vectors)


def adamw_fast(weight, first_moment, second_moment, gradient, rate):
    first_next = 0.9 * first_moment + 0.1 * gradient
    second_next = 0.95 * second_moment + 0.05 * gradient * gradient
    scaled = second_next * (1.0 / (1.0 - 0.95**STEP))
    root = scaled * lax.rsqrt(scaled) + 1e-08
    update = first_next * (rate / (1.0 - 0.9**STEP)) / root
    return first_next, second_next, (1.0 - 0.1 * rate) * weight - update


def step_kernel(rates, gin_ref, gout_ref, *refs):
    ins, outs = refs[:12], refs[12:]
    pieces = gin_ref.shape[0]
    part = gin_ref.shape[2] // 7

    def one(i, at, grad):
        values = adamw_fast(*[ref[at] for ref in ins[3 * i:3 * i + 3]], grad, rates[i])
        for ref, value in zip(outs[3 * i:3 * i + 3], values):
            ref[at] = value

    for z in range(pieces):
        at = pl.ds(z * part, part)
        for k in range(3):
            one(0, (k, slice(None), at), gin_ref[z, :, pl.ds(k * part, part)].astype(f32))
        for k in range(4):
            one(1, (slice(None), k, at), gin_ref[z, :, pl.ds((3 + k) * part, part)].astype(f32))
    one(2, (slice(None), slice(None)), gout_ref[0])
    for k in range(4):
        one(3, (slice(None), k, slice(None)), gout_ref[1 + k])


def step_all(grad_in, grad_out, qkv, up, dense, down):
    steps = 8
    rates = (D ** (-0.5), D ** (-0.5), max(D // 128, 4) ** (-0.5), FF ** (-0.5))

    def spec(shape, axis):
        block = tuple(size // steps if i == axis else size for i, size in enumerate(shape))
        return pl.BlockSpec(block, lambda i: tuple(i if a == axis else 0 for a in range(len(shape))))

    arrays = [*qkv, *up, *dense, *down]
    axes = [1] * 3 + [0] * 9
    specs = [spec(value.shape, axis) for value, axis in zip(arrays, axes)]
    out = pl.pallas_call(
        functools.partial(step_kernel, rates),
        grid=(steps,),
        out_shape=[jax.ShapeDtypeStruct(value.shape, f32) for value in arrays],
        in_specs=[spec(grad_in.shape, 1), spec(grad_out.shape, 1)] + specs,
        out_specs=specs,
        compiler_params=pltpu.CompilerParams(vmem_limit_bytes=62 << 20),
    )(grad_in, grad_out, *arrays)
    return [out[i:i + 3] for i in range(0, 12, 3)]


def per_device(
    tokens,
    cotangent,
    doc_lengths,
    doc_groups,
    w_qkv,
    w_up,
    w_dense,
    w_down,
    vectors,
    m_qkv,
    v_qkv,
    m_up,
    v_up,
    m_dense,
    v_dense,
    m_down,
    v_down,
    m_vec,
    v_vec,
):
    dp_count = lax.axis_size("dp")
    tier_count = dp_count // LINE
    row_count = lax.axis_size("row")
    col_count = lax.axis_size("col")
    assert row_count == 4 and col_count == 2 and dp_count % LINE == 0
    tok_dev, half_width = tokens.shape
    slot_count = tok_dev * row_count
    full_width = half_width * col_count
    row_width = full_width // row_count
    part = row_width // LINE
    tier_groups = [[line * tier_count + tier for tier in range(tier_count)] for line in range(LINE)]


    def tier_gather(value):
        if tier_count > 1:
            value = lax.all_gather(value, "dp", axis=0, tiled=True, axis_index_groups=tier_groups)
        return value

    if tier_count > 1:
        full_qkv, full_up, full_dense, full_down = [
            tier_gather(weight.astype(bf16)).astype(f32) for weight in (w_qkv, w_up, w_dense, w_down)
        ]
    else:
        full_qkv, full_up, full_dense, full_down = w_qkv, w_up, w_dense, w_down
    normed, back, qkv_mat, up_mat, out_mat, back_own, *fresh = gather(
        tier_count,
        doc_lengths,
        doc_groups,
        tokens,
        cotangent,
        vectors,
        full_qkv.transpose(1, 0, 2),
        full_up,
        full_dense,
        full_down,
    )
    rows_all = 2 * slot_count
    normed = normed.reshape(rows_all, full_width)
    back = back.reshape(rows_all, full_width)
    qkv_mat = qkv_mat.reshape(full_width, 3 * part)
    up_mat = up_mat.reshape(full_width, 4 * part)

    fresh = [value.reshape(rows_all, value.shape[-1]) for value in fresh]
    block_out, grad_tokens, grad_in, grad_out, vec_grad = backward(
        tier_count, *fresh, normed, back, out_mat, qkv_mat, up_mat, tokens, back_own, vectors
    )

    def tier_sum(value):
        if tier_count > 1:
            value = lax.psum_scatter(
                value, "dp", scatter_dimension=0, tiled=True, axis_index_groups=tier_groups
            )
        return value

    def own_columns(value, parts):
        value = value.astype(f32).reshape(LINE, half_width // LINE, parts, part)
        return tier_sum(value.transpose(1, 2, 0, 3).reshape(half_width // LINE, parts, row_width))

    if tier_count > 1:
        vec_grad = lax.psum(vec_grad, "dp", axis_index_groups=tier_groups)
        red_qkv = own_columns(grad_in[:, :, : 3 * part], 3)
        red_up = own_columns(grad_in[:, :, 3 * part :], 4)
        red_dense = tier_sum(grad_out[:part])
        red_down = tier_sum(grad_out[part:].reshape(4, part, half_width).transpose(1, 0, 2))
        qkv_new = adamw(w_qkv, m_qkv, v_qkv, red_qkv, D ** (-0.5), 0.1)
        up_new = adamw(w_up, m_up, v_up, red_up, D ** (-0.5), 0.1)
        dense_new = adamw(w_dense, m_dense, v_dense, red_dense, max(D // 128, 4) ** (-0.5), 0.1)
        down_new = adamw(w_down, m_down, v_down, red_down, FF ** (-0.5), 0.1)
    else:
        qkv_new, up_new, dense_new, down_new = step_all(
            grad_in,
            grad_out.reshape(5, part, half_width),
            [value.transpose(1, 0, 2) for value in (w_qkv, m_qkv, v_qkv)],
            (w_up, m_up, v_up),
            (w_dense, m_dense, v_dense),
            (w_down, m_down, v_down),
        )
        qkv_new = [value.transpose(1, 0, 2) for value in qkv_new]
    vec_new = adamw(vectors, m_vec, v_vec, vec_grad, 0.5, 0.0)
    return (
        block_out,
        grad_tokens,
        qkv_new[0],
        qkv_new[1],
        qkv_new[2],
        up_new[0],
        up_new[1],
        up_new[2],
        dense_new[0],
        dense_new[1],
        dense_new[2],
        down_new[0],
        down_new[1],
        down_new[2],
        vec_new[0],
        vec_new[1],
        vec_new[2],
    )


def solution(mesh):
    placed = (
        P(("dp", "row"), "col"),
        P(("dp", "row"), "col"),
        P(),
        P(),
        P(("col", "dp"), None, "row"),
        P(("col", "dp"), None, "row"),
        P(("row", "dp"), "col"),
        P(("row", "dp"), None, "col"),
        P(),
        P(("col", "dp"), None, "row"),
        P(("col", "dp"), None, "row"),
        P(("col", "dp"), None, "row"),
        P(("col", "dp"), None, "row"),
        P(("row", "dp"), "col"),
        P(("row", "dp"), "col"),
        P(("row", "dp"), None, "col"),
        P(("row", "dp"), None, "col"),
        P(),
        P(),
    )
    return jax.shard_map(
        per_device,
        mesh=mesh,
        in_specs=placed,
        out_specs=(
            P(("dp", "row"), "col"),
            P(("dp", "row"), "col"),
            P(("col", "dp"), None, "row"),
            P(("col", "dp"), None, "row"),
            P(("col", "dp"), None, "row"),
            P(("col", "dp"), None, "row"),
            P(("col", "dp"), None, "row"),
            P(("col", "dp"), None, "row"),
            P(("row", "dp"), "col"),
            P(("row", "dp"), "col"),
            P(("row", "dp"), "col"),
            P(("row", "dp"), None, "col"),
            P(("row", "dp"), None, "col"),
            P(("row", "dp"), None, "col"),
            P(),
            P(),
            P(),
        ),
        check_vma=False,
    )
```

```python
import functools

import jax
import jax.numpy as jnp
from jax import lax
from jax.experimental import pallas as pl
from jax.experimental.pallas import tpu as pltpu
from jax.sharding import PartitionSpec as P

D = 2048
HDIM = 64
ROT = 32
FF = 8192
BLK = 512
STEP = 10
LINE = 4


eps_norm = 1e-05
f32 = jnp.float32
bf16 = jnp.bfloat16


def adamw(weight, first_moment, second_moment, gradient, rate, decay):
    first_next = 0.9 * first_moment + 0.1 * gradient
    second_next = 0.95 * second_moment + 0.05 * gradient * gradient
    correct_one = 1.0 - 0.9**STEP
    correct_two = 1.0 - 0.95**STEP
    update = first_next / correct_one / (jnp.sqrt(second_next / correct_two) + 1e-08)
    return (first_next, second_next, weight - rate * (update + decay * weight))


def mm(a, b):
    return jnp.dot(a, b, preferred_element_type=f32)


def mm_t(a, b):
    return lax.dot_general(a, b, (((1,), (1,)), ((), ())), preferred_element_type=f32)


def t_mm(a, b):
    return lax.dot_general(a, b, (((0,), (0,)), ((), ())), preferred_element_type=f32)


def gelu_both(v):
    root = 0.7978845608028654
    square = v * v
    slope = root * (1.0 + 3 * 0.044715 * square)
    tanh = jnp.tanh(root * v * (1.0 + 0.044715 * square))
    outer = 0.5 * (1.0 + tanh)
    return v * outer, outer + 0.5 * v * (1.0 - tanh * tanh) * slope


def turn(value, turns, sign):
    part = value.shape[1]
    quarter = ROT // 2
    lead = lax.broadcasted_iota(jnp.int32, (1, part), 1) % HDIM < quarter
    other = jnp.where(lead, jnp.roll(value, -quarter, axis=1), jnp.roll(value, quarter, axis=1))
    return value * turns[:, 0:part] + sign * (other * turns[:, part:])


class Forward:
    def __init__(self, tier_count, lengths, groups, x_ref, wq_ref, wu_ref, vec_ref, attn_ref, hidden_ref, slope_ref, qkv_ref, turn_ref, stat_ref):
        self.tier_count, self.lengths, self.groups = tier_count, lengths, groups
        self.x_ref, self.wq_ref, self.wu_ref = x_ref, wq_ref, wu_ref
        self.attn_ref, self.hidden_ref, self.slope_ref = attn_ref, hidden_ref, slope_ref
        self.qkv_ref, self.turn_ref, self.stat_ref = qkv_ref, turn_ref, stat_ref
        slots, part = attn_ref.shape
        self.slots, self.part, self.rows = slots, part, slots // 4
        row_id = lax.axis_index("row")
        self.quarters = [row_id, row_id + 1 - 2 * (row_id % 2), (row_id + 2) % 4, 3 - row_id]
        self.line_id = lax.axis_index("dp") // tier_count
        bias_at = pl.ds(pl.multiple_of((row_id * LINE + self.line_id) * part, part), part)
        self.bias = jnp.concatenate([vec_ref[k:k + 1, bias_at] for k in range(2, 9)], axis=1)
        self.key_place = jnp.concatenate(
            [self.quarters[t] * self.rows + lax.broadcasted_iota(jnp.int32, (1, self.rows), 1) for t in range(4)], axis=1)

    def cut(self, i):
        return pl.ds(i * self.rows, self.rows)

    def angles(self, p):
        lengths, groups, part, rows, quarters = self.lengths, self.groups, self.part, self.rows, self.quarters
        line_id, tier_id = self.line_id, lax.axis_index("dp") % self.tier_count
        turn_ref, stat_ref = self.turn_ref, self.stat_ref
        quarter = ROT // 2
        bit = (line_id % 2 + lax.axis_index("col")) % 2
        group = line_id + bit * (1 - 2 * (line_id % 2))
        group = ((group + 2 * p) % 4) * self.tier_count + tier_id
        lanes = lax.broadcasted_iota(jnp.int32, (1, part), 1) % HDIM
        lead = lanes < quarter
        powers = (lanes % quarter).astype(f32) * (-2.0 / ROT)
        speed = jnp.where(lanes < ROT, jnp.exp(powers * 9.210340371976184), 0.0)
        fine = lax.broadcasted_iota(jnp.int32, (32, part), 0).astype(f32) * speed
        fine_cos, fine_sin = jnp.cos(fine), jnp.sin(fine)
        count = lengths.shape[0] + 1
        starts, start = [], jnp.int32(0)
        for i in range(count - 1):
            here = groups[i] == group
            starts.append(jnp.where(here, start, 1 << 30))
            start = start + jnp.where(here, lengths[i], 0)
        starts.append(start)
        which = lax.broadcasted_iota(jnp.int32, (-(-count // 8) * 8, part), 0)
        start_angle = jnp.zeros(which.shape, f32)
        for i in range(count):
            start_angle = jnp.where(which == i, jnp.where(starts[i] < (1 << 30), starts[i], 0).astype(f32), start_angle)
        start_angle = start_angle * speed
        start_cos, start_sin = jnp.cos(start_angle), jnp.sin(start_angle)
        steps = rows // 32
        for t in range(4):
            base = quarters[t] * rows
            coarse = (base + 32 * lax.broadcasted_iota(jnp.int32, (steps, part), 0)).astype(f32) * speed
            coarse_cos, coarse_sin = jnp.cos(coarse), jnp.sin(coarse)
            for j in range(2):
                some = range(j * steps // 2, (j + 1) * steps // 2)
                size = rows // 2
                place_cos = jnp.concatenate([coarse_cos[i:i + 1] * fine_cos - coarse_sin[i:i + 1] * fine_sin for i in some])
                place_sin = jnp.concatenate([coarse_sin[i:i + 1] * fine_cos + coarse_cos[i:i + 1] * fine_sin for i in some])
                place = base + j * size + lax.broadcasted_iota(jnp.int32, (size, part), 0)
                first = jnp.zeros((size, part), jnp.int32)
                first_cos = jnp.ones((size, part), f32)
                first_sin = jnp.zeros((size, part), f32)
                for i in range(count):
                    after = place >= starts[i]
                    first = jnp.where(after, starts[i], first)
                    first_cos = jnp.where(after, start_cos[i:i + 1], first_cos)
                    first_sin = jnp.where(after, start_sin[i:i + 1], first_sin)
                at = pl.ds(t * rows + j * size, size)
                turn_ref[at, 0:part] = place_cos * first_cos + place_sin * first_sin
                sin = place_sin * first_cos - place_cos * first_sin
                turn_ref[at, part:] = jnp.where(lead, -sin, sin)
                lane = lax.broadcasted_iota(jnp.int32, (size, part), 1)
                stat_ref[at, :] = jnp.where(lane == part - 1, first.astype(f32), 0.0)

    def project(self, i):
        part, at = self.part, self.cut(i)
        pre = mm(self.x_ref[at, :], self.wq_ref[...]) + self.bias[:, 0:3 * part]
        turns = self.turn_ref[at, :]
        self.qkv_ref[at, 0:part] = turn(pre[:, 0:part], turns, 1.0).astype(bf16)
        self.qkv_ref[at, part:2 * part] = turn(pre[:, part:2 * part], turns, 1.0).astype(bf16)
        self.qkv_ref[at, 2 * part:] = pre[:, 2 * part:].astype(bf16)

    def up(self, i):
        at = self.cut(i)
        value, slope = gelu_both(mm(self.x_ref[at, :], self.wu_ref[...]) + self.bias[:, 3 * self.part:])
        self.hidden_ref[at, :] = value.astype(bf16)
        self.slope_ref[at, :] = slope

    def attend(self, i):
        part, at, rows = self.part, self.cut(i), self.rows
        lane = lax.broadcasted_iota(jnp.int32, (rows, part), 1)
        keys, values = self.qkv_ref[:, part:2 * part], self.qkv_ref[:, 2 * part:]
        stat = self.stat_ref[at, :]
        place = self.quarters[i] * rows + lax.broadcasted_iota(jnp.int32, (rows, 1), 0)
        allowed = (self.key_place >= stat[:, part - 1:part].astype(jnp.int32)) & (self.key_place <= place)
        queries = self.qkv_ref[at, 0:part]
        out = jnp.zeros((rows, part), f32)
        for h in range(part // HDIM):
            head = (lane >= h * HDIM) & (lane < (h + 1) * HDIM)
            q_h = jnp.where(head, queries, jnp.zeros_like(queries))
            scores = jnp.where(allowed, mm_t(q_h, keys) * HDIM ** (-0.5), -1e30)
            top = jnp.max(scores, axis=-1, keepdims=True)
            weights = jnp.exp(scores - top)
            total = jnp.sum(weights, axis=-1, keepdims=True)
            low = (weights * (1.0 / total)).astype(bf16)
            out = jnp.where(head, mm(low, values), out)
            stat = jnp.where(lane == h, top + jnp.log(total), stat)
        self.attn_ref[at, :] = out.astype(bf16)
        self.stat_ref[at, :] = stat


class Copies:
    def __init__(self, send_sems, recv_sems):
        self.send_sems, self.recv_sems, self.sent, self.received = send_sems, recv_sems, 0, 0

    def slot(self):
        self.received += 1
        return self.received - 1

    def make(self, src, dst, device, slot=None):
        slot = self.slot() if slot is None else slot
        self.sent += 1
        return pltpu.make_async_remote_copy(
            src_ref=src, dst_ref=dst, send_sem=self.send_sems.at[self.sent - 1], recv_sem=self.recv_sems.at[slot],
            device_id=device, device_id_type=pl.DeviceIdType.MESH)

def neighbours(tier_count):
    dp_id, row_id, col_id = lax.axis_index("dp"), lax.axis_index("row"), lax.axis_index("col")
    line_id, tier_id = dp_id // tier_count, dp_id % tier_count
    flips = [line_id, line_id + 1 - 2 * (line_id % 2), (line_id + 2) % 4, 3 - line_id]
    line = [(flip * tier_count + tier_id, row_id, col_id) for flip in flips]
    core = (dp_id, row_id + 1 - 2 * (row_id % 2), col_id)
    far = (dp_id, (row_id + 2) % 4, col_id)
    col = (dp_id, row_id, 1 - col_id)
    return line_id, flips, line, core, far, col

def meet(peers):
    barrier = pltpu.get_barrier_semaphore()
    for peer in peers:
        pl.semaphore_signal(barrier, inc=1, device_id=peer, device_id_type=pl.DeviceIdType.MESH)
    pl.semaphore_wait(barrier, len(peers))


CH = 2
DEPTH = 2

def gather_kernel(tier_count, order, lengths, groups, tok, cot, vec_ref, w_qkv, w_up, w_dense, w_down,
                  x_out, b_out, wq_out, wu_out, d_out, cot_s, attn_out, hidden_out, slope_out, qkv_out, turn_out, stat_out,
                  x_v, wq_v, wu_v, attn_v, hidden_v, slope_v, qkv_v, turn_v, stat_v, tz, cz, ty, xs, qkv_f, up_f, dense_f, down_f, wq, wu, dh,
                  send_sems, recv_sems, local_sems, load_sems, into_sems, out_sems):
    line_id, flips, line, core, far, col = neighbours(tier_count)
    bit = (line_id % 2 + lax.axis_index("col")) % 2
    middle = (line_id == 1) | (line_id == 2)
    rows, half = tok.shape
    chunk = rows // CH
    copies = Copies(send_sems, recv_sems)
    sent, mid_sent, local_left, last = [], [], [], []
    n_local = [0]

    def local(src, dst):
        copy = pltpu.make_async_copy(src, dst, local_sems.at[n_local[0]])
        n_local[0] += 1
        copy.start()
        local_left.append(copy)
        return copy

    def settle(copy):
        if any(c is copy for c in local_left):
            copy.wait()
            local_left[:] = [c for c in local_left if c is not copy]

    def arrive(copy):
        if any(c is copy for c in last):
            copy.wait_recv()
            last[:] = [c for c in last if c is not copy]

    def send(src, dst, device, slot=None):
        copy = copies.make(src, dst, device, slot)
        copy.start()
        sent.append(copy)
        return copy

    def cut(c):
        return pl.ds(c * chunk, chunk)

    class Stream:
        def __init__(self, own, stage, out, normed):
            self.own, self.stage, self.out, self.normed = own, stage, out, normed
            self.line, self.swap, self.spread, self.keep, self.whole = {}, {}, {}, {}, ([], [])

        def start(self, c):
            own, stage = self.own.at[cut(c)], self.stage
            own_copy = local(own, stage.at[0, cut(c)])
            near = send(own, stage.at[1, cut(c)], line[1])
            two = send(own, stage.at[2, cut(c)], line[2])
            slot = copies.slot()
            three = copies.make(own, stage.at[3, cut(c)], line[3], slot)
            relay = copies.make(stage.at[2, cut(c)], stage.at[3, cut(c)], line[1], slot)
            pl.when(middle)(three.start)
            mid_sent.extend([three, relay])
            self.line[c] = own_copy, near, two, three, relay

        def swap_cols(self, c, p):
            own_copy, near, two, three, relay = self.line[c]
            if p == 0:
                settle(own_copy)
                near.wait_recv()
            else:
                three.wait_recv()
            if self.normed:
                dst = ty.at[p, cut(c)]
            else:
                dst = self.out.at[p, 0, cut(c), pl.ds(half, half)]
                self.keep[c, p] = local(self.stage.at[2 * p + bit, cut(c)], self.out.at[p, 0, cut(c), pl.ds(0, half)])
            self.swap[c, p] = send(self.stage.at[2 * p + 1 - bit, cut(c)], dst, col)

        def pass_on(self, c):
            own_copy, near, two, three, relay = self.line[c]
            two.wait_recv()
            pl.when(middle)(relay.start)

        def give(self, c, p):
            self.swap[c, p].wait_recv()
            if self.normed:
                norm(c, p)
                src = xs.at[p, cut(c)]
                self.whole[p].append((settle, local(src, self.out.at[p, 0, cut(c)])))
            else:
                settle(self.keep[c, p])
                src = self.out.at[p, 0, cut(c)]
            self.spread[c, p] = send(src, self.out.at[p, 2, cut(c)], far)
            last.append(send(src, self.out.at[p, 1, cut(c)], core))
            self.whole[p].append((arrive, last[-1]))

        def relay(self, c, p):
            self.spread[c, p].wait_recv()
            last.append(send(self.out.at[p, 2, cut(c)], self.out.at[p, 3, cut(c)], core))
            self.whole[p].append((arrive, last[-1]))

    norm_ref = [[vec_ref.at[i:i + 1, pl.ds(pl.multiple_of(side * half, half), half)] for i in range(2)]
                for side in (lax.axis_index("col"), 1 - lax.axis_index("col"))]

    def norm(c, p):
        step = 64
        def body(i, carry):
            at = pl.ds(pl.multiple_of(c * chunk + i * step, step), step)
            one = tz[2 * p + bit, at, :].astype(f32)
            two = ty[p, at, :].astype(f32)
            width = 2 * half
            mean = (jnp.sum(one, axis=-1, keepdims=True) + jnp.sum(two, axis=-1, keepdims=True)) / width
            square = (jnp.sum(one * one, axis=-1, keepdims=True) + jnp.sum(two * two, axis=-1, keepdims=True)) / width
            inv = lax.rsqrt(square - mean * mean + eps_norm)
            xs[p, at, pl.ds(0, half)] = ((one - mean) * inv * norm_ref[0][0][...] + norm_ref[0][1][...]).astype(bf16)
            xs[p, at, pl.ds(half, half)] = ((two - mean) * inv * norm_ref[1][0][...] + norm_ref[1][1][...]).astype(bf16)
            return carry
        lax.fori_loop(0, chunk // step, body, 0)

    class Weight:
        def __init__(self, src, out):
            self.src, self.out, self.got, self.whole = src, out, {}, []

        def own(self):
            self.whole.append((settle, local(self.src.at[line_id], self.out.at[0, line_id])))
            last.append(send(self.src.at[line_id], self.out.at[1, line_id], col))
            self.whole.append((arrive, last[-1]))

        def start(self):
            for s in (1, 2, 3):
                self.got[s] = send(self.src.at[flips[s]], self.out.at[0, line_id], line[s])

        def swap(self):
            for s in (1, 2, 3):
                self.got[s].wait_recv()
                last.append(send(self.out.at[0, flips[s]], self.out.at[1, flips[s]], col))
                self.whole.append((arrive, last[-1]))

    part = dh.shape[0] // 5
    loads = []
    for i, (src, dst) in enumerate(((w_qkv, qkv_f), (w_up, up_f), (w_dense, dense_f), (w_down, down_f), (cot, cot_s))):
        loads.append(pltpu.make_async_copy(src, dst, load_sems.at[i]))
        loads[-1].start()

    def prepare(what):
        if what == 0:
            loads[0].wait()
            for j in range(LINE):
                for k in range(3):
                    wq[j, :, k * part:(k + 1) * part] = qkv_f[k, :, j * part:(j + 1) * part].astype(bf16)
        if what == 1:
            loads[1].wait()
            for j in range(LINE):
                for k in range(4):
                    wu[j, :, k * part:(k + 1) * part] = up_f[:, k, j * part:(j + 1) * part].astype(bf16)
        if what == 2:
            loads[2].wait()
            dh[0:part, :] = dense_f[...].astype(bf16)
        if what == 3:
            loads[3].wait()
            for k in range(4):
                dh[(k + 1) * part:(k + 2) * part, :] = down_f[:, k, :].astype(bf16)
        if what == 4:
            loads[4].wait()
            total = jnp.int32(0)
            for i in range(lengths.shape[0]):
                total = total + jnp.where(groups[i] == lax.axis_index("dp"), lengths[i], 0)
            place = lax.axis_index("row") * rows + lax.broadcasted_iota(jnp.int32, (rows, half), 0)
            cot_s[...] = jnp.where(place < total, cot_s[...], jnp.zeros_like(cot_s))

    def dense(i):
        at = pl.ds(i * part, part)
        last.append(send(dh.at[at], d_out.at[at, pl.ds(half, half)], col))

    meet([line[1], line[2], line[3], core, far, col])
    T = Stream(tok, tz, x_out, True)
    C = Stream(cot_s, cz, b_out, False)
    Q = Weight(wq, wq_out)
    U = Weight(wu, wu_out)
    slots = 4 * rows
    wide = [ref.reshape(2 * half, ref.shape[-1]) for ref in (wq_v, wu_v)]
    fresh = (attn_v, hidden_v, slope_v, qkv_v, turn_v, stat_v)
    steps = [Forward(tier_count, lengths, groups, x_v.at[p].reshape(slots, 2 * half), *wide, vec_ref, *[ref.at[p] for ref in fresh])
             for p in range(2)]
    going, stored = {}, []

    def fetch(i, src, dst, whole):
        for wait, copy in whole:
            wait(copy)
        going[i] = pltpu.make_async_copy(src, dst, into_sems.at[i])
        going[i].start()

    def store(p, *pairs):
        for src, dst in pairs:
            stored.append(pltpu.make_async_copy(src.at[p], dst.at[p], out_sems.at[len(stored)]))
            stored[-1].start()

    def need(*which):
        for i in which:
            if i in going:
                going.pop(i).wait()

    for what, *args in order:
        if what == "Wq":
            for j in range(2):
                fetch(j, wq_out.at[j], wq_v.at[j], Q.whole)
        if what == "Wu":
            for j in range(2):
                fetch(2 + j, wu_out.at[j], wu_v.at[j], U.whole)
        if what == "X":
            fetch(4 + args[0], x_out.at[args[0]], x_v.at[args[0]], T.whole[args[0]])
        if what == "Fa":
            steps[args[0]].angles(args[0])
        if what == "Fp":
            need(0, 1, 4 + args[0])
            steps[args[0]].project(args[1])
        if what == "Fs":
            steps[args[0]].attend(args[1])
            if args[1] == 3:
                store(args[0], (attn_v, attn_out), (qkv_v, qkv_out), (turn_v, turn_out), (stat_v, stat_out))
        if what == "Fu":
            need(2, 3, 4 + args[0])
            steps[args[0]].up(args[1])
            if args[1] == 3:
                store(args[0], (hidden_v, hidden_out), (slope_v, slope_out))
        if what == "P": prepare(*args)
        if what == "Ts": T.start(*args)
        if what == "Tr": T.pass_on(*args)
        if what == "Cr": C.pass_on(*args)
        if what == "Ty": T.swap_cols(*args)
        if what == "Tx": T.give(*args)
        if what == "Tk": T.relay(*args)
        if what == "Cs": C.start(*args)
        if what == "Cy": C.swap_cols(*args)
        if what == "Cx": C.give(*args)
        if what == "Ck": C.relay(*args)
        if what == "Qo": Q.own()
        if what == "Qs": Q.start()
        if what == "Qy": Q.swap()
        if what == "Uo": U.own()
        if what == "Us": U.start()
        if what == "Uy": U.swap()
        if what == "D": dense(*args)
        if what == "Dl": local(dh, d_out.at[:, pl.ds(0, half)])
    for copy in list(last):
        arrive(copy)
    for copy in stored:
        copy.wait()
    for copy in list(local_left):
        settle(copy)
    for copy in sent:
        copy.wait_send()
    for copy in mid_sent:
        pl.when(middle)(copy.wait_send)

ORDER_A = [
    ("Ts", 0), ("P", 2), ("D", 0), ("P", 3), ("D", 3), ("Ty", 0, 0), ("P", 4), ("Ts", 1), ("Ty", 1, 0), ("Tx", 0, 0), ("Cs", 0), ("P", 0),
    ("D", 1), ("D", 2), ("Tx", 1, 0), ("Tr", 0), ("Fa", 1), ("Cs", 1), ("Cy", 0, 0), ("Tk", 0, 0), ("P", 1), ("Tr", 1), ("Qo",),
    ("Cy", 1, 0), ("Cr", 0), ("Ty", 0, 1), ("Ty", 1, 1), ("Cx", 1, 0), ("Qs",), ("Cr", 1), ("Dl",), ("Tx", 0, 1), ("Uo",), ("Fa", 0),
    ("Tx", 1, 1), ("Tk", 1, 0), ("Qy",), ("Us",), ("Tk", 0, 1), ("Cy", 0, 1), ("Tk", 1, 1), ("X", 0), ("Cx", 0, 0), ("Wq",), ("Fp", 0, 0),
    ("X", 1), ("Cy", 1, 1), ("Fp", 0, 1), ("Fp", 1, 0), ("Cx", 0, 1), ("Fp", 0, 2), ("Fp", 1, 1), ("Fp", 1, 2), ("Uy",), ("Fp", 1, 3),
    ("Fp", 0, 3), ("Fs", 0, 0), ("Fs", 1, 0), ("Fs", 1, 1), ("Fs", 0, 1), ("Ck", 1, 0), ("Fs", 0, 2), ("Cx", 1, 1), ("Fs", 1, 2),
    ("Ck", 0, 1), ("Fs", 0, 3), ("Fs", 1, 3), ("Ck", 0, 0), ("Wu",), ("D", 4), ("Fu", 1, 0), ("Fu", 0, 0), ("Fu", 0, 1), ("Fu", 0, 2),
    ("Fu", 0, 3), ("Ck", 1, 1), ("Fu", 1, 1), ("Fu", 1, 2), ("Fu", 1, 3),
]


def gather(tier_count, lengths, groups, tok, cot, vectors, w_qkv, w_up, w_dense, w_down, order=None):
    rows, half = tok.shape
    part = w_dense.shape[0]
    c_rows = w_up.shape[0]
    results = ((1, bf16), (4, bf16), (4, f32), (3, bf16), (2, f32), (1, f32))
    sds = jax.ShapeDtypeStruct
    any_ = pl.BlockSpec(memory_space=pl.ANY)
    smem = pl.BlockSpec(memory_space=pltpu.SMEM)
    return pl.pallas_call(
        functools.partial(gather_kernel, tier_count, order or ORDER_A),
        out_shape=[sds((2, 4, rows, 2 * half), bf16), sds((2, 4, rows, 2 * half), bf16),
                   sds((2, LINE, c_rows, 3 * part), bf16), sds((2, LINE, c_rows, 4 * part), bf16), sds((5 * part, 2 * half), bf16), sds(cot.shape, bf16),
                   *[sds((2, 4 * rows, count * part), kind) for count, kind in results]],
        in_specs=[smem, smem, any_, any_, pl.BlockSpec(memory_space=pltpu.VMEM), any_, any_, any_, any_],
        out_specs=[any_] * 5 + [pl.BlockSpec(memory_space=pltpu.VMEM)] + [any_] * 6,
        scratch_shapes=[pltpu.VMEM((2, 4, rows, 2 * half), bf16), pltpu.VMEM((2, LINE, c_rows, 3 * part), bf16), pltpu.VMEM((2, LINE, c_rows, 4 * part), bf16),
                        *[pltpu.VMEM((2, 4 * rows, count * part), kind) for count, kind in results],
                        pltpu.VMEM((4, rows, half), bf16), pltpu.VMEM((4, rows, half), bf16), pltpu.VMEM((2, rows, half), bf16),
                        pltpu.VMEM((2, rows, 2 * half), bf16),
                        pltpu.VMEM(w_qkv.shape, f32), pltpu.VMEM(w_up.shape, f32), pltpu.VMEM(w_dense.shape, f32), pltpu.VMEM(w_down.shape, f32),
                        pltpu.VMEM((LINE, c_rows, 3 * part), bf16), pltpu.VMEM((LINE, c_rows, 4 * part), bf16), pltpu.VMEM((5 * part, half), bf16),
                        pltpu.SemaphoreType.DMA((80,)), pltpu.SemaphoreType.DMA((80,)), pltpu.SemaphoreType.DMA((24,)), pltpu.SemaphoreType.DMA((5,)),
                        pltpu.SemaphoreType.DMA((6,)), pltpu.SemaphoreType.DMA((12,))],
        compiler_params=pltpu.CompilerParams(collective_id=1, has_side_effects=True, vmem_limit_bytes=60 << 20),
    )(lengths, groups, tok, cot, vectors, w_qkv, w_up, w_dense, w_down)


class Sender:
    def __init__(self, send_sems, recv_sems, load_sems):
        self.copies = Copies(send_sems, recv_sems)
        self.load_sems, self.loads, self.sent = load_sems, [], []

    def load(self, src, dst):
        copy = pltpu.make_async_copy(src, dst, self.load_sems.at[len(self.loads)])
        copy.start()
        self.loads.append([copy, False])
        return len(self.loads) - 1

    def need(self, *which):
        for i in which:
            if not self.loads[i][1]:
                self.loads[i][0].wait()
                self.loads[i][1] = True

    def send(self, src, dst, device, when=None, slot=None):
        copy = self.copies.make(src, dst, device, slot)
        if when is None:
            copy.start()
        else:
            pl.when(when)(copy.start)
        self.sent.append([copy, when])
        return copy

    def late(self, copy):
        self.sent = [[e[0], None] if e[0] is copy else e for e in self.sent]

    def wait_sent(self, copy):
        for entry in self.sent:
            if entry[0] is copy:
                self.sent = [e for e in self.sent if e is not entry]
                copy.wait_send()
                return

    def wait_all(self):
        self.need(*range(len(self.loads)))
        for copy, when in self.sent:
            if when is None:
                copy.wait_send()
            else:
                pl.when(when)(copy.wait_send)


class Columns:
    def __init__(self, buffer, sems, wanted):
        self.buffer, self.sems, self.wanted, self.taken, self.fetches = buffer, sems, wanted, 0, []
        if wanted:
            self.fetch(0)

    def fetch(self, i):
        src, at = self.wanted[i]
        copy = pltpu.make_async_copy(src.at[at], self.buffer.at[i % 2], self.sems.at[i % 2])
        copy.start()
        self.fetches.append(copy)

    def take(self):
        i = self.taken
        self.taken += 1
        if i + 1 < len(self.wanted):
            self.fetch(i + 1)
        self.fetches[i].wait()
        return self.buffer.at[i % 2]


def columns(first, count):
    if not isinstance(first, int):
        first = pl.multiple_of(first, count)
    return slice(None), pl.ds(first, count)


class Stream:
    def __init__(self, sender, tier_count, rows, half, product, part_s, near_r, far_r, line_s, line_r, total_s, free_core, free_far, before=None):
        self.sender, self.rows, self.half, self.product = sender, rows, half, product
        self.part_s, self.near_r, self.far_r, self.line_s, self.line_r, self.total_s = part_s, near_r, far_r, line_s, line_r, total_s
        self.line_id, flips, self.line, self.core, self.far_peer, self.col_peer = neighbours(tier_count)
        self.bit = (self.line_id % 2 + lax.axis_index("col")) % 2
        self.middle = (self.line_id == 1) | (self.line_id == 2)
        self.ends = (self.line_id == 0) | (self.line_id == 3)
        self.chunk = rows // CH
        self.free_core, self.free_far, self.before, self.far_here = free_core, free_far, before, []
        self.near, self.far, self.col, self.one, self.two, self.three, self.relay = {}, {}, {}, {}, {}, {}, {}

    def cut(self, c):
        return pl.ds(c * self.chunk, self.chunk)

    def compute(self, p, c):
        place = CH * p + c
        out = self.part_s.at[place]
        chunk, rows = self.chunk, self.rows
        if self.before:
            for copy in [*self.before.near[p, c], self.before.far[p, c], self.before.col[p, c]]:
                self.sender.wait_sent(copy)
        step = self.half // 2

        def body(n, carry):
            at = pl.ds(pl.multiple_of(n * step, step), step)

            def lhs(ref):
                base = p * 4 * rows + c * chunk
                return jnp.concatenate([ref[pl.ds(base + t * rows, chunk), :] for t in range(4)], axis=0)

            low = self.product(lhs, at).astype(bf16)
            for t in range(4):
                out[t, :, at] = low[t * chunk:(t + 1) * chunk]
            return carry

        lax.fori_loop(0, 2 * self.half // step, body, 0)
        into = self.near_r.at[place]
        if self.before:
            pl.semaphore_wait(self.free_core.at[place], 1)
        self.near[p, c] = [self.sender.send(out.at[1], into.at[0], self.core), self.sender.send(out.at[3], into.at[1], self.core)]

    def give_far(self, p, c):
        place = CH * p + c
        self.near[p, c][1].wait_recv()
        mine = self.part_s.at[place, 2]
        mine[...] = (mine[...].astype(f32) + self.near_r[place, 1].astype(f32)).astype(bf16)
        for copy in list(self.far.values())[:max(0, len(self.far) + 1 - DEPTH)]:
            if not any(copy is other for other in self.far_here):
                copy.wait_recv()
                self.far_here.append(copy)
        if self.before:
            pl.semaphore_wait(self.free_far.at[place], 1)
        self.far[p, c] = self.sender.send(mine, self.far_r.at[place], self.far_peer)

    def give_col(self, p, c):
        place, half = CH * p + c, self.half
        self.near[p, c][0].wait_recv()
        if not any(copy is self.far[p, c] for copy in self.far_here):
            self.far[p, c].wait_recv()
            self.far_here.append(self.far[p, c])
        mine = self.part_s.at[place, 0]
        total = mine[...].astype(f32) + self.near_r[place, 0].astype(f32)
        total = (total + self.far_r[place].astype(f32)).astype(bf16)
        if not self.before:
            for sem, peer in ((self.free_core, self.core), (self.free_far, self.far_peer)):
                pl.semaphore_signal(sem.at[place], inc=1, device_id=peer, device_id_type=pl.DeviceIdType.MESH)
        self.line_s[2 * p + self.bit, self.cut(c), :] = total[:, :half]
        mine[:, pl.ds(half, half)] = total[:, half:]
        self.col[p, c] = self.sender.send(mine.at[:, pl.ds(half, half)], self.line_s.at[2 * p + self.bit, self.cut(c)], self.col_peer)

    def give_line(self, p, c):
        self.col[p, c].wait_recv()
        own, got, cut, send = self.line_s, self.line_r, self.cut(c), self.sender.send
        if p == 0:
            self.one[c] = send(own.at[1, cut], got.at[0, cut], self.line[1])
        else:
            self.relay[c] = send(own.at[3, cut], got.at[3, cut], self.line[1], self.ends)
            self.three[c] = send(own.at[3, cut], got.at[2, cut], self.line[3], self.middle)
            self.two[c] = send(own.at[2, cut], got.at[1, cut], self.line[2], self.ends)

    def relay_line(self, c):
        own, got, cut = self.line_s, self.line_r, self.cut(c)

        @pl.when(self.middle)
        def _():
            self.relay[c].wait_recv()
            own[2, cut, :] = (own[2, cut, :].astype(f32) + got[3, cut, :].astype(f32)).astype(bf16)
            self.two[c].start()

        self.sender.late(self.two[c])

    def finish(self, c):
        own, got, cut, total_s = self.line_s, self.line_r, self.cut(c), self.total_s
        self.one[c].wait_recv()
        self.two[c].wait_recv()
        total_s[cut, :] = own[0, cut, :].astype(f32) + got[0, cut, :].astype(f32) + got[1, cut, :].astype(f32)

        @pl.when(self.middle)
        def _():
            self.three[c].wait_recv()
            total_s[cut, :] += got[2, cut, :].astype(f32)

    def run(self, what, args):
        {"c": self.compute, "x": self.give_far, "y": self.give_col, "z": self.give_line, "r": self.relay_line, "f": self.finish}[what](*args)


class InGrad:
    def __init__(self, sender, tier_count, taker, rhs, out, mine_s, mine_r):
        self.sender, self.taker, self.rhs, self.out, self.mine_s, self.mine_r = sender, taker, rhs, out, mine_s, mine_r
        self.line_id, flips, self.line, core, far, self.col = neighbours(tier_count)
        self.near, self.given = {}, []

    def other(self, s):
        self.mine_s[s] = t_mm(self.taker.take()[...], self.rhs[...]).astype(bf16)
        self.near[s] = self.sender.send(self.mine_s.at[s], self.mine_r.at[s], self.col)

    def mine(self, s):
        value = t_mm(self.taker.take()[...], self.rhs[...])
        self.near[s].wait_recv()
        self.sender.wait_sent(self.near[s])
        self.mine_s[s] = (value + self.mine_r[s].astype(f32)).astype(bf16)
        if s:
            self.given.append(self.sender.send(self.mine_s.at[s], self.out.at[self.line_id], self.line[s]))
        else:
            self.sender.load(self.mine_s.at[0], self.out.at[self.line_id])

    def wait(self):
        for copy in self.given:
            copy.wait_recv()


def backward_kernel(tier_count, order, attn, hidden, slope, qkv, turns, stat, x_in, b_in, dm, wq, wu, tok, cot, vec_ref,
                  block_out, grad_out, gin_out, gd_out, vec_out,
                  a_v, h_v, d_v, at_v, qkv_v, turn_v, stat_v, wq_v, wu_v, da_v, dq_v, du_v, dk_s, dv_s, col_v, back_v, slope_v,
                  part_s, near_r, far_r, line_s, line_r, dn_s, gq_s, gq_r, gu_s, gu_r, do_s, do_r, dm_s,
                  stat_s, stat_r, stat_own, hat_s, hat_r, row_s, row_r, mid_s, mid_r, end_s, end_r, out_s, out_r, out_mid, out_end,
                  bias_s, bias_r, bias_v, send_sems, recv_sems, load_sems, free_core, free_far, col_sems, back_sems, slope_sems):
    line_id, flips, line, core, far, col = neighbours(tier_count)
    rows, half = tok.shape
    part = a_v.shape[1]
    slots = 4 * rows
    width = 2 * half
    col_id, row_id = lax.axis_index("col"), lax.axis_index("row")
    across = (lax.axis_index("dp"), 3 - row_id, col_id)
    row_peers = [core, far, across]
    block = half // 4
    scale = HDIM ** (-0.5)
    sender = Sender(send_sems, recv_sems, load_sems)
    for src, dst in ((attn, a_v), (hidden, h_v), (dm, d_v), (qkv, qkv_v), (turns, turn_v), (stat, stat_v), (wq, wq_v), (wu, wu_v)):
        sender.load(src, dst)
    send = sender.send
    wanted = []
    for what, *args in order:
        if what in ("qo", "qm", "uo", "um"):
            wanted.append((x_in, columns(flips[args[0]] * block + (half if what[1] == "o" else 0), block)))
        if what in ("do", "dm"):
            wanted.append((b_in, columns(args[0] * block + (half if what == "do" else 0), block)))
    taker = Columns(col_v, col_sems, wanted)
    b_rows = Columns(back_v, back_sems, [(b_in, (pl.ds(args[0] * rows, rows), slice(None))) for what, *args in order if what == "a"])
    s_rows = Columns(slope_v, slope_sems, [(slope, (pl.ds(args[0] * rows, rows), slice(None))) for what, *args in order if what == "a"])
    meet([line[1], line[2], line[3], core, far, across, col])
    own_columns = pl.ds(pl.multiple_of(col_id * half, half), half)
    other_columns = pl.ds(pl.multiple_of((1 - col_id) * half, half), half)

    def rows_to_lanes(one, two):
        lane = lax.broadcasted_iota(jnp.int32, (rows, 128), 1)
        return jnp.where(lane == 0, one, jnp.where(lane == 1, two, 0.0)).T[0:8]

    def lanes_to_rows(value):
        return jnp.concatenate([value, jnp.zeros((120, rows), f32)], axis=0).T

    tail = {}

    def stats_start():
        wide = tok[...].astype(f32)
        stat_s[...] = rows_to_lanes(jnp.sum(wide, axis=1, keepdims=True), jnp.sum(wide * wide, axis=1, keepdims=True))
        tail["stat"] = send(stat_s, stat_r, col)

    def stats_end():
        tail["stat"].wait_recv()
        both = lanes_to_rows((stat_s[...] + stat_r[...]) / width)
        mean = both[:, 0:1]
        inv = lax.rsqrt(both[:, 1:2] - mean * mean + eps_norm)
        lane = lax.broadcasted_iota(jnp.int32, (rows, 128), 1)
        stat_own[...] = jnp.where(lane == 0, mean, inv)

    def fold(rows_of):
        step = half // 8
        return jnp.concatenate([jnp.concatenate([row[:, i * step:(i + 1) * step] for i in range(8)]) for row in rows_of], axis=1)

    def unfold(value, i):
        step = half // 8
        return jnp.concatenate([value[j:j + 1, i * step:(i + 1) * step] for j in range(8)], axis=1)

    def early_one():
        total = jnp.concatenate([jnp.sum(ref[...].astype(f32), axis=0, keepdims=True) for ref in (dq_v, du_v)], axis=1)
        blocks = [total[:, k * part:(k + 1) * part] for k in range(7)]
        bias_s[...] = jnp.concatenate(blocks + [jnp.zeros((1, part), f32)])
        tail["bias"] = [send(bias_s, bias_r, col)]
        out_s[...] = fold([jnp.sum(cot[...].astype(f32), axis=0, keepdims=True)])
        tail["out"] = [send(out_s, out_r.at[i], peer) for i, peer in enumerate(row_peers)]

    def early_two():
        for copy in tail["bias"] + tail["out"]:
            copy.wait_recv()
        bias_v[line_id, row_id] = bias_s[...] + bias_r[...]
        mine = bias_v.at[line_id, row_id]
        tail["bias"] = [send(mine, mine, peer) for peer in row_peers]
        out_mid[...] = (out_s[...] + out_r[0]) + (out_r[1] + out_r[2])
        tail["out"] = [send(out_mid, out_r.at[3 + i], line[1 + i]) for i in range(3)]

    def early_three():
        for copy in tail["bias"] + tail["out"]:
            copy.wait_recv()
        tail["bias"] = [send(bias_v.at[line_id], bias_v.at[line_id], line[1 + i]) for i in range(3)]
        out_end[...] = (out_mid[...] + out_r[3]) + (out_r[4] + out_r[5])
        tail["out"] = [send(out_end, out_r.at[6], col)]

    def early_four():
        for copy in tail["bias"] + tail["out"]:
            copy.wait_recv()
        for columns_of, value in ((own_columns, out_end[...]), (other_columns, out_r[6])):
            vec_out[9:10, columns_of] = unfold(value, 0)
            vec_out[10:11, columns_of] = unfold(value, 0)
        for r in range(4):
            for z in range(LINE):
                vec_out[2:9, (r * LINE + z) * part:(r * LINE + z + 1) * part] = bias_v[z, r, 0:7, :]

    def vectors_end():
        gain = vec_ref[0:1, own_columns]
        cuts = [pl.ds(i * 64, 64) for i in range(rows // 64)]
        sums, crosses = [], []
        totals = [jnp.zeros((1, half), f32) for _ in range(2)]
        for at in cuts:
            centred = (tok[at, :].astype(f32) - stat_own[at, 0:1]) * stat_own[at, 1:2]
            grad = dn_s[at, :]
            hat = grad * gain
            sums.append(jnp.sum(hat, axis=1, keepdims=True))
            crosses.append(jnp.sum(hat * centred, axis=1, keepdims=True))
            totals[0] += jnp.sum(grad * centred, axis=0, keepdims=True)
            totals[1] += jnp.sum(grad, axis=0, keepdims=True)
        row_s[...] = fold(totals)
        row_copies = [send(row_s, row_r.at[i], peer) for i, peer in enumerate(row_peers)]
        hat_s[...] = rows_to_lanes(jnp.concatenate(sums), jnp.concatenate(crosses))
        hat_copy = send(hat_s, hat_r, col)
        for copy in row_copies:
            copy.wait_recv()
        mid_s[...] = (row_s[...] + row_r[0]) + (row_r[1] + row_r[2])
        mid_copies = [send(mid_s, mid_r.at[i], line[1 + i]) for i in range(3)]
        hat_copy.wait_recv()
        both = lanes_to_rows((hat_s[...] + hat_r[...]) / width)
        for at, first in zip(cuts, range(0, rows, 64)):
            centred = (tok[at, :].astype(f32) - stat_own[at, 0:1]) * stat_own[at, 1:2]
            mine = both[first:first + 64]
            hat = dn_s[at, :] * gain
            grad_out[at, :] = stat_own[at, 1:2] * (hat - mine[:, 0:1] - centred * mine[:, 1:2]) + cot[at, :].astype(f32)
        for copy in mid_copies:
            copy.wait_recv()
        end_s[...] = (mid_s[...] + mid_r[0]) + (mid_r[1] + mid_r[2])
        end_copy = send(end_s, end_r, col)
        end_copy.wait_recv()
        for columns_of, value in ((own_columns, end_s[...]), (other_columns, end_r[...])):
            for i in range(2):
                vec_out[i:i + 1, columns_of] = unfold(value, i)


    def product(lhs, at):
        return mm(lhs(a_v), d_v[0:part, at]) + mm(lhs(h_v), d_v[part:, at])

    def product_back(lhs, at):
        return mm_t(lhs(dq_v), wq_v[at, :]) + mm_t(lhs(du_v), wu_v[at, :])

    first = Stream(sender, tier_count, rows, half, product, part_s, near_r, far_r, line_s.at[0], line_r.at[0], dn_s, free_core, free_far)
    second = Stream(sender, tier_count, rows, half, product_back, part_s, near_r, far_r, line_s.at[1], line_r.at[1], dn_s,
                    free_core, free_far, first)
    qkv_grad = InGrad(sender, tier_count, taker, dq_v, gin_out.at[:, :, pl.ds(0, 3 * part)], gq_s, gq_r)
    up_grad = InGrad(sender, tier_count, taker, du_v, gin_out.at[:, :, pl.ds(3 * part, 4 * part)], gu_s, gu_r)

    def back_block(i):
        sender.need(2)
        back, slopes = b_rows.take(), s_rows.take()
        at = pl.ds(i * rows, rows)
        da_v[at, :] = mm_t(back[...], d_v[0:part, :]).astype(bf16)
        du_v[at, :] = (mm_t(back[...], d_v[part:, :]) * slopes[...]).astype(bf16)

    quarters = [row_id, row_id + 1 - 2 * (row_id % 2), (row_id + 2) % 4, 3 - row_id]
    lane = lax.broadcasted_iota(jnp.int32, (rows, part), 1)

    def attend_back(p, i):
        sender.need(3, 4, 5)
        if i == 0:
            dk_s[...] = jnp.zeros_like(dk_s)
            dv_s[...] = jnp.zeros_like(dv_s)
        whole = pl.ds(p * slots, slots)
        at = pl.ds(p * slots + i * rows, rows)
        key_place = jnp.concatenate([quarters[t] * rows + lax.broadcasted_iota(jnp.int32, (1, rows), 1) for t in range(4)], axis=1)
        place = quarters[i] * rows + lax.broadcasted_iota(jnp.int32, (rows, 1), 0)
        allowed = (key_place >= stat_v[at, part - 1:part].astype(jnp.int32)) & (key_place <= place)
        queries, d_attn = qkv_v[at, 0:part], da_v[at, :]
        keys, values = qkv_v[whole, part:2 * part], qkv_v[whole, 2 * part:]
        d_q = jnp.zeros((rows, part), f32)
        for h in range(part // HDIM):
            head = (lane >= h * HDIM) & (lane < (h + 1) * HDIM)
            q_h = jnp.where(head, queries, jnp.zeros_like(queries))
            da_h = jnp.where(head, d_attn, jnp.zeros_like(d_attn))
            scores = jnp.where(allowed, mm_t(q_h, keys) * scale, -1e30)
            probs = jnp.exp(scores - stat_v[at, h:h + 1])
            low = probs.astype(bf16)
            d_probs = mm_t(da_h, values)
            delta = jnp.sum(probs * d_probs, axis=-1, keepdims=True)
            d_scores = (probs * (d_probs - delta)).astype(bf16)
            d_q = jnp.where(head, mm(d_scores, keys), d_q)
            dk_s[...] += t_mm(q_h, d_scores)
            dv_s[...] += t_mm(da_h, low)
        dq_v[at, 0:part] = turn(d_q * scale, turn_v[at, :], -1.0).astype(bf16)
        if i == 3:
            dq_v[whole, part:2 * part] = turn(dk_s[...].T * scale, turn_v[whole, :], -1.0).astype(bf16)
            dq_v[whole, 2 * part:] = dv_s[...].T.astype(bf16)

    d_near = {}

    def out_other(j):
        sender.need(0, 1)
        if not d_near:
            at_v[0:part, :] = a_v[...].T
            at_v[part:, :] = h_v[...].T
        do_s[j] = mm(at_v[...], taker.take()[...]).astype(bf16)
        d_near[j] = send(do_s.at[j], do_r.at[j], col)

    d_done = []

    def out_mine(j):
        if len(d_done) > 1:
            sender.need(d_done[-2])
        value = mm(at_v[...], taker.take()[...])
        d_near[j].wait_recv()
        staged = dm_s.at[len(d_done) % 2]
        staged[...] = value + do_r[j].astype(f32)
        d_done.append(sender.load(staged, gd_out.at[:, pl.ds(j * block, block)]))

    actions = {"a": back_block, "b": attend_back, "qo": qkv_grad.other, "qm": qkv_grad.mine, "uo": up_grad.other, "um": up_grad.mine,
               "do": out_other, "dm": out_mine, "s": stats_start, "S": stats_end, "e1": early_one, "e2": early_two, "e3": early_three,
               "e4": early_four, "v": vectors_end}
    for what, *args in order:
        if what in actions:
            actions[what](*args)
            continue
        which, args = args[0], args[1:]
        if what == "c":
            sender.need(*((6, 7) if which else (0, 1, 2)))
        (second if which else first).run(what, args)
        if what == "f" and not which:
            at = first.cut(args[0])
            bias = vec_ref[9:10, own_columns] + vec_ref[10:11, own_columns]
            block_out[at, :] = (tok[at, :].astype(f32) + dn_s[at, :] + bias).astype(bf16)
    qkv_grad.wait()
    up_grad.wait()
    sender.wait_all()


BACKWARD_ORDER = [
    ("c", 0, 1, 0), ("do", 2), ("x", 0, 1, 0), ("a", 6), ("a", 2), ("a", 3), ("c", 0, 0, 0), ("do", 3), ("c", 0, 1, 1), ("a", 5), ("a", 1),
    ("x", 0, 0, 0), ("y", 0, 1, 0), ("a", 0), ("a", 4), ("x", 0, 1, 1), ("b", 0, 0), ("a", 7), ("z", 0, 1, 0), ("uo", 2), ("b", 0, 1),
    ("c", 0, 0, 1), ("uo", 3), ("b", 0, 2), ("um", 2), ("b", 0, 3), ("y", 0, 0, 0), ("b", 1, 0), ("y", 0, 1, 1), ("r", 0, 0), ("b", 1, 1),
    ("x", 0, 0, 1), ("b", 1, 2), ("b", 1, 3), ("c", 1, 1, 0), ("qo", 0), ("z", 0, 1, 1), ("z", 0, 0, 0), ("x", 1, 1, 0), ("qo", 2), ("e1",),
    ("c", 1, 0, 0), ("y", 0, 0, 1), ("qm", 2), ("qo", 1), ("dm", 3), ("c", 1, 1, 1), ("x", 1, 1, 1), ("uo", 0), ("y", 1, 1, 0), ("um", 3),
    ("dm", 2), ("z", 0, 0, 1), ("f", 0, 0), ("e2",), ("c", 1, 0, 1), ("r", 0, 1), ("do", 1), ("qm", 0), ("qm", 1), ("x", 1, 0, 0), ("e3",),
    ("e4",), ("y", 1, 1, 1), ("s",), ("x", 1, 0, 1), ("um", 0), ("z", 1, 1, 0), ("do", 0), ("z", 1, 1, 1), ("y", 1, 0, 0), ("y", 1, 0, 1),
    ("dm", 1), ("f", 0, 1), ("dm", 0), ("z", 1, 0, 0), ("r", 1, 0), ("uo", 1), ("z", 1, 0, 1), ("S",), ("qo", 3), ("r", 1, 1), ("um", 1),
    ("f", 1, 0), ("qm", 3), ("f", 1, 1), ("v",),
]


def backward(tier_count, attn, hidden, slope, qkv, turns, stat, normed, back, out_mat, qkv_mat, up_mat, tok, cot, vectors, order=None):
    rows, half = tok.shape
    width = 2 * half
    chunk = rows // CH
    all_rows, part = attn.shape
    block = half // 4
    sds = jax.ShapeDtypeStruct
    any_ = pl.BlockSpec(memory_space=pl.ANY)
    vmem = pl.BlockSpec(memory_space=pltpu.VMEM)

    def buf(*shape, kind=bf16):
        return pltpu.VMEM(shape, kind)

    dma = pltpu.SemaphoreType.DMA
    regular = pltpu.SemaphoreType.REGULAR
    return pl.pallas_call(
        functools.partial(backward_kernel, tier_count, order or BACKWARD_ORDER),
        out_shape=[sds((rows, half), bf16), sds((rows, half), f32), sds((LINE, block, 7 * part), bf16), sds((5 * part, half), f32), sds((11, width), f32)],
        in_specs=[any_] * 11 + [vmem] * 3,
        out_specs=[vmem, vmem, any_, any_, vmem],
        scratch_shapes=[
            buf(all_rows, part), buf(all_rows, 4 * part), buf(5 * part, width), buf(5 * part, all_rows),
            buf(all_rows, 3 * part), buf(all_rows, 2 * part, kind=f32), buf(all_rows, part, kind=f32), buf(width, 3 * part), buf(width, 4 * part),
            buf(all_rows, part), buf(all_rows, 3 * part), buf(all_rows, 4 * part), buf(part, 4 * rows, kind=f32), buf(part, 4 * rows, kind=f32),
            buf(2, all_rows, block), buf(2, rows, width), buf(2, rows, 4 * part, kind=f32),
            buf(2 * CH, 4, chunk, width), buf(2 * CH, 2, chunk, width), buf(2 * CH, chunk, width),
            buf(2, 4, rows, half), buf(2, 4, rows, half), buf(rows, half, kind=f32),
            buf(4, block, 3 * part), buf(4, block, 3 * part), buf(4, block, 4 * part), buf(4, block, 4 * part),
            buf(4, 5 * part, block), buf(4, 5 * part, block), buf(2, 5 * part, block, kind=f32),
            buf(8, rows, kind=f32), buf(8, rows, kind=f32), buf(rows, 128, kind=f32), buf(8, rows, kind=f32), buf(8, rows, kind=f32),
            buf(8, half // 4, kind=f32), buf(3, 8, half // 4, kind=f32), buf(8, half // 4, kind=f32), buf(3, 8, half // 4, kind=f32),
            buf(8, half // 4, kind=f32), buf(8, half // 4, kind=f32),
            buf(8, half // 8, kind=f32), buf(7, 8, half // 8, kind=f32), buf(8, half // 8, kind=f32), buf(8, half // 8, kind=f32),
            buf(8, part, kind=f32), buf(8, part, kind=f32), buf(LINE, 4, 8, part, kind=f32),
            dma((128,)), dma((128,)), dma((24,)), regular((2 * CH,)), regular((2 * CH,)), dma((2,)), dma((2,)), dma((2,)),
        ],
        compiler_params=pltpu.CompilerParams(collective_id=2, has_side_effects=True, vmem_limit_bytes=63 << 20),
    )(attn, hidden, slope, qkv, turns, stat, normed, back, out_mat, qkv_mat, up_mat, tok, cot, vectors)


def adamw_fast(weight, first_moment, second_moment, gradient, rate):
    first_next = 0.9 * first_moment + 0.1 * gradient
    second_next = 0.95 * second_moment + 0.05 * gradient * gradient
    scaled = second_next * (1.0 / (1.0 - 0.95**STEP))
    root = scaled * lax.rsqrt(scaled) + 1e-08
    update = first_next * (rate / (1.0 - 0.9**STEP)) / root
    return first_next, second_next, (1.0 - 0.1 * rate) * weight - update


def step_kernel(rates, gin_ref, gout_ref, *refs):
    ins, outs = refs[:12], refs[12:]
    pieces = gin_ref.shape[0]
    part = gin_ref.shape[2] // 7

    def one(i, at, grad):
        values = adamw_fast(*[ref[at] for ref in ins[3 * i:3 * i + 3]], grad, rates[i])
        for ref, value in zip(outs[3 * i:3 * i + 3], values):
            ref[at] = value

    for z in range(pieces):
        at = pl.ds(z * part, part)
        for k in range(3):
            one(0, (k, slice(None), at), gin_ref[z, :, pl.ds(k * part, part)].astype(f32))
        for k in range(4):
            one(1, (slice(None), k, at), gin_ref[z, :, pl.ds((3 + k) * part, part)].astype(f32))
    one(2, (slice(None), slice(None)), gout_ref[0])
    for k in range(4):
        one(3, (slice(None), k, slice(None)), gout_ref[1 + k])


def step_all(grad_in, grad_out, qkv, up, dense, down):
    steps = 8
    rates = (D ** (-0.5), D ** (-0.5), max(D // 128, 4) ** (-0.5), FF ** (-0.5))

    def spec(shape, axis):
        block = tuple(size // steps if i == axis else size for i, size in enumerate(shape))
        return pl.BlockSpec(block, lambda i: tuple(i if a == axis else 0 for a in range(len(shape))))

    arrays = [*qkv, *up, *dense, *down]
    axes = [1] * 3 + [0] * 9
    specs = [spec(value.shape, axis) for value, axis in zip(arrays, axes)]
    out = pl.pallas_call(
        functools.partial(step_kernel, rates),
        grid=(steps,),
        out_shape=[jax.ShapeDtypeStruct(value.shape, f32) for value in arrays],
        in_specs=[spec(grad_in.shape, 1), spec(grad_out.shape, 1)] + specs,
        out_specs=specs,
        compiler_params=pltpu.CompilerParams(vmem_limit_bytes=62 << 20),
    )(grad_in, grad_out, *arrays)
    return [out[i:i + 3] for i in range(0, 12, 3)]


def per_device(
    tokens,
    cotangent,
    doc_lengths,
    doc_groups,
    w_qkv,
    w_up,
    w_dense,
    w_down,
    vectors,
    m_qkv,
    v_qkv,
    m_up,
    v_up,
    m_dense,
    v_dense,
    m_down,
    v_down,
    m_vec,
    v_vec,
):
    dp_count = lax.axis_size("dp")
    tier_count = dp_count // LINE
    row_count = lax.axis_size("row")
    col_count = lax.axis_size("col")
    assert row_count == 4 and col_count == 2 and dp_count % LINE == 0
    tok_dev, half_width = tokens.shape
    slot_count = tok_dev * row_count
    full_width = half_width * col_count
    row_width = full_width // row_count
    part = row_width // LINE
    tier_groups = [[line * tier_count + tier for tier in range(tier_count)] for line in range(LINE)]


    def tier_gather(value):
        if tier_count > 1:
            value = lax.all_gather(value, "dp", axis=0, tiled=True, axis_index_groups=tier_groups)
        return value

    if tier_count > 1:
        full_qkv, full_up, full_dense, full_down = [
            tier_gather(weight.astype(bf16)).astype(f32) for weight in (w_qkv, w_up, w_dense, w_down)
        ]
    else:
        full_qkv, full_up, full_dense, full_down = w_qkv, w_up, w_dense, w_down
    normed, back, qkv_mat, up_mat, out_mat, back_own, *fresh = gather(
        tier_count,
        doc_lengths,
        doc_groups,
        tokens,
        cotangent,
        vectors,
        full_qkv.transpose(1, 0, 2),
        full_up,
        full_dense,
        full_down,
    )
    rows_all = 2 * slot_count
    normed = normed.reshape(rows_all, full_width)
    back = back.reshape(rows_all, full_width)
    qkv_mat = qkv_mat.reshape(full_width, 3 * part)
    up_mat = up_mat.reshape(full_width, 4 * part)

    fresh = [value.reshape(rows_all, value.shape[-1]) for value in fresh]
    block_out, grad_tokens, grad_in, grad_out, vec_grad = backward(
        tier_count, *fresh, normed, back, out_mat, qkv_mat, up_mat, tokens, back_own, vectors
    )

    def tier_sum(value):
        if tier_count > 1:
            value = lax.psum_scatter(
                value, "dp", scatter_dimension=0, tiled=True, axis_index_groups=tier_groups
            )
        return value

    def own_columns(value, parts):
        value = value.astype(f32).reshape(LINE, half_width // LINE, parts, part)
        return tier_sum(value.transpose(1, 2, 0, 3).reshape(half_width // LINE, parts, row_width))

    if tier_count > 1:
        vec_grad = lax.psum(vec_grad, "dp", axis_index_groups=tier_groups)
        red_qkv = own_columns(grad_in[:, :, : 3 * part], 3)
        red_up = own_columns(grad_in[:, :, 3 * part :], 4)
        red_dense = tier_sum(grad_out[:part])
        red_down = tier_sum(grad_out[part:].reshape(4, part, half_width).transpose(1, 0, 2))
        qkv_new = adamw(w_qkv, m_qkv, v_qkv, red_qkv, D ** (-0.5), 0.1)
        up_new = adamw(w_up, m_up, v_up, red_up, D ** (-0.5), 0.1)
        dense_new = adamw(w_dense, m_dense, v_dense, red_dense, max(D // 128, 4) ** (-0.5), 0.1)
        down_new = adamw(w_down, m_down, v_down, red_down, FF ** (-0.5), 0.1)
    else:
        qkv_new, up_new, dense_new, down_new = step_all(
            grad_in,
            grad_out.reshape(5, part, half_width),
            [value.transpose(1, 0, 2) for value in (w_qkv, m_qkv, v_qkv)],
            (w_up, m_up, v_up),
            (w_dense, m_dense, v_dense),
            (w_down, m_down, v_down),
        )
        qkv_new = [value.transpose(1, 0, 2) for value in qkv_new]
    vec_new = adamw(vectors, m_vec, v_vec, vec_grad, 0.5, 0.0)
    return (
        block_out,
        grad_tokens,
        qkv_new[0],
        qkv_new[1],
        qkv_new[2],
        up_new[0],
        up_new[1],
        up_new[2],
        dense_new[0],
        dense_new[1],
        dense_new[2],
        down_new[0],
        down_new[1],
        down_new[2],
        vec_new[0],
        vec_new[1],
        vec_new[2],
    )


def solution(mesh):
    placed = (
        P(("dp", "row"), "col"),
        P(("dp", "row"), "col"),
        P(),
        P(),
        P(("col", "dp"), None, "row"),
        P(("col", "dp"), None, "row"),
        P(("row", "dp"), "col"),
        P(("row", "dp"), None, "col"),
        P(),
        P(("col", "dp"), None, "row"),
        P(("col", "dp"), None, "row"),
        P(("col", "dp"), None, "row"),
        P(("col", "dp"), None, "row"),
        P(("row", "dp"), "col"),
        P(("row", "dp"), "col"),
        P(("row", "dp"), None, "col"),
        P(("row", "dp"), None, "col"),
        P(),
        P(),
    )
    return jax.shard_map(
        per_device,
        mesh=mesh,
        in_specs=placed,
        out_specs=(
            P(("dp", "row"), "col"),
            P(("dp", "row"), "col"),
            P(("col", "dp"), None, "row"),
            P(("col", "dp"), None, "row"),
            P(("col", "dp"), None, "row"),
            P(("col", "dp"), None, "row"),
            P(("col", "dp"), None, "row"),
            P(("col", "dp"), None, "row"),
            P(("row", "dp"), "col"),
            P(("row", "dp"), "col"),
            P(("row", "dp"), "col"),
            P(("row", "dp"), None, "col"),
            P(("row", "dp"), None, "col"),
            P(("row", "dp"), None, "col"),
            P(),
            P(),
            P(),
        ),
        check_vma=False,
    )
```

```python
import functools

import jax
import jax.numpy as jnp
from jax import lax
from jax.experimental import pallas as pl
from jax.experimental.pallas import tpu as pltpu
from jax.sharding import PartitionSpec as P

D = 2048
HDIM = 64
ROT = 32
FF = 8192
BLK = 512
STEP = 10
LINE = 4


eps_norm = 1e-05
f32 = jnp.float32
bf16 = jnp.bfloat16


def adamw(weight, first_moment, second_moment, gradient, rate, decay):
    first_next = 0.9 * first_moment + 0.1 * gradient
    second_next = 0.95 * second_moment + 0.05 * gradient * gradient
    correct_one = 1.0 - 0.9**STEP
    correct_two = 1.0 - 0.95**STEP
    update = first_next / correct_one / (jnp.sqrt(second_next / correct_two) + 1e-08)
    return (first_next, second_next, weight - rate * (update + decay * weight))


def mm(a, b):
    return jnp.dot(a, b, preferred_element_type=f32)


def mm_t(a, b):
    return lax.dot_general(a, b, (((1,), (1,)), ((), ())), preferred_element_type=f32)


def t_mm(a, b):
    return lax.dot_general(a, b, (((0,), (0,)), ((), ())), preferred_element_type=f32)


def gelu_both(v):
    root = 0.7978845608028654
    square = v * v
    slope = root * (1.0 + 3 * 0.044715 * square)
    tanh = jnp.tanh(root * v * (1.0 + 0.044715 * square))
    outer = 0.5 * (1.0 + tanh)
    return v * outer, outer + 0.5 * v * (1.0 - tanh * tanh) * slope


def turn(value, turns, sign):
    part = value.shape[1]
    quarter = ROT // 2
    lead = lax.broadcasted_iota(jnp.int32, (1, part), 1) % HDIM < quarter
    other = jnp.where(lead, jnp.roll(value, -quarter, axis=1), jnp.roll(value, quarter, axis=1))
    return value * turns[:, 0:part] + sign * (other * turns[:, part:])


class Forward:
    def __init__(self, tier_count, lengths, groups, x_ref, wq_ref, wu_ref, vec_ref, attn_ref, hidden_ref, slope_ref, qkv_ref, turn_ref, stat_ref):
        self.tier_count, self.lengths, self.groups = tier_count, lengths, groups
        self.x_ref, self.wq_ref, self.wu_ref = x_ref, wq_ref, wu_ref
        self.attn_ref, self.hidden_ref, self.slope_ref = attn_ref, hidden_ref, slope_ref
        self.qkv_ref, self.turn_ref, self.stat_ref = qkv_ref, turn_ref, stat_ref
        slots, part = attn_ref.shape
        self.slots, self.part, self.rows = slots, part, slots // 4
        row_id = lax.axis_index("row")
        self.quarters = [row_id, row_id + 1 - 2 * (row_id % 2), (row_id + 2) % 4, 3 - row_id]
        self.line_id = lax.axis_index("dp") // tier_count
        bias_at = pl.ds(pl.multiple_of((row_id * LINE + self.line_id) * part, part), part)
        self.bias = jnp.concatenate([vec_ref[k:k + 1, bias_at] for k in range(2, 9)], axis=1)
        self.key_place = jnp.concatenate(
            [self.quarters[t] * self.rows + lax.broadcasted_iota(jnp.int32, (1, self.rows), 1) for t in range(4)], axis=1)

    def cut(self, i):
        return pl.ds(i * self.rows, self.rows)

    def angles(self, p):
        lengths, groups, part, rows, quarters = self.lengths, self.groups, self.part, self.rows, self.quarters
        line_id, tier_id = self.line_id, lax.axis_index("dp") % self.tier_count
        turn_ref, stat_ref = self.turn_ref, self.stat_ref
        quarter = ROT // 2
        bit = (line_id % 2 + lax.axis_index("col")) % 2
        group = line_id + bit * (1 - 2 * (line_id % 2))
        group = ((group + 2 * p) % 4) * self.tier_count + tier_id
        lanes = lax.broadcasted_iota(jnp.int32, (1, part), 1) % HDIM
        lead = lanes < quarter
        powers = (lanes % quarter).astype(f32) * (-2.0 / ROT)
        speed = jnp.where(lanes < ROT, jnp.exp(powers * 9.210340371976184), 0.0)
        fine = lax.broadcasted_iota(jnp.int32, (32, part), 0).astype(f32) * speed
        fine_cos, fine_sin = jnp.cos(fine), jnp.sin(fine)
        count = lengths.shape[0] + 1
        starts, start = [], jnp.int32(0)
        for i in range(count - 1):
            here = groups[i] == group
            starts.append(jnp.where(here, start, 1 << 30))
            start = start + jnp.where(here, lengths[i], 0)
        starts.append(start)
        which = lax.broadcasted_iota(jnp.int32, (-(-count // 8) * 8, part), 0)
        start_angle = jnp.zeros(which.shape, f32)
        for i in range(count):
            start_angle = jnp.where(which == i, jnp.where(starts[i] < (1 << 30), starts[i], 0).astype(f32), start_angle)
        start_angle = start_angle * speed
        start_cos, start_sin = jnp.cos(start_angle), jnp.sin(start_angle)
        steps = rows // 32
        for t in range(4):
            base = quarters[t] * rows
            coarse = (base + 32 * lax.broadcasted_iota(jnp.int32, (steps, part), 0)).astype(f32) * speed
            coarse_cos, coarse_sin = jnp.cos(coarse), jnp.sin(coarse)
            for j in range(2):
                some = range(j * steps // 2, (j + 1) * steps // 2)
                size = rows // 2
                place_cos = jnp.concatenate([coarse_cos[i:i + 1] * fine_cos - coarse_sin[i:i + 1] * fine_sin for i in some])
                place_sin = jnp.concatenate([coarse_sin[i:i + 1] * fine_cos + coarse_cos[i:i + 1] * fine_sin for i in some])
                place = base + j * size + lax.broadcasted_iota(jnp.int32, (size, part), 0)
                first = jnp.zeros((size, part), jnp.int32)
                first_cos = jnp.ones((size, part), f32)
                first_sin = jnp.zeros((size, part), f32)
                for i in range(count):
                    after = place >= starts[i]
                    first = jnp.where(after, starts[i], first)
                    first_cos = jnp.where(after, start_cos[i:i + 1], first_cos)
                    first_sin = jnp.where(after, start_sin[i:i + 1], first_sin)
                at = pl.ds(t * rows + j * size, size)
                turn_ref[at, 0:part] = place_cos * first_cos + place_sin * first_sin
                sin = place_sin * first_cos - place_cos * first_sin
                turn_ref[at, part:] = jnp.where(lead, -sin, sin)
                lane = lax.broadcasted_iota(jnp.int32, (size, part), 1)
                stat_ref[at, :] = jnp.where(lane == part - 1, first.astype(f32), 0.0)

    def project(self, i):
        part, at = self.part, self.cut(i)
        pre = mm(self.x_ref[at, :], self.wq_ref[...]) + self.bias[:, 0:3 * part]
        turns = self.turn_ref[at, :]
        self.qkv_ref[at, 0:part] = turn(pre[:, 0:part], turns, 1.0).astype(bf16)
        self.qkv_ref[at, part:2 * part] = turn(pre[:, part:2 * part], turns, 1.0).astype(bf16)
        self.qkv_ref[at, 2 * part:] = pre[:, 2 * part:].astype(bf16)

    def up(self, i):
        at = self.cut(i)
        value, slope = gelu_both(mm(self.x_ref[at, :], self.wu_ref[...]) + self.bias[:, 3 * self.part:])
        self.hidden_ref[at, :] = value.astype(bf16)
        self.slope_ref[at, :] = slope

    def attend(self, i):
        part, at, rows = self.part, self.cut(i), self.rows
        lane = lax.broadcasted_iota(jnp.int32, (rows, part), 1)
        keys, values = self.qkv_ref[:, part:2 * part], self.qkv_ref[:, 2 * part:]
        stat = self.stat_ref[at, :]
        place = self.quarters[i] * rows + lax.broadcasted_iota(jnp.int32, (rows, 1), 0)
        allowed = (self.key_place >= stat[:, part - 1:part].astype(jnp.int32)) & (self.key_place <= place)
        queries = self.qkv_ref[at, 0:part]
        out = jnp.zeros((rows, part), f32)
        for h in range(part // HDIM):
            head = (lane >= h * HDIM) & (lane < (h + 1) * HDIM)
            q_h = jnp.where(head, queries, jnp.zeros_like(queries))
            scores = jnp.where(allowed, mm_t(q_h, keys) * HDIM ** (-0.5), -1e30)
            top = jnp.max(scores, axis=-1, keepdims=True)
            weights = jnp.exp(scores - top)
            total = jnp.sum(weights, axis=-1, keepdims=True)
            low = (weights * (1.0 / total)).astype(bf16)
            out = jnp.where(head, mm(low, values), out)
            stat = jnp.where(lane == h, top + jnp.log(total), stat)
        self.attn_ref[at, :] = out.astype(bf16)
        self.stat_ref[at, :] = stat


class Copies:
    def __init__(self, send_sems, recv_sems):
        self.send_sems, self.recv_sems, self.sent, self.received = send_sems, recv_sems, 0, 0

    def slot(self):
        self.received += 1
        return self.received - 1

    def make(self, src, dst, device, slot=None):
        slot = self.slot() if slot is None else slot
        self.sent += 1
        return pltpu.make_async_remote_copy(
            src_ref=src, dst_ref=dst, send_sem=self.send_sems.at[self.sent - 1], recv_sem=self.recv_sems.at[slot],
            device_id=device, device_id_type=pl.DeviceIdType.MESH)

def neighbours(tier_count):
    dp_id, row_id, col_id = lax.axis_index("dp"), lax.axis_index("row"), lax.axis_index("col")
    line_id, tier_id = dp_id // tier_count, dp_id % tier_count
    flips = [line_id, line_id + 1 - 2 * (line_id % 2), (line_id + 2) % 4, 3 - line_id]
    line = [(flip * tier_count + tier_id, row_id, col_id) for flip in flips]
    core = (dp_id, row_id + 1 - 2 * (row_id % 2), col_id)
    far = (dp_id, (row_id + 2) % 4, col_id)
    col = (dp_id, row_id, 1 - col_id)
    return line_id, flips, line, core, far, col

def meet(peers):
    barrier = pltpu.get_barrier_semaphore()
    for peer in peers:
        pl.semaphore_signal(barrier, inc=1, device_id=peer, device_id_type=pl.DeviceIdType.MESH)
    pl.semaphore_wait(barrier, len(peers))


CH = 2
DEPTH = 2

def gather_kernel(tier_count, order, lengths, groups, tok, cot, vec_ref, w_qkv, w_up, w_dense, w_down,
                  x_out, b_out, wq_out, wu_out, d_out, cot_s, attn_out, hidden_out, slope_out, qkv_out, turn_out, stat_out,
                  x_v, wq_v, wu_v, attn_v, hidden_v, slope_v, qkv_v, turn_v, stat_v, tz, cz, ty, xs, qkv_f, up_f, dense_f, down_f, wq, wu, dh,
                  send_sems, recv_sems, local_sems, load_sems, into_sems, out_sems):
    line_id, flips, line, core, far, col = neighbours(tier_count)
    bit = (line_id % 2 + lax.axis_index("col")) % 2
    middle = (line_id == 1) | (line_id == 2)
    rows, half = tok.shape
    chunk = rows // CH
    copies = Copies(send_sems, recv_sems)
    sent, mid_sent, local_left, last = [], [], [], []
    n_local = [0]

    def local(src, dst):
        copy = pltpu.make_async_copy(src, dst, local_sems.at[n_local[0]])
        n_local[0] += 1
        copy.start()
        local_left.append(copy)
        return copy

    def settle(copy):
        if any(c is copy for c in local_left):
            copy.wait()
            local_left[:] = [c for c in local_left if c is not copy]

    def arrive(copy):
        if any(c is copy for c in last):
            copy.wait_recv()
            last[:] = [c for c in last if c is not copy]

    def send(src, dst, device, slot=None):
        copy = copies.make(src, dst, device, slot)
        copy.start()
        sent.append(copy)
        return copy

    def cut(c):
        return pl.ds(c * chunk, chunk)

    class Stream:
        def __init__(self, own, stage, out, normed):
            self.own, self.stage, self.out, self.normed = own, stage, out, normed
            self.line, self.swap, self.spread, self.keep, self.whole = {}, {}, {}, {}, ([], [])

        def start(self, c):
            own, stage = self.own.at[cut(c)], self.stage
            own_copy = local(own, stage.at[0, cut(c)])
            near = send(own, stage.at[1, cut(c)], line[1])
            two = send(own, stage.at[2, cut(c)], line[2])
            slot = copies.slot()
            three = copies.make(own, stage.at[3, cut(c)], line[3], slot)
            relay = copies.make(stage.at[2, cut(c)], stage.at[3, cut(c)], line[1], slot)
            pl.when(middle)(three.start)
            mid_sent.extend([three, relay])
            self.line[c] = own_copy, near, two, three, relay

        def swap_cols(self, c, p):
            own_copy, near, two, three, relay = self.line[c]
            if p == 0:
                settle(own_copy)
                near.wait_recv()
            else:
                three.wait_recv()
            if self.normed:
                dst = ty.at[p, cut(c)]
            else:
                dst = self.out.at[p, 0, cut(c), pl.ds(half, half)]
                self.keep[c, p] = local(self.stage.at[2 * p + bit, cut(c)], self.out.at[p, 0, cut(c), pl.ds(0, half)])
            self.swap[c, p] = send(self.stage.at[2 * p + 1 - bit, cut(c)], dst, col)

        def pass_on(self, c):
            own_copy, near, two, three, relay = self.line[c]
            two.wait_recv()
            pl.when(middle)(relay.start)

        def give(self, c, p):
            self.swap[c, p].wait_recv()
            if self.normed:
                norm(c, p)
                src = xs.at[p, cut(c)]
                self.whole[p].append((settle, local(src, self.out.at[p, 0, cut(c)])))
            else:
                settle(self.keep[c, p])
                src = self.out.at[p, 0, cut(c)]
            self.spread[c, p] = send(src, self.out.at[p, 2, cut(c)], far)
            last.append(send(src, self.out.at[p, 1, cut(c)], core))
            self.whole[p].append((arrive, last[-1]))

        def relay(self, c, p):
            self.spread[c, p].wait_recv()
            last.append(send(self.out.at[p, 2, cut(c)], self.out.at[p, 3, cut(c)], core))
            self.whole[p].append((arrive, last[-1]))

    norm_ref = [[vec_ref.at[i:i + 1, pl.ds(pl.multiple_of(side * half, half), half)] for i in range(2)]
                for side in (lax.axis_index("col"), 1 - lax.axis_index("col"))]

    def norm(c, p):
        step = 64
        def body(i, carry):
            at = pl.ds(pl.multiple_of(c * chunk + i * step, step), step)
            one = tz[2 * p + bit, at, :].astype(f32)
            two = ty[p, at, :].astype(f32)
            width = 2 * half
            mean = (jnp.sum(one, axis=-1, keepdims=True) + jnp.sum(two, axis=-1, keepdims=True)) / width
            square = (jnp.sum(one * one, axis=-1, keepdims=True) + jnp.sum(two * two, axis=-1, keepdims=True)) / width
            inv = lax.rsqrt(square - mean * mean + eps_norm)
            xs[p, at, pl.ds(0, half)] = ((one - mean) * inv * norm_ref[0][0][...] + norm_ref[0][1][...]).astype(bf16)
            xs[p, at, pl.ds(half, half)] = ((two - mean) * inv * norm_ref[1][0][...] + norm_ref[1][1][...]).astype(bf16)
            return carry
        lax.fori_loop(0, chunk // step, body, 0)

    class Weight:
        def __init__(self, src, out):
            self.src, self.out, self.got, self.whole = src, out, {}, []

        def own(self):
            self.whole.append((settle, local(self.src.at[line_id], self.out.at[0, line_id])))
            last.append(send(self.src.at[line_id], self.out.at[1, line_id], col))
            self.whole.append((arrive, last[-1]))

        def start(self):
            for s in (1, 2, 3):
                self.got[s] = send(self.src.at[flips[s]], self.out.at[0, line_id], line[s])

        def swap(self):
            for s in (1, 2, 3):
                self.got[s].wait_recv()
                last.append(send(self.out.at[0, flips[s]], self.out.at[1, flips[s]], col))
                self.whole.append((arrive, last[-1]))

    part = dh.shape[0] // 5
    loads = []
    for i, (src, dst) in enumerate(((w_qkv, qkv_f), (w_up, up_f), (w_dense, dense_f), (w_down, down_f), (cot, cot_s))):
        loads.append(pltpu.make_async_copy(src, dst, load_sems.at[i]))
        loads[-1].start()

    def prepare(what):
        if what == 0:
            loads[0].wait()
            for j in range(LINE):
                for k in range(3):
                    wq[j, :, k * part:(k + 1) * part] = qkv_f[k, :, j * part:(j + 1) * part].astype(bf16)
        if what == 1:
            loads[1].wait()
            for j in range(LINE):
                for k in range(4):
                    wu[j, :, k * part:(k + 1) * part] = up_f[:, k, j * part:(j + 1) * part].astype(bf16)
        if what == 2:
            loads[2].wait()
            dh[0:part, :] = dense_f[...].astype(bf16)
        if what == 3:
            loads[3].wait()
            for k in range(4):
                dh[(k + 1) * part:(k + 2) * part, :] = down_f[:, k, :].astype(bf16)
        if what == 4:
            loads[4].wait()
            total = jnp.int32(0)
            for i in range(lengths.shape[0]):
                total = total + jnp.where(groups[i] == lax.axis_index("dp"), lengths[i], 0)
            place = lax.axis_index("row") * rows + lax.broadcasted_iota(jnp.int32, (rows, half), 0)
            cot_s[...] = jnp.where(place < total, cot_s[...], jnp.zeros_like(cot_s))

    def dense(i):
        at = pl.ds(i * part, part)
        last.append(send(dh.at[at], d_out.at[at, pl.ds(half, half)], col))

    meet([line[1], line[2], line[3], core, far, col])
    T = Stream(tok, tz, x_out, True)
    C = Stream(cot_s, cz, b_out, False)
    Q = Weight(wq, wq_out)
    U = Weight(wu, wu_out)
    slots = 4 * rows
    wide = [ref.reshape(2 * half, ref.shape[-1]) for ref in (wq_v, wu_v)]
    fresh = (attn_v, hidden_v, slope_v, qkv_v, turn_v, stat_v)
    steps = [Forward(tier_count, lengths, groups, x_v.at[p].reshape(slots, 2 * half), *wide, vec_ref, *[ref.at[p] for ref in fresh])
             for p in range(2)]
    going, stored = {}, []

    def fetch(i, src, dst, whole):
        for wait, copy in whole:
            wait(copy)
        going[i] = pltpu.make_async_copy(src, dst, into_sems.at[i])
        going[i].start()

    def store(p, *pairs):
        for src, dst in pairs:
            stored.append(pltpu.make_async_copy(src.at[p], dst.at[p], out_sems.at[len(stored)]))
            stored[-1].start()

    def need(*which):
        for i in which:
            if i in going:
                going.pop(i).wait()

    for what, *args in order:
        if what == "Wq":
            for j in range(2):
                fetch(j, wq_out.at[j], wq_v.at[j], Q.whole)
        if what == "Wu":
            for j in range(2):
                fetch(2 + j, wu_out.at[j], wu_v.at[j], U.whole)
        if what == "X":
            fetch(4 + args[0], x_out.at[args[0]], x_v.at[args[0]], T.whole[args[0]])
        if what == "Fa":
            steps[args[0]].angles(args[0])
        if what == "Fp":
            need(0, 1, 4 + args[0])
            steps[args[0]].project(args[1])
        if what == "Fs":
            steps[args[0]].attend(args[1])
            if args[1] == 3:
                store(args[0], (attn_v, attn_out), (qkv_v, qkv_out), (turn_v, turn_out), (stat_v, stat_out))
        if what == "Fu":
            need(2, 3, 4 + args[0])
            steps[args[0]].up(args[1])
            if args[1] == 3:
                store(args[0], (hidden_v, hidden_out), (slope_v, slope_out))
        if what == "P": prepare(*args)
        if what == "Ts": T.start(*args)
        if what == "Tr": T.pass_on(*args)
        if what == "Cr": C.pass_on(*args)
        if what == "Ty": T.swap_cols(*args)
        if what == "Tx": T.give(*args)
        if what == "Tk": T.relay(*args)
        if what == "Cs": C.start(*args)
        if what == "Cy": C.swap_cols(*args)
        if what == "Cx": C.give(*args)
        if what == "Ck": C.relay(*args)
        if what == "Qo": Q.own()
        if what == "Qs": Q.start()
        if what == "Qy": Q.swap()
        if what == "Uo": U.own()
        if what == "Us": U.start()
        if what == "Uy": U.swap()
        if what == "D": dense(*args)
        if what == "Dl": local(dh, d_out.at[:, pl.ds(0, half)])
    for copy in list(last):
        arrive(copy)
    for copy in stored:
        copy.wait()
    for copy in list(local_left):
        settle(copy)
    for copy in sent:
        copy.wait_send()
    for copy in mid_sent:
        pl.when(middle)(copy.wait_send)

ORDER_A = [
    ("Ts", 0), ("P", 2), ("D", 0), ("P", 3), ("D", 3), ("Ty", 0, 0), ("P", 4), ("Ts", 1), ("Ty", 1, 0), ("Tx", 0, 0), ("Cs", 0), ("P", 0),
    ("D", 1), ("D", 2), ("Tx", 1, 0), ("Tr", 0), ("Fa", 1), ("Cs", 1), ("Cy", 0, 0), ("Tk", 0, 0), ("P", 1), ("Tr", 1), ("Qo",),
    ("Cy", 1, 0), ("Cr", 0), ("Ty", 0, 1), ("Ty", 1, 1), ("Cx", 1, 0), ("Qs",), ("Cr", 1), ("Dl",), ("Tx", 0, 1), ("Uo",), ("Fa", 0),
    ("Tx", 1, 1), ("Tk", 1, 0), ("Qy",), ("Us",), ("Tk", 0, 1), ("Cy", 0, 1), ("Tk", 1, 1), ("X", 0), ("Cx", 0, 0), ("Wq",), ("Fp", 0, 0),
    ("X", 1), ("Cy", 1, 1), ("Fp", 0, 1), ("Fp", 1, 0), ("Cx", 0, 1), ("Fp", 0, 2), ("Fp", 1, 1), ("Fp", 1, 2), ("Uy",), ("Fp", 1, 3),
    ("Fp", 0, 3), ("Fs", 0, 0), ("Fs", 1, 0), ("Fs", 1, 1), ("Fs", 0, 1), ("Ck", 1, 0), ("Fs", 0, 2), ("Cx", 1, 1), ("Fs", 1, 2),
    ("Ck", 0, 1), ("Fs", 0, 3), ("Fs", 1, 3), ("Ck", 0, 0), ("Wu",), ("D", 4), ("Fu", 1, 0), ("Fu", 0, 0), ("Fu", 0, 1), ("Fu", 0, 2),
    ("Fu", 0, 3), ("Ck", 1, 1), ("Fu", 1, 1), ("Fu", 1, 2), ("Fu", 1, 3),
]


def gather(tier_count, lengths, groups, tok, cot, vectors, w_qkv, w_up, w_dense, w_down, order=None):
    rows, half = tok.shape
    part = w_dense.shape[0]
    c_rows = w_up.shape[0]
    results = ((1, bf16), (4, bf16), (4, f32), (3, bf16), (2, f32), (1, f32))
    sds = jax.ShapeDtypeStruct
    any_ = pl.BlockSpec(memory_space=pl.ANY)
    smem = pl.BlockSpec(memory_space=pltpu.SMEM)
    return pl.pallas_call(
        functools.partial(gather_kernel, tier_count, order or ORDER_A),
        out_shape=[sds((2, 4, rows, 2 * half), bf16), sds((2, 4, rows, 2 * half), bf16),
                   sds((2, LINE, c_rows, 3 * part), bf16), sds((2, LINE, c_rows, 4 * part), bf16), sds((5 * part, 2 * half), bf16), sds(cot.shape, bf16),
                   *[sds((2, 4 * rows, count * part), kind) for count, kind in results]],
        in_specs=[smem, smem, any_, any_, pl.BlockSpec(memory_space=pltpu.VMEM), any_, any_, any_, any_],
        out_specs=[any_] * 5 + [pl.BlockSpec(memory_space=pltpu.VMEM)] + [any_] * 6,
        scratch_shapes=[pltpu.VMEM((2, 4, rows, 2 * half), bf16), pltpu.VMEM((2, LINE, c_rows, 3 * part), bf16), pltpu.VMEM((2, LINE, c_rows, 4 * part), bf16),
                        *[pltpu.VMEM((2, 4 * rows, count * part), kind) for count, kind in results],
                        pltpu.VMEM((4, rows, half), bf16), pltpu.VMEM((4, rows, half), bf16), pltpu.VMEM((2, rows, half), bf16),
                        pltpu.VMEM((2, rows, 2 * half), bf16),
                        pltpu.VMEM(w_qkv.shape, f32), pltpu.VMEM(w_up.shape, f32), pltpu.VMEM(w_dense.shape, f32), pltpu.VMEM(w_down.shape, f32),
                        pltpu.VMEM((LINE, c_rows, 3 * part), bf16), pltpu.VMEM((LINE, c_rows, 4 * part), bf16), pltpu.VMEM((5 * part, half), bf16),
                        pltpu.SemaphoreType.DMA((80,)), pltpu.SemaphoreType.DMA((80,)), pltpu.SemaphoreType.DMA((24,)), pltpu.SemaphoreType.DMA((5,)),
                        pltpu.SemaphoreType.DMA((6,)), pltpu.SemaphoreType.DMA((12,))],
        compiler_params=pltpu.CompilerParams(collective_id=1, has_side_effects=True, vmem_limit_bytes=60 << 20),
    )(lengths, groups, tok, cot, vectors, w_qkv, w_up, w_dense, w_down)


class Sender:
    def __init__(self, send_sems, recv_sems, load_sems):
        self.copies = Copies(send_sems, recv_sems)
        self.load_sems, self.loads, self.sent = load_sems, [], []

    def load(self, src, dst):
        copy = pltpu.make_async_copy(src, dst, self.load_sems.at[len(self.loads)])
        copy.start()
        self.loads.append([copy, False])
        return len(self.loads) - 1

    def need(self, *which):
        for i in which:
            if not self.loads[i][1]:
                self.loads[i][0].wait()
                self.loads[i][1] = True

    def send(self, src, dst, device, when=None, slot=None):
        copy = self.copies.make(src, dst, device, slot)
        if when is None:
            copy.start()
        else:
            pl.when(when)(copy.start)
        self.sent.append([copy, when])
        return copy

    def late(self, copy):
        self.sent = [[e[0], None] if e[0] is copy else e for e in self.sent]

    def wait_sent(self, copy):
        for entry in self.sent:
            if entry[0] is copy:
                self.sent = [e for e in self.sent if e is not entry]
                copy.wait_send()
                return

    def wait_all(self):
        self.need(*range(len(self.loads)))
        for copy, when in self.sent:
            if when is None:
                copy.wait_send()
            else:
                pl.when(when)(copy.wait_send)


class Columns:
    def __init__(self, buffer, sems, wanted):
        self.buffer, self.sems, self.wanted, self.taken, self.fetches = buffer, sems, wanted, 0, []
        if wanted:
            self.fetch(0)

    def fetch(self, i):
        src, at = self.wanted[i]
        copy = pltpu.make_async_copy(src.at[at], self.buffer.at[i % 2], self.sems.at[i % 2])
        copy.start()
        self.fetches.append(copy)

    def take(self):
        i = self.taken
        self.taken += 1
        if i + 1 < len(self.wanted):
            self.fetch(i + 1)
        self.fetches[i].wait()
        return self.buffer.at[i % 2]


def columns(first, count):
    if not isinstance(first, int):
        first = pl.multiple_of(first, count)
    return slice(None), pl.ds(first, count)


class Stream:
    def __init__(self, sender, tier_count, rows, half, product, part_s, near_r, far_r, line_s, line_r, total_s, free_core, free_far, before=None):
        self.sender, self.rows, self.half, self.product = sender, rows, half, product
        self.part_s, self.near_r, self.far_r, self.line_s, self.line_r, self.total_s = part_s, near_r, far_r, line_s, line_r, total_s
        self.line_id, flips, self.line, self.core, self.far_peer, self.col_peer = neighbours(tier_count)
        self.bit = (self.line_id % 2 + lax.axis_index("col")) % 2
        self.middle = (self.line_id == 1) | (self.line_id == 2)
        self.ends = (self.line_id == 0) | (self.line_id == 3)
        self.chunk = rows // CH
        self.free_core, self.free_far, self.before, self.far_here = free_core, free_far, before, []
        self.near, self.far, self.col, self.one, self.two, self.three, self.relay = {}, {}, {}, {}, {}, {}, {}

    def cut(self, c):
        return pl.ds(c * self.chunk, self.chunk)

    def compute(self, p, c):
        place = CH * p + c
        out = self.part_s.at[place]
        chunk, rows = self.chunk, self.rows
        if self.before:
            for copy in [*self.before.near[p, c], self.before.far[p, c], self.before.col[p, c]]:
                self.sender.wait_sent(copy)
        step = self.half // 2

        def body(n, carry):
            at = pl.ds(pl.multiple_of(n * step, step), step)

            def lhs(ref):
                base = p * 4 * rows + c * chunk
                return jnp.concatenate([ref[pl.ds(base + t * rows, chunk), :] for t in range(4)], axis=0)

            low = self.product(lhs, at).astype(bf16)
            for t in range(4):
                out[t, :, at] = low[t * chunk:(t + 1) * chunk]
            return carry

        lax.fori_loop(0, 2 * self.half // step, body, 0)
        into = self.near_r.at[place]
        if self.before:
            pl.semaphore_wait(self.free_core.at[place], 1)
        self.near[p, c] = [self.sender.send(out.at[1], into.at[0], self.core), self.sender.send(out.at[3], into.at[1], self.core)]

    def give_far(self, p, c):
        place = CH * p + c
        self.near[p, c][1].wait_recv()
        mine = self.part_s.at[place, 2]
        mine[...] = (mine[...].astype(f32) + self.near_r[place, 1].astype(f32)).astype(bf16)
        for copy in list(self.far.values())[:max(0, len(self.far) + 1 - DEPTH)]:
            if not any(copy is other for other in self.far_here):
                copy.wait_recv()
                self.far_here.append(copy)
        if self.before:
            pl.semaphore_wait(self.free_far.at[place], 1)
        self.far[p, c] = self.sender.send(mine, self.far_r.at[place], self.far_peer)

    def give_col(self, p, c):
        place, half = CH * p + c, self.half
        self.near[p, c][0].wait_recv()
        if not any(copy is self.far[p, c] for copy in self.far_here):
            self.far[p, c].wait_recv()
            self.far_here.append(self.far[p, c])
        mine = self.part_s.at[place, 0]
        total = mine[...].astype(f32) + self.near_r[place, 0].astype(f32)
        total = (total + self.far_r[place].astype(f32)).astype(bf16)
        if not self.before:
            for sem, peer in ((self.free_core, self.core), (self.free_far, self.far_peer)):
                pl.semaphore_signal(sem.at[place], inc=1, device_id=peer, device_id_type=pl.DeviceIdType.MESH)
        self.line_s[2 * p + self.bit, self.cut(c), :] = total[:, :half]
        mine[:, pl.ds(half, half)] = total[:, half:]
        self.col[p, c] = self.sender.send(mine.at[:, pl.ds(half, half)], self.line_s.at[2 * p + self.bit, self.cut(c)], self.col_peer)

    def give_line(self, p, c):
        self.col[p, c].wait_recv()
        own, got, cut, send = self.line_s, self.line_r, self.cut(c), self.sender.send
        if p == 0:
            self.one[c] = send(own.at[1, cut], got.at[0, cut], self.line[1])
        else:
            self.relay[c] = send(own.at[3, cut], got.at[3, cut], self.line[1], self.ends)
            self.three[c] = send(own.at[3, cut], got.at[2, cut], self.line[3], self.middle)
            self.two[c] = send(own.at[2, cut], got.at[1, cut], self.line[2], self.ends)

    def relay_line(self, c):
        own, got, cut = self.line_s, self.line_r, self.cut(c)

        @pl.when(self.middle)
        def _():
            self.relay[c].wait_recv()
            own[2, cut, :] = (own[2, cut, :].astype(f32) + got[3, cut, :].astype(f32)).astype(bf16)
            self.two[c].start()

        self.sender.late(self.two[c])

    def finish(self, c):
        own, got, cut, total_s = self.line_s, self.line_r, self.cut(c), self.total_s
        self.one[c].wait_recv()
        self.two[c].wait_recv()
        total_s[cut, :] = own[0, cut, :].astype(f32) + got[0, cut, :].astype(f32) + got[1, cut, :].astype(f32)

        @pl.when(self.middle)
        def _():
            self.three[c].wait_recv()
            total_s[cut, :] += got[2, cut, :].astype(f32)

    def run(self, what, args):
        {"c": self.compute, "x": self.give_far, "y": self.give_col, "z": self.give_line, "r": self.relay_line, "f": self.finish}[what](*args)


class InGrad:
    def __init__(self, sender, tier_count, taker, rhs, out, mine_s, mine_r):
        self.sender, self.taker, self.rhs, self.out, self.mine_s, self.mine_r = sender, taker, rhs, out, mine_s, mine_r
        self.line_id, flips, self.line, core, far, self.col = neighbours(tier_count)
        self.near, self.given = {}, []

    def other(self, s):
        self.mine_s[s] = t_mm(self.taker.take()[...], self.rhs[...]).astype(bf16)
        self.near[s] = self.sender.send(self.mine_s.at[s], self.mine_r.at[s], self.col)

    def mine(self, s):
        value = t_mm(self.taker.take()[...], self.rhs[...])
        self.near[s].wait_recv()
        self.sender.wait_sent(self.near[s])
        self.mine_s[s] = (value + self.mine_r[s].astype(f32)).astype(bf16)
        if s:
            self.given.append(self.sender.send(self.mine_s.at[s], self.out.at[self.line_id], self.line[s]))
        else:
            self.sender.load(self.mine_s.at[0], self.out.at[self.line_id])

    def wait(self):
        for copy in self.given:
            copy.wait_recv()


def backward_kernel(tier_count, order, attn, hidden, slope, qkv, turns, stat, x_in, b_in, dm, wq, wu, tok, cot, vec_ref,
                  block_out, grad_out, gin_out, gd_out, vec_out,
                  a_v, h_v, d_v, at_v, qkv_v, turn_v, stat_v, wq_v, wu_v, da_v, dq_v, du_v, dk_s, dv_s, col_v, back_v, slope_v,
                  part_s, near_r, far_r, line_s, line_r, dn_s, gq_s, gq_r, gu_s, gu_r, do_s, do_r, dm_s,
                  stat_s, stat_r, stat_own, hat_s, hat_r, row_s, row_r, mid_s, mid_r, end_s, end_r, out_s, out_r, out_mid, out_end,
                  bias_s, bias_r, bias_v, send_sems, recv_sems, load_sems, free_core, free_far, col_sems, back_sems, slope_sems):
    line_id, flips, line, core, far, col = neighbours(tier_count)
    rows, half = tok.shape
    part = a_v.shape[1]
    slots = 4 * rows
    width = 2 * half
    col_id, row_id = lax.axis_index("col"), lax.axis_index("row")
    across = (lax.axis_index("dp"), 3 - row_id, col_id)
    row_peers = [core, far, across]
    block = half // 4
    scale = HDIM ** (-0.5)
    sender = Sender(send_sems, recv_sems, load_sems)
    for src, dst in ((attn, a_v), (hidden, h_v), (dm, d_v), (qkv, qkv_v), (turns, turn_v), (stat, stat_v), (wq, wq_v), (wu, wu_v)):
        sender.load(src, dst)
    send = sender.send
    wanted = []
    for what, *args in order:
        if what in ("qo", "qm", "uo", "um"):
            wanted.append((x_in, columns(flips[args[0]] * block + (half if what[1] == "o" else 0), block)))
        if what in ("do", "dm"):
            wanted.append((b_in, columns(args[0] * block + (half if what == "do" else 0), block)))
    taker = Columns(col_v, col_sems, wanted)
    b_rows = Columns(back_v, back_sems, [(b_in, (pl.ds(args[0] * rows, rows), slice(None))) for what, *args in order if what == "a"])
    s_rows = Columns(slope_v, slope_sems, [(slope, (pl.ds(args[0] * rows, rows), slice(None))) for what, *args in order if what == "a"])
    meet([line[1], line[2], line[3], core, far, across, col])
    own_columns = pl.ds(pl.multiple_of(col_id * half, half), half)
    other_columns = pl.ds(pl.multiple_of((1 - col_id) * half, half), half)

    def rows_to_lanes(one, two):
        lane = lax.broadcasted_iota(jnp.int32, (rows, 128), 1)
        return jnp.where(lane == 0, one, jnp.where(lane == 1, two, 0.0)).T[0:8]

    def lanes_to_rows(value):
        return jnp.concatenate([value, jnp.zeros((120, rows), f32)], axis=0).T

    tail = {}

    def stats_start():
        wide = tok[...].astype(f32)
        stat_s[...] = rows_to_lanes(jnp.sum(wide, axis=1, keepdims=True), jnp.sum(wide * wide, axis=1, keepdims=True))
        tail["stat"] = send(stat_s, stat_r, col)

    def stats_end():
        tail["stat"].wait_recv()
        both = lanes_to_rows((stat_s[...] + stat_r[...]) / width)
        mean = both[:, 0:1]
        inv = lax.rsqrt(both[:, 1:2] - mean * mean + eps_norm)
        lane = lax.broadcasted_iota(jnp.int32, (rows, 128), 1)
        stat_own[...] = jnp.where(lane == 0, mean, inv)

    def fold(rows_of):
        step = half // 8
        return jnp.concatenate([jnp.concatenate([row[:, i * step:(i + 1) * step] for i in range(8)]) for row in rows_of], axis=1)

    def unfold(value, i):
        step = half // 8
        return jnp.concatenate([value[j:j + 1, i * step:(i + 1) * step] for j in range(8)], axis=1)

    def early_one():
        total = jnp.concatenate([jnp.sum(ref[...].astype(f32), axis=0, keepdims=True) for ref in (dq_v, du_v)], axis=1)
        blocks = [total[:, k * part:(k + 1) * part] for k in range(7)]
        bias_s[...] = jnp.concatenate(blocks + [jnp.zeros((1, part), f32)])
        tail["bias"] = [send(bias_s, bias_r, col)]
        out_s[...] = fold([jnp.sum(cot[...].astype(f32), axis=0, keepdims=True)])
        tail["out"] = [send(out_s, out_r.at[i], peer) for i, peer in enumerate(row_peers)]

    def early_two():
        for copy in tail["bias"] + tail["out"]:
            copy.wait_recv()
        bias_v[line_id, row_id] = bias_s[...] + bias_r[...]
        mine = bias_v.at[line_id, row_id]
        tail["bias"] = [send(mine, mine, peer) for peer in row_peers]
        out_mid[...] = (out_s[...] + out_r[0]) + (out_r[1] + out_r[2])
        tail["out"] = [send(out_mid, out_r.at[3 + i], line[1 + i]) for i in range(3)]

    def early_three():
        for copy in tail["bias"] + tail["out"]:
            copy.wait_recv()
        tail["bias"] = [send(bias_v.at[line_id], bias_v.at[line_id], line[1 + i]) for i in range(3)]
        out_end[...] = (out_mid[...] + out_r[3]) + (out_r[4] + out_r[5])
        tail["out"] = [send(out_end, out_r.at[6], col)]

    def early_four():
        for copy in tail["bias"] + tail["out"]:
            copy.wait_recv()
        for columns_of, value in ((own_columns, out_end[...]), (other_columns, out_r[6])):
            vec_out[9:10, columns_of] = unfold(value, 0)
            vec_out[10:11, columns_of] = unfold(value, 0)
        for r in range(4):
            for z in range(LINE):
                vec_out[2:9, (r * LINE + z) * part:(r * LINE + z + 1) * part] = bias_v[z, r, 0:7, :]

    def vectors_end():
        gain = vec_ref[0:1, own_columns]
        cuts = [pl.ds(i * 64, 64) for i in range(rows // 64)]
        sums, crosses = [], []
        totals = [jnp.zeros((1, half), f32) for _ in range(2)]
        for at in cuts:
            centred = (tok[at, :].astype(f32) - stat_own[at, 0:1]) * stat_own[at, 1:2]
            grad = dn_s[at, :]
            hat = grad * gain
            sums.append(jnp.sum(hat, axis=1, keepdims=True))
            crosses.append(jnp.sum(hat * centred, axis=1, keepdims=True))
            totals[0] += jnp.sum(grad * centred, axis=0, keepdims=True)
            totals[1] += jnp.sum(grad, axis=0, keepdims=True)
        row_s[...] = fold(totals)
        row_copies = [send(row_s, row_r.at[i], peer) for i, peer in enumerate(row_peers)]
        hat_s[...] = rows_to_lanes(jnp.concatenate(sums), jnp.concatenate(crosses))
        hat_copy = send(hat_s, hat_r, col)
        for copy in row_copies:
            copy.wait_recv()
        mid_s[...] = (row_s[...] + row_r[0]) + (row_r[1] + row_r[2])
        mid_copies = [send(mid_s, mid_r.at[i], line[1 + i]) for i in range(3)]
        hat_copy.wait_recv()
        both = lanes_to_rows((hat_s[...] + hat_r[...]) / width)
        for at, first in zip(cuts, range(0, rows, 64)):
            centred = (tok[at, :].astype(f32) - stat_own[at, 0:1]) * stat_own[at, 1:2]
            mine = both[first:first + 64]
            hat = dn_s[at, :] * gain
            grad_out[at, :] = stat_own[at, 1:2] * (hat - mine[:, 0:1] - centred * mine[:, 1:2]) + cot[at, :].astype(f32)
        for copy in mid_copies:
            copy.wait_recv()
        end_s[...] = (mid_s[...] + mid_r[0]) + (mid_r[1] + mid_r[2])
        end_copy = send(end_s, end_r, col)
        end_copy.wait_recv()
        for columns_of, value in ((own_columns, end_s[...]), (other_columns, end_r[...])):
            for i in range(2):
                vec_out[i:i + 1, columns_of] = unfold(value, i)


    def product(lhs, at):
        return mm(lhs(a_v), d_v[0:part, at]) + mm(lhs(h_v), d_v[part:, at])

    def product_back(lhs, at):
        return mm_t(lhs(dq_v), wq_v[at, :]) + mm_t(lhs(du_v), wu_v[at, :])

    first = Stream(sender, tier_count, rows, half, product, part_s, near_r, far_r, line_s.at[0], line_r.at[0], dn_s, free_core, free_far)
    second = Stream(sender, tier_count, rows, half, product_back, part_s, near_r, far_r, line_s.at[1], line_r.at[1], dn_s,
                    free_core, free_far, first)
    qkv_grad = InGrad(sender, tier_count, taker, dq_v, gin_out.at[:, :, pl.ds(0, 3 * part)], gq_s, gq_r)
    up_grad = InGrad(sender, tier_count, taker, du_v, gin_out.at[:, :, pl.ds(3 * part, 4 * part)], gu_s, gu_r)

    def back_block(i):
        sender.need(2)
        back, slopes = b_rows.take(), s_rows.take()
        at = pl.ds(i * rows, rows)
        da_v[at, :] = mm_t(back[...], d_v[0:part, :]).astype(bf16)
        du_v[at, :] = (mm_t(back[...], d_v[part:, :]) * slopes[...]).astype(bf16)

    quarters = [row_id, row_id + 1 - 2 * (row_id % 2), (row_id + 2) % 4, 3 - row_id]
    lane = lax.broadcasted_iota(jnp.int32, (rows, part), 1)

    def attend_back(p, i):
        sender.need(3, 4, 5)
        if i == 0:
            dk_s[...] = jnp.zeros_like(dk_s)
            dv_s[...] = jnp.zeros_like(dv_s)
        whole = pl.ds(p * slots, slots)
        at = pl.ds(p * slots + i * rows, rows)
        key_place = jnp.concatenate([quarters[t] * rows + lax.broadcasted_iota(jnp.int32, (1, rows), 1) for t in range(4)], axis=1)
        place = quarters[i] * rows + lax.broadcasted_iota(jnp.int32, (rows, 1), 0)
        allowed = (key_place >= stat_v[at, part - 1:part].astype(jnp.int32)) & (key_place <= place)
        queries, d_attn = qkv_v[at, 0:part], da_v[at, :]
        keys, values = qkv_v[whole, part:2 * part], qkv_v[whole, 2 * part:]
        d_q = jnp.zeros((rows, part), f32)
        for h in range(part // HDIM):
            head = (lane >= h * HDIM) & (lane < (h + 1) * HDIM)
            q_h = jnp.where(head, queries, jnp.zeros_like(queries))
            da_h = jnp.where(head, d_attn, jnp.zeros_like(d_attn))
            scores = jnp.where(allowed, mm_t(q_h, keys) * scale, -1e30)
            probs = jnp.exp(scores - stat_v[at, h:h + 1])
            low = probs.astype(bf16)
            d_probs = mm_t(da_h, values)
            delta = jnp.sum(probs * d_probs, axis=-1, keepdims=True)
            d_scores = (probs * (d_probs - delta)).astype(bf16)
            d_q = jnp.where(head, mm(d_scores, keys), d_q)
            dk_s[...] += t_mm(q_h, d_scores)
            dv_s[...] += t_mm(da_h, low)
        dq_v[at, 0:part] = turn(d_q * scale, turn_v[at, :], -1.0).astype(bf16)
        if i == 3:
            dq_v[whole, part:2 * part] = turn(dk_s[...].T * scale, turn_v[whole, :], -1.0).astype(bf16)
            dq_v[whole, 2 * part:] = dv_s[...].T.astype(bf16)

    d_near = {}

    def out_other(j):
        sender.need(0, 1)
        if not d_near:
            at_v[0:part, :] = a_v[...].T
            at_v[part:, :] = h_v[...].T
        do_s[j] = mm(at_v[...], taker.take()[...]).astype(bf16)
        d_near[j] = send(do_s.at[j], do_r.at[j], col)

    d_done = []

    def out_mine(j):
        if len(d_done) > 1:
            sender.need(d_done[-2])
        value = mm(at_v[...], taker.take()[...])
        d_near[j].wait_recv()
        staged = dm_s.at[len(d_done) % 2]
        staged[...] = value + do_r[j].astype(f32)
        d_done.append(sender.load(staged, gd_out.at[:, pl.ds(j * block, block)]))

    actions = {"a": back_block, "b": attend_back, "qo": qkv_grad.other, "qm": qkv_grad.mine, "uo": up_grad.other, "um": up_grad.mine,
               "do": out_other, "dm": out_mine, "s": stats_start, "S": stats_end, "e1": early_one, "e2": early_two, "e3": early_three,
               "e4": early_four, "v": vectors_end}
    for what, *args in order:
        if what in actions:
            actions[what](*args)
            continue
        which, args = args[0], args[1:]
        if what == "c":
            sender.need(*((6, 7) if which else (0, 1, 2)))
        (second if which else first).run(what, args)
        if what == "f" and not which:
            at = first.cut(args[0])
            bias = vec_ref[9:10, own_columns] + vec_ref[10:11, own_columns]
            block_out[at, :] = (tok[at, :].astype(f32) + dn_s[at, :] + bias).astype(bf16)
    qkv_grad.wait()
    up_grad.wait()
    sender.wait_all()


BACKWARD_ORDER = [
    ("c", 0, 1, 0), ("do", 2), ("x", 0, 1, 0), ("a", 6), ("a", 2), ("a", 3), ("c", 0, 0, 0), ("do", 3), ("c", 0, 1, 1), ("a", 5), ("a", 1),
    ("x", 0, 0, 0), ("y", 0, 1, 0), ("a", 0), ("a", 4), ("x", 0, 1, 1), ("b", 0, 0), ("a", 7), ("z", 0, 1, 0), ("uo", 2), ("b", 0, 1),
    ("c", 0, 0, 1), ("uo", 3), ("b", 0, 2), ("um", 2), ("b", 0, 3), ("y", 0, 0, 0), ("b", 1, 0), ("y", 0, 1, 1), ("r", 0, 0), ("b", 1, 1),
    ("x", 0, 0, 1), ("b", 1, 2), ("b", 1, 3), ("c", 1, 1, 0), ("qo", 0), ("z", 0, 1, 1), ("z", 0, 0, 0), ("x", 1, 1, 0), ("qo", 2), ("e1",),
    ("c", 1, 0, 0), ("y", 0, 0, 1), ("qm", 2), ("qo", 1), ("dm", 3), ("c", 1, 1, 1), ("x", 1, 1, 1), ("uo", 0), ("y", 1, 1, 0), ("um", 3),
    ("dm", 2), ("z", 0, 0, 1), ("f", 0, 0), ("e2",), ("c", 1, 0, 1), ("r", 0, 1), ("do", 1), ("qm", 0), ("qm", 1), ("x", 1, 0, 0), ("e3",),
    ("e4",), ("y", 1, 1, 1), ("s",), ("x", 1, 0, 1), ("um", 0), ("z", 1, 1, 0), ("do", 0), ("z", 1, 1, 1), ("y", 1, 0, 0), ("y", 1, 0, 1),
    ("dm", 1), ("f", 0, 1), ("dm", 0), ("z", 1, 0, 0), ("r", 1, 0), ("uo", 1), ("z", 1, 0, 1), ("S",), ("qo", 3), ("r", 1, 1), ("um", 1),
    ("f", 1, 0), ("qm", 3), ("f", 1, 1), ("v",),
]


def backward(tier_count, attn, hidden, slope, qkv, turns, stat, normed, back, out_mat, qkv_mat, up_mat, tok, cot, vectors, order=None):
    rows, half = tok.shape
    width = 2 * half
    chunk = rows // CH
    all_rows, part = attn.shape
    block = half // 4
    sds = jax.ShapeDtypeStruct
    any_ = pl.BlockSpec(memory_space=pl.ANY)
    vmem = pl.BlockSpec(memory_space=pltpu.VMEM)

    def buf(*shape, kind=bf16):
        return pltpu.VMEM(shape, kind)

    dma = pltpu.SemaphoreType.DMA
    regular = pltpu.SemaphoreType.REGULAR
    return pl.pallas_call(
        functools.partial(backward_kernel, tier_count, order or BACKWARD_ORDER),
        out_shape=[sds((rows, half), bf16), sds((rows, half), f32), sds((LINE, block, 7 * part), bf16), sds((5 * part, half), f32), sds((11, width), f32)],
        in_specs=[any_] * 11 + [vmem] * 3,
        out_specs=[vmem, vmem, any_, any_, vmem],
        scratch_shapes=[
            buf(all_rows, part), buf(all_rows, 4 * part), buf(5 * part, width), buf(5 * part, all_rows),
            buf(all_rows, 3 * part), buf(all_rows, 2 * part, kind=f32), buf(all_rows, part, kind=f32), buf(width, 3 * part), buf(width, 4 * part),
            buf(all_rows, part), buf(all_rows, 3 * part), buf(all_rows, 4 * part), buf(part, 4 * rows, kind=f32), buf(part, 4 * rows, kind=f32),
            buf(2, all_rows, block), buf(2, rows, width), buf(2, rows, 4 * part, kind=f32),
            buf(2 * CH, 4, chunk, width), buf(2 * CH, 2, chunk, width), buf(2 * CH, chunk, width),
            buf(2, 4, rows, half), buf(2, 4, rows, half), buf(rows, half, kind=f32),
            buf(4, block, 3 * part), buf(4, block, 3 * part), buf(4, block, 4 * part), buf(4, block, 4 * part),
            buf(4, 5 * part, block), buf(4, 5 * part, block), buf(2, 5 * part, block, kind=f32),
            buf(8, rows, kind=f32), buf(8, rows, kind=f32), buf(rows, 128, kind=f32), buf(8, rows, kind=f32), buf(8, rows, kind=f32),
            buf(8, half // 4, kind=f32), buf(3, 8, half // 4, kind=f32), buf(8, half // 4, kind=f32), buf(3, 8, half // 4, kind=f32),
            buf(8, half // 4, kind=f32), buf(8, half // 4, kind=f32),
            buf(8, half // 8, kind=f32), buf(7, 8, half // 8, kind=f32), buf(8, half // 8, kind=f32), buf(8, half // 8, kind=f32),
            buf(8, part, kind=f32), buf(8, part, kind=f32), buf(LINE, 4, 8, part, kind=f32),
            dma((128,)), dma((128,)), dma((24,)), regular((2 * CH,)), regular((2 * CH,)), dma((2,)), dma((2,)), dma((2,)),
        ],
        compiler_params=pltpu.CompilerParams(collective_id=2, has_side_effects=True, vmem_limit_bytes=63 << 20),
    )(attn, hidden, slope, qkv, turns, stat, normed, back, out_mat, qkv_mat, up_mat, tok, cot, vectors)


def adamw_fast(weight, first_moment, second_moment, gradient, rate):
    first_next = 0.9 * first_moment + 0.1 * gradient
    second_next = 0.95 * second_moment + 0.05 * gradient * gradient
    scaled = second_next * (1.0 / (1.0 - 0.95**STEP))
    root = scaled * lax.rsqrt(scaled) + 1e-08
    update = first_next * (rate / (1.0 - 0.9**STEP)) / root
    return first_next, second_next, (1.0 - 0.1 * rate) * weight - update


def step_kernel(rates, gin_ref, gout_ref, out_ref, back_ref, gvec_ref, *refs):
    ins, vec_ins, outs, rest = refs[:12], refs[12:15], refs[15:27], refs[27:]
    rest[0][...] = out_ref[...]
    rest[1][...] = back_ref[...]

    @pl.when(pl.program_id(0) == 0)
    def _():
        values = adamw(*[ref[...] for ref in vec_ins], gvec_ref[...], 0.5, 0.0)
        for ref, value in zip(rest[2:], values):
            ref[...] = value

    pieces = gin_ref.shape[0]
    part = gin_ref.shape[2] // 7

    def one(i, at, grad):
        values = adamw_fast(*[ref[at] for ref in ins[3 * i:3 * i + 3]], grad, rates[i])
        for ref, value in zip(outs[3 * i:3 * i + 3], values):
            ref[at] = value

    for z in range(pieces):
        at = pl.ds(z * part, part)
        for k in range(3):
            one(0, (k, slice(None), at), gin_ref[z, :, pl.ds(k * part, part)].astype(f32))
        for k in range(4):
            one(1, (slice(None), k, at), gin_ref[z, :, pl.ds((3 + k) * part, part)].astype(f32))
    one(2, (slice(None), slice(None)), gout_ref[0])
    for k in range(4):
        one(3, (slice(None), k, slice(None)), gout_ref[1 + k])


def step_all(grad_in, grad_out, block_out, grad_tokens, vec_grad, qkv, up, dense, down, vec):
    steps = 8
    rates = (D ** (-0.5), D ** (-0.5), max(D // 128, 4) ** (-0.5), FF ** (-0.5))

    def spec(shape, axis):
        block = tuple(size // steps if i == axis else size for i, size in enumerate(shape))
        return pl.BlockSpec(block, lambda i: tuple(i if a == axis else 0 for a in range(len(shape))))

    arrays = [*qkv, *up, *dense, *down]
    axes = [1] * 3 + [0] * 9
    specs = [spec(value.shape, axis) for value, axis in zip(arrays, axes)]
    rows = [spec(value.shape, 0) for value in (block_out, grad_tokens)]
    whole = pl.BlockSpec(vec_grad.shape, lambda i: (0, 0))
    kinds = [*arrays, block_out, grad_tokens, *vec]
    out = pl.pallas_call(
        functools.partial(step_kernel, rates),
        grid=(steps,),
        out_shape=[jax.ShapeDtypeStruct(value.shape, value.dtype) for value in kinds],
        in_specs=[spec(grad_in.shape, 1), spec(grad_out.shape, 1), *rows, whole, *specs, *[whole] * 3],
        out_specs=[*specs, *rows, *[whole] * 3],
        compiler_params=pltpu.CompilerParams(vmem_limit_bytes=62 << 20),
    )(grad_in, grad_out, block_out, grad_tokens, vec_grad, *arrays, *vec)
    return [out[i:i + 3] for i in range(0, 12, 3)] + [out[12], out[13], out[14:]]


def per_device(
    tokens,
    cotangent,
    doc_lengths,
    doc_groups,
    w_qkv,
    w_up,
    w_dense,
    w_down,
    vectors,
    m_qkv,
    v_qkv,
    m_up,
    v_up,
    m_dense,
    v_dense,
    m_down,
    v_down,
    m_vec,
    v_vec,
):
    dp_count = lax.axis_size("dp")
    tier_count = dp_count // LINE
    row_count = lax.axis_size("row")
    col_count = lax.axis_size("col")
    assert row_count == 4 and col_count == 2 and dp_count % LINE == 0
    tok_dev, half_width = tokens.shape
    slot_count = tok_dev * row_count
    full_width = half_width * col_count
    row_width = full_width // row_count
    part = row_width // LINE
    tier_groups = [[line * tier_count + tier for tier in range(tier_count)] for line in range(LINE)]


    def tier_gather(value):
        if tier_count > 1:
            value = lax.all_gather(value, "dp", axis=0, tiled=True, axis_index_groups=tier_groups)
        return value

    if tier_count > 1:
        full_qkv, full_up, full_dense, full_down = [
            tier_gather(weight.astype(bf16)).astype(f32) for weight in (w_qkv, w_up, w_dense, w_down)
        ]
    else:
        full_qkv, full_up, full_dense, full_down = w_qkv, w_up, w_dense, w_down
    normed, back, qkv_mat, up_mat, out_mat, back_own, *fresh = gather(
        tier_count,
        doc_lengths,
        doc_groups,
        tokens,
        cotangent,
        vectors,
        full_qkv.transpose(1, 0, 2),
        full_up,
        full_dense,
        full_down,
    )
    rows_all = 2 * slot_count
    normed = normed.reshape(rows_all, full_width)
    back = back.reshape(rows_all, full_width)
    qkv_mat = qkv_mat.reshape(full_width, 3 * part)
    up_mat = up_mat.reshape(full_width, 4 * part)

    fresh = [value.reshape(rows_all, value.shape[-1]) for value in fresh]
    block_out, grad_tokens, grad_in, grad_out, vec_grad = backward(
        tier_count, *fresh, normed, back, out_mat, qkv_mat, up_mat, tokens, back_own, vectors
    )

    def tier_sum(value):
        if tier_count > 1:
            value = lax.psum_scatter(
                value, "dp", scatter_dimension=0, tiled=True, axis_index_groups=tier_groups
            )
        return value

    def own_columns(value, parts):
        value = value.astype(f32).reshape(LINE, half_width // LINE, parts, part)
        return tier_sum(value.transpose(1, 2, 0, 3).reshape(half_width // LINE, parts, row_width))

    if tier_count > 1:
        vec_grad = lax.psum(vec_grad, "dp", axis_index_groups=tier_groups)
        red_qkv = own_columns(grad_in[:, :, : 3 * part], 3)
        red_up = own_columns(grad_in[:, :, 3 * part :], 4)
        red_dense = tier_sum(grad_out[:part])
        red_down = tier_sum(grad_out[part:].reshape(4, part, half_width).transpose(1, 0, 2))
        qkv_new = adamw(w_qkv, m_qkv, v_qkv, red_qkv, D ** (-0.5), 0.1)
        up_new = adamw(w_up, m_up, v_up, red_up, D ** (-0.5), 0.1)
        dense_new = adamw(w_dense, m_dense, v_dense, red_dense, max(D // 128, 4) ** (-0.5), 0.1)
        down_new = adamw(w_down, m_down, v_down, red_down, FF ** (-0.5), 0.1)
        vec_new = adamw(vectors, m_vec, v_vec, vec_grad, 0.5, 0.0)
    else:
        qkv_new, up_new, dense_new, down_new, block_out, grad_tokens, vec_new = step_all(
            grad_in,
            grad_out.reshape(5, part, half_width),
            block_out,
            grad_tokens,
            vec_grad,
            [value.transpose(1, 0, 2) for value in (w_qkv, m_qkv, v_qkv)],
            (w_up, m_up, v_up),
            (w_dense, m_dense, v_dense),
            (w_down, m_down, v_down),
            (vectors, m_vec, v_vec),
        )
        qkv_new = [value.transpose(1, 0, 2) for value in qkv_new]
    return (
        block_out,
        grad_tokens,
        qkv_new[0],
        qkv_new[1],
        qkv_new[2],
        up_new[0],
        up_new[1],
        up_new[2],
        dense_new[0],
        dense_new[1],
        dense_new[2],
        down_new[0],
        down_new[1],
        down_new[2],
        vec_new[0],
        vec_new[1],
        vec_new[2],
    )


def solution(mesh):
    placed = (
        P(("dp", "row"), "col"),
        P(("dp", "row"), "col"),
        P(),
        P(),
        P(("col", "dp"), None, "row"),
        P(("col", "dp"), None, "row"),
        P(("row", "dp"), "col"),
        P(("row", "dp"), None, "col"),
        P(),
        P(("col", "dp"), None, "row"),
        P(("col", "dp"), None, "row"),
        P(("col", "dp"), None, "row"),
        P(("col", "dp"), None, "row"),
        P(("row", "dp"), "col"),
        P(("row", "dp"), "col"),
        P(("row", "dp"), None, "col"),
        P(("row", "dp"), None, "col"),
        P(),
        P(),
    )
    return jax.shard_map(
        per_device,
        mesh=mesh,
        in_specs=placed,
        out_specs=(
            P(("dp", "row"), "col"),
            P(("dp", "row"), "col"),
            P(("col", "dp"), None, "row"),
            P(("col", "dp"), None, "row"),
            P(("col", "dp"), None, "row"),
            P(("col", "dp"), None, "row"),
            P(("col", "dp"), None, "row"),
            P(("col", "dp"), None, "row"),
            P(("row", "dp"), "col"),
            P(("row", "dp"), "col"),
            P(("row", "dp"), "col"),
            P(("row", "dp"), None, "col"),
            P(("row", "dp"), None, "col"),
            P(("row", "dp"), None, "col"),
            P(),
            P(),
            P(),
        ),
        check_vma=False,
    )
```
